512 devices in a mesh: dp: 32 (over x, y, core), seq: 16 (over z).
Axes of the slice: x: 4, y: 4, z: 16, core: 2. Of those that a mesh axis runs over, the one named last changes fastest.
Arguments:
- inputs: bfloat16 [32, 2, 1024, 1024], P('dp', None, 'seq'), may hold values from -6 to 6
- cotangent: bfloat16 [32, 2, 1024, 1024], P('dp', None, 'seq'), may hold values from -6 to 6
- lengths: int32 [32, 2, 3], P('dp'), may hold values from 1 to 512, 1024 in all within a row
- item_ids: int32 [32, 2, 1024], P('dp', None, 'seq'), may hold values from 0 to 8191, as said below
- owner_row: int32 [8192], replicated, may hold values from 0 to 8191, as said below
- w_project: bfloat16 [1024, 4096], P('dp', 'seq'), may hold values from -0.1875 to 0.1875
- w_output: bfloat16 [1024, 1024], P('seq', 'dp'), may hold values from -0.1875 to 0.1875
Outputs:
- grad_w_project: float32 [1024, 4096], P('dp', 'seq')
- grad_w_output: float32 [1024, 1024], P('seq', 'dp')
- grad_table: float32 [8192, 1024], P('dp', 'seq')
The draws below stay inside these ranges and needn't reach their ends.
Inputs may be any that keep to these rules, and one draw needn't show every extreme that they name: `item_ids`: row owner_row[i] of the item table is held by dp index owner_row[i] // 256. The 128 positions of one device (both packs) hold items of at most 8 positions for any one owner. `owner_row`: A permutation of the rows of the item table.
All inputs are finite; a program needn't handle non-finite values.
Results may differ from the reference program's by a relative error of at most 0.02.
Values may be sent and summed in bfloat16 or wider, within the bound.
No kernel may reach another device: no remote copies, remote signals or barrier semaphores. Data moves between devices by JAX's collectives and lax.ppermute only.
A program may use at most 64 MiB of HBM per device.

```python
import math
import jax
import jax.numpy as jnp
import numpy as np
from jax import lax

D = 1024
HEADS = 8
HEAD_DIM = 128
HALF_ROWS = 64
SEQS = 3
ROWS_DEV = 256
PACK_LEN = 1024
CAP = 8
ITEMS = 8192
N_DP = 32
N_SEQ = 16


def owner_table(key):
    return jax.random.permutation(key, ITEMS).astype(jnp.int32)


def draw_owner_row(key, part):
    return owner_table(key)


def draw_item_ids(key, part):
    table = owner_table(key)
    key = jax.random.fold_in(key, 7)
    inverse = jnp.argsort(table, stable=True).astype(jnp.int32)
    per_device = 2 * HALF_ROWS
    slots = N_DP * CAP
    hot_owners = jax.random.randint(jax.random.fold_in(key, 1), (N_SEQ,), 0, N_DP).astype(jnp.int32)
    device_keys = jax.random.split(jax.random.fold_in(key, 2), N_DP * N_SEQ)
    device_hot = jnp.tile(hot_owners, N_DP)

    def device_draw(device_key, hot_owner):
        first_key, second_key, third_key = jax.random.split(device_key, 3)
        order = jax.random.permutation(first_key, slots).astype(jnp.int32)
        owners = order // CAP
        ranking = jnp.where(owners == hot_owner, -1, jnp.arange(slots, dtype=jnp.int32))
        chosen = order[jnp.argsort(ranking, stable=True)[:per_device]]
        shuffle = jax.random.permutation(second_key, per_device)
        chosen_owner = (chosen // CAP)[shuffle]
        local_rows = jax.random.randint(third_key, (per_device,), 0, ROWS_DEV).astype(jnp.int32)
        return inverse[chosen_owner * ROWS_DEV + local_rows]
    drawn = jax.vmap(device_draw)(device_keys, device_hot)
    drawn = drawn.reshape(N_DP, N_SEQ, 2, HALF_ROWS).transpose(0, 2, 1, 3)
    return drawn.reshape(N_DP, 2, N_SEQ * HALF_ROWS).astype(jnp.int32)


def levels(key, shape, shards, low, largest):
    gain, own = 1.0, jax.random.fold_in(key, 6)
    for dim, blocks in shards:
        heights = jnp.exp(jax.random.uniform(jax.random.fold_in(own, dim), (blocks,), jnp.float32, low / len(shards), largest / len(shards)))
        gain = gain * jnp.repeat(heights, shape[dim] // blocks).reshape([-1 if axis == dim else 1 for axis in range(len(shape))])
    return gain


def profile(number_of, total, limit, lean):
    weights = [(1 << 20) // math.isqrt(standing ** lean) + 1 for standing in range(2, number_of + 1)]
    surplus, holding = total - limit - (number_of - 1), [1] * (number_of - 1)
    while surplus > 0:
        free = [i for i in range(number_of - 1) if holding[i] < limit]
        mass, remaining = sum([weights[i] for i in free]), surplus
        for i in free:
            more = min(limit - holding[i], max(1, remaining * weights[i] // mass), surplus)
            holding[i] = holding[i] + more
            surplus = surplus - more
    return np.array([limit] + holding)


def uneven_parts(rng, amount, total, reach, slope):
    if amount == 2:
        one = jax.random.randint(rng, (), max(1, total - reach), min(reach, total - 1) + 1)
        return jnp.stack([one, total - one])
    sizes = jnp.asarray(profile(amount, total, reach, slope), jnp.int32)
    couples = (amount - 1) // 2
    donor, receiver = sizes[1:1 + 2 * couples:2], sizes[2:2 + 2 * couples:2]
    margin = jnp.minimum(donor - 1, reach - receiver)
    moved = jax.random.randint(jax.random.fold_in(rng, 1), (couples,), 0, 1 << 20) % (margin + 1)
    sizes = sizes.at[1:1 + 2 * couples:2].set(donor - moved).at[2:2 + 2 * couples:2].set(receiver + moved)
    return sizes[jax.random.permutation(jax.random.fold_in(rng, 2), amount)]


def gaussian(rng, extent, deviation, reach, cuts=(), held_as=jnp.bfloat16):
    values = deviation * jax.random.normal(rng, extent, jnp.float32)
    if cuts:
        values = values * levels(rng, extent, cuts, -0.22, 0.18)
    return jnp.clip(values, -reach, reach).astype(held_as)


def setup_inputs(seed: int = 0) -> dict:
    keys = jax.random.split(jax.random.key(seed), 8)
    inputs = gaussian(keys[0], (N_DP, 2, PACK_LEN, D), 1.0, 6.0, ((0, 32), (2, 16)))
    cotangent = gaussian(keys[1], (N_DP, 2, PACK_LEN, D), 1.0, 6.0, ((0, 32), (2, 16)))
    lengths = jax.vmap(lambda own: uneven_parts(own, SEQS, PACK_LEN, PACK_LEN // 2, 2))(jax.random.split(keys[2], N_DP * 2)).reshape((N_DP, 2, SEQS)).astype(jnp.int32)
    item_ids = draw_item_ids(jax.random.fold_in(keys[7], 71), 0)
    owner_row = draw_owner_row(jax.random.fold_in(keys[7], 71), 0)
    w_project = gaussian(keys[5], (D, 4 * D), D ** -0.5, 0.1875, ((0, 32), (1, 16)))
    w_output = gaussian(keys[6], (D, D), D ** -0.5, 0.1875, ((0, 16), (1, 32)))
    return {"inputs": inputs, "cotangent": cotangent, "lengths": lengths, "item_ids": item_ids, "owner_row": owner_row, "w_project": w_project, "w_output": w_output}


norm_floor = 1.0

def silu_grad(values):
    sigma = jax.nn.sigmoid(values)
    return sigma * (1.0 + values * (1.0 - sigma))

def pack_grads(pack_x, pack_dy, pack_lens, w_project, w_output):
    length = pack_x.shape[0]
    f32 = jnp.float32
    positions = jnp.arange(length, dtype=jnp.int32)
    ends = jnp.cumsum(pack_lens).astype(jnp.int32)
    segment = lax.optimization_barrier(jnp.sum((positions[:, None] >= ends[None, :]).astype(jnp.int32), axis=1)).astype(jnp.int32)
    masked = (segment[:, None] == segment[None, :]) & (positions[None, :] <= positions[:, None])
    z_pre = jnp.dot(pack_x, w_project, preferred_element_type=f32).reshape(length, HEADS, 4, HEAD_DIM)
    acted = jax.nn.silu(z_pre).astype(jnp.bfloat16)
    gating = acted[:, :, 0].astype(f32)
    value_part = acted[:, :, 1].astype(f32)
    queries = acted[:, :, 2].astype(f32)
    key_part = acted[:, :, 3].astype(f32)
    scale = HEAD_DIM ** (-0.5)
    scores = jnp.einsum('qhe,khe->hqk', queries, key_part) * scale
    attn = jnp.where(masked[None], jax.nn.silu(scores), 0.0).astype(jnp.bfloat16).astype(f32)
    mixed = jnp.einsum('hqk,khe->qhe', attn, value_part)
    centred = mixed - lax.optimization_barrier(jnp.mean(mixed, axis=-1, keepdims=True))
    inv_std = lax.rsqrt(lax.optimization_barrier(jnp.mean(centred * centred, axis=-1, keepdims=True)) + norm_floor)
    normed = centred * inv_std
    gated = (normed * gating).astype(jnp.bfloat16).astype(f32)
    out_heads = w_output.astype(f32).reshape(HEADS, HEAD_DIM, D)
    dy_f = pack_dy.astype(f32)
    d_gated = jnp.einsum('qd,hed->qhe', dy_f, out_heads)
    grad_out = jnp.einsum('qhe,qd->hed', gated, dy_f).reshape(D, D)
    d_gate = d_gated * normed
    d_normed = d_gated * gating
    d_mixed = inv_std * (d_normed - lax.optimization_barrier(jnp.mean(d_normed, axis=-1, keepdims=True)) - normed * lax.optimization_barrier(jnp.mean(d_normed * normed, axis=-1, keepdims=True)))
    d_mixed = d_mixed.astype(jnp.bfloat16).astype(f32)
    d_attn = jnp.einsum('qhe,khe->hqk', d_mixed, value_part)
    d_scores = (jnp.where(masked[None], d_attn * silu_grad(scores), 0.0) * scale).astype(jnp.bfloat16).astype(f32)
    d_value = jnp.einsum('hqk,qhe->khe', attn, d_mixed)
    d_query = jnp.einsum('hqk,khe->qhe', d_scores, key_part)
    d_key = jnp.einsum('hqk,qhe->khe', d_scores, queries)
    d_act = jnp.stack([d_gate, d_value, d_query, d_key], axis=2)
    d_z = (d_act * silu_grad(z_pre)).astype(jnp.bfloat16).reshape(length, 4 * D)
    grad_proj = jnp.dot(pack_x.T, d_z, preferred_element_type=f32)
    parts = jnp.einsum('qhc,dhc->hqd', d_z.astype(f32).reshape(length, HEADS, 4 * HEAD_DIM), w_project.astype(f32).reshape(D, HEADS, 4 * HEAD_DIM)).astype(jnp.bfloat16)
    token_grad = (dy_f + lax.optimization_barrier(jnp.sum(parts.astype(f32), axis=0))).astype(jnp.bfloat16)
    return (token_grad, grad_proj, grad_out)

def reference(inputs, cotangent, lengths, item_ids, owner_row, w_project, w_output):
    packed_x = inputs.reshape(N_DP * 2, PACK_LEN, D)
    packed_dy = cotangent.reshape(N_DP * 2, PACK_LEN, D)
    packed_lens = lengths.reshape(N_DP * 2, SEQS)

    def step(carry, pieces):
        token_grad, grad_proj, grad_out = pack_grads(pieces[0], pieces[1], pieces[2], w_project, w_output)
        return ((carry[0] + grad_proj, carry[1] + grad_out), token_grad)
    start_sums = (jnp.zeros((D, 4 * D), jnp.float32), jnp.zeros((D, D), jnp.float32))
    (grad_proj, grad_out), token_grads = lax.scan(step, start_sums, (packed_x, packed_dy, packed_lens))
    table_rows = owner_row[item_ids.reshape(-1)]
    grad_table = jnp.zeros((ITEMS, D), jnp.float32).at[table_rows].add(token_grads.reshape(-1, D).astype(jnp.float32))
    return (grad_proj, grad_out, grad_table)
```

```python
import jax
import jax.numpy as jnp
from jax import lax
from jax.sharding import Mesh, PartitionSpec as P

HEAD_DIM = 128
NORM_FLOOR = 1.0
F32 = jnp.float32
BF16 = jnp.bfloat16

X, Y, C, ZQ, ZR = 4, 4, 2, 4, 4
YC = Y * C
Z = ZQ * ZR
PAIR = ("y", "c")
DP = ("x", "y", "c")
SEQ = ("zq", "zr")
SHARE = ("x", "zr")
ALL = ("x", "y", "c", "zq", "zr")
OWNERS = X * YC
CAP = 8
ROWS = 256
SLOTS = OWNERS * CAP
LANES = 128


def exchange(value, axes):
    return lax.all_to_all(value, axes, split_axis=0, concat_axis=0, tiled=True)


def silu_grad(values):
    sigma = jax.nn.sigmoid(values)
    return sigma * (1.0 + values * (1.0 - sigma))


def routing(item_ids, owner_row):
    rows = jnp.take(owner_row, item_ids.reshape(-1))
    owner = rows // ROWS
    count = owner.shape[0]
    order = jnp.arange(count, dtype=jnp.int32)
    before = (owner[None, :] == owner[:, None]) & (order[None, :] < order[:, None])
    rank = jnp.sum(before.astype(jnp.int32), axis=1)
    return owner * CAP + rank, rows % ROWS


def heads_backward(px, pdy, weights, ends):
    length = px.shape[0]
    hd = HEAD_DIM
    wp = weights[:, : 4 * hd]
    wo = weights[:, 4 * hd :]
    row = jnp.arange(length, dtype=jnp.int32)
    pos = (row // 8) % Z * 64 + row // LANES * 8 + row % 8
    segment = jnp.sum((pos[:, None] >= ends[None, :]).astype(jnp.int32), axis=1)
    masked = (segment[:, None] == segment[None, :]) & (pos[None, :] <= pos[:, None])
    z_pre = jnp.dot(px, wp, preferred_element_type=F32)
    acted = jax.nn.silu(z_pre).astype(BF16)
    gating, value, query, key = (acted[:, m * hd : (m + 1) * hd] for m in range(4))
    scale = hd**-0.5
    scores = lax.dot_general(query, key, (((1,), (1,)), ((), ())), preferred_element_type=F32) * scale
    attn = jnp.where(masked, jax.nn.silu(scores), 0.0).astype(BF16)
    mixed = jnp.dot(attn, value, preferred_element_type=F32)
    centred = mixed - jnp.mean(mixed, axis=-1, keepdims=True)
    inv_std = lax.rsqrt(jnp.mean(centred * centred, axis=-1, keepdims=True) + NORM_FLOOR)
    normed = centred * inv_std
    gated = (normed * gating).astype(BF16)
    d_gated = jnp.dot(pdy, wo, preferred_element_type=F32)
    d_gate = d_gated * normed
    d_normed = d_gated * gating
    d_mixed = (
        inv_std
        * (
            d_normed
            - jnp.mean(d_normed, axis=-1, keepdims=True)
            - normed * jnp.mean(d_normed * normed, axis=-1, keepdims=True)
        )
    ).astype(BF16)
    d_attn = lax.dot_general(d_mixed, value, (((1,), (1,)), ((), ())), preferred_element_type=F32)
    d_scores = (jnp.where(masked, d_attn * silu_grad(scores), 0.0) * scale).astype(BF16)
    first = (((0,), (0,)), ((), ()))
    d_value = lax.dot_general(attn, d_mixed, first, preferred_element_type=F32)
    d_query = jnp.dot(d_scores, key, preferred_element_type=F32)
    d_key = lax.dot_general(d_scores, query, first, preferred_element_type=F32)
    d_act = jnp.concatenate([d_gate, d_value, d_query, d_key], axis=1)
    d_z = (d_act * silu_grad(z_pre)).astype(BF16)
    part = lax.dot_general(d_z, wp, (((1,), (1,)), ((), ())), preferred_element_type=F32).astype(BF16)
    grads = jnp.concatenate(
        [
            lax.dot_general(px, d_z, first, preferred_element_type=F32),
            lax.dot_general(pdy, gated, first, preferred_element_type=F32),
        ],
        axis=1,
    ).astype(BF16)
    return part, grads


def per_device(inputs, cotangent, lengths, item_ids, owner_row, w_project, w_output):
    width = inputs.shape[3]
    blocks = width // LANES
    core = lax.axis_index("c")
    y_here = lax.axis_index("y")
    z_here = lax.axis_index(SEQ)
    lane = jnp.arange(LANES, dtype=jnp.int32)

    slot, local_row = routing(item_ids, owner_row)
    lens = lengths.reshape(-1)
    lens_row = jnp.concatenate([lens // 256, lens % 256])
    lens_row = jnp.pad(lens_row, (0, LANES - lens_row.shape[0]))
    small = jnp.pad(jnp.stack([slot, local_row, lens_row]), ((0, 5), (0, 0))).astype(BF16)
    wp_tiles = w_project.reshape(ZR, 8, 2, LANES).transpose(0, 2, 1, 3)
    wo_t = w_output.T
    wo_tiles = jnp.concatenate([wo_t, wo_t], axis=1).reshape(ZR, 1, 8, LANES)
    small = jnp.broadcast_to(small[None, None], (ZR, 1, 8, LANES))
    w_tiles = jnp.concatenate([wp_tiles, wo_tiles, small], axis=1)

    both = jnp.stack([inputs[0], cotangent[0]]).reshape(2, 2, 8, 8, blocks, LANES)
    spread = exchange(both.transpose(2, 1, 0, 4, 3, 5), PAIR)
    spread = spread.reshape(Z, 2 * blocks, 8, LANES)
    w_tiles = jnp.broadcast_to(w_tiles[None], (ZQ, ZR, 4, 8, LANES)).reshape(Z, 4, 8, LANES)
    arrived = exchange(jnp.concatenate([spread, w_tiles], axis=1), SEQ)
    mine = arrived[:, : 2 * blocks].reshape(Z, 2, blocks, 8, LANES)
    mine = mine.transpose(1, 0, 3, 2, 4).reshape(2, Z * 8, width)
    packs = lax.all_gather(mine, PAIR, axis=1, tiled=True)

    by_head = exchange(arrived[:, 2 * blocks :].reshape(YC, 2, 4, 8, LANES), PAIR)
    wp_part = by_head[:, :, :2].transpose(0, 3, 1, 2, 4).reshape(YC, 8, 4 * HEAD_DIM)
    wo_part = jnp.where(lane < 64, by_head[:, 0, 2], by_head[:, 1, 2])
    w_part = jnp.concatenate([wp_part, wo_part], axis=2)
    w_all = jnp.broadcast_to(w_part[None], (X * ZR,) + w_part.shape)
    weights = exchange(w_all, SHARE).reshape(X, ZR, YC, 8, 5 * HEAD_DIM)
    weights = weights.transpose(0, 2, 1, 3, 4).reshape(width, 5 * HEAD_DIM)

    facts = by_head[:, :, 3].astype(F32)
    slots = facts[:, :, 0].astype(jnp.int32)
    tag_of = facts[:, :, 1]
    lens_all = facts[:, 0, 2, :12].reshape(YC, 2, 2, 3)
    lens_all = (lens_all[:, 0] * 256.0 + lens_all[:, 1]).astype(jnp.int32).reshape(Z, 3)
    pack_lens = lax.dynamic_index_in_dim(lens_all, z_here, 0, keepdims=False)
    ends = jnp.cumsum(pack_lens)

    part, grads = heads_backward(packs[0], packs[1], weights, ends)

    part = part.reshape(8, Y, C, 16, width)
    kept = lax.dynamic_index_in_dim(part, core, 2, keepdims=False)
    sent = lax.dynamic_index_in_dim(part, 1 - core, 2, keepdims=False)
    got = lax.ppermute(sent, "c", [(0, 1), (1, 0)])
    pair_sum = (kept.astype(F32) + got.astype(F32)).astype(BF16).transpose(1, 0, 2, 3)
    quad = lax.dynamic_index_in_dim(pair_sum, y_here, 0, keepdims=False).astype(F32)
    for step in range(1, Y):
        there = lax.dynamic_index_in_dim(pair_sum, (y_here + step) % Y, 0, keepdims=False)
        came = lax.ppermute(there, "y", [(i, (i + step) % Y) for i in range(Y)])
        quad = quad + came.astype(F32)
    own = y_here * C + core
    dy_own = lax.dynamic_index_in_dim(
        packs[1].reshape(8, YC, 16, width), own, 1, keepdims=False
    )
    token = (dy_own.astype(F32) + quad).astype(BF16)
    token = token.reshape(8, 2, 8, Z, 64).transpose(3, 0, 2, 1, 4).reshape(Z, 8, 8, LANES)

    grads = grads.reshape(X, YC, ZR, 8, 5 * HEAD_DIM).transpose(0, 2, 1, 3, 4)
    shared = exchange(grads.reshape(X * ZR, YC, 8, 5 * HEAD_DIM), SHARE)
    w_sum = jnp.sum(shared.astype(F32), axis=0).astype(BF16)
    wp_sum = w_sum[:, :, : 4 * HEAD_DIM].reshape(YC, 8, 2, 2, LANES)
    wp_sum = wp_sum.transpose(0, 2, 3, 1, 4).reshape(Z, 2, 8, LANES)
    wo_sum = w_sum[:, None, None, :, 4 * HEAD_DIM :]
    wo_sum = jnp.broadcast_to(wo_sum, (YC, 2, 1, 8, LANES)).reshape(Z, 1, 8, LANES)

    merged = exchange(jnp.concatenate([token, wp_sum, wo_sum], axis=1), SEQ)
    w_grad = jnp.sum(merged[:, 8:].astype(F32).reshape(ZQ, ZR, 3, 8, LANES), axis=0)
    turn = [
        ((x * YC + a) * Z + b * 2 + s, (x * YC + b) * Z + a * 2 + s)
        for x in range(X)
        for a in range(YC)
        for b in range(YC)
        for s in range(2)
    ]
    w_grad = lax.ppermute(w_grad, ALL, turn)
    grad_proj = w_grad[:, :2].transpose(0, 2, 1, 3).reshape(32, 2 * LANES)
    both_out = w_grad[:, 2].reshape(32, 2, 64)
    grad_out = lax.dynamic_index_in_dim(both_out, z_here % 2, 1, keepdims=False).T

    tokens = merged[:, :8].reshape(YC, LANES, LANES)
    slot_ids = jnp.arange(SLOTS, dtype=jnp.int32)
    placed = slots[:, :, None, :] == slot_ids[None, None, :, None]
    tags = jnp.sum(jnp.where(placed, tag_of[:, :, None, :], 0.0), axis=3)
    moved = jnp.einsum(
        "asut,atl->saul", placed.astype(BF16), tokens, preferred_element_type=F32
    )
    rows_out = jnp.where(lane < 64, moved[0], moved[1]).astype(BF16)
    rows_out = rows_out.reshape(YC, OWNERS, CAP, LANES).transpose(1, 0, 2, 3)
    tags = tags.reshape(YC, 2, OWNERS, CAP).transpose(2, 0, 1, 3).reshape(OWNERS, 1, 1, LANES)
    tags = jnp.pad(tags.astype(BF16), ((0, 0), (0, 0), (0, 7), (0, 0)))
    owned = exchange(jnp.concatenate([rows_out, tags], axis=1), DP)
    got_rows = owned[:, :YC].reshape(OWNERS * YC * CAP, LANES)
    got_tags = owned[:, YC, 0].astype(F32).astype(jnp.int32).reshape(OWNERS, YC, 2, CAP)
    got_tags = got_tags.transpose(2, 0, 1, 3).reshape(2, 1, OWNERS * YC * CAP)
    row_ids = jnp.arange(ROWS, dtype=jnp.int32)
    select = (got_tags == row_ids[None, :, None]).astype(BF16)
    sums = jnp.einsum("srk,kl->srl", select, got_rows, preferred_element_type=F32)
    grad_table = sums[0, :, :64] + sums[1, :, 64:]
    return (grad_proj, grad_out, grad_table)


def solution(mesh):
    fine = Mesh(mesh.devices.reshape(X, Y, C, ZQ, ZR), ALL)
    return jax.shard_map(
        per_device,
        mesh=fine,
        in_specs=(
            P(DP, None, SEQ, None),
            P(DP, None, SEQ, None),
            P(DP, None, None),
            P(DP, None, SEQ),
            P(),
            P(DP, SEQ),
            P(SEQ, DP),
        ),
        out_specs=(P(DP, SEQ), P(SEQ, DP), P(DP, SEQ)),
        check_vma=False,
    )
```

```python
import jax
import jax.numpy as jnp
from jax import lax
from jax.experimental import pallas as pl
from jax.experimental.pallas import tpu as pltpu
from jax.sharding import Mesh, PartitionSpec as P

HEAD_DIM = 128
NORM_FLOOR = 1.0
F32 = jnp.float32
BF16 = jnp.bfloat16

X, Y, C, ZQ, ZR = 4, 4, 2, 8, 2
YC = Y * C
Z = ZQ * ZR
PAIR = ("y", "c")
DP = ("x", "y", "c")
SEQ = ("zq", "zr")
SHARE = ("x", "zr")
ALL = ("x", "y", "c", "zq", "zr")
OWNERS = X * YC
CAP = 8
ROWS = 256
SLOTS = OWNERS * CAP
LANES = 128
LENGTH = 1024
WIDTH = 1024
HIDDEN = 5 * HEAD_DIM
PART_ROWS = 32 // ZR
STEP = 256


def exchange(value, axes):
    return lax.all_to_all(value, axes, split_axis=0, concat_axis=0, tiled=True)


def routing(item_ids, owner_row):
    rows = jnp.take(owner_row, item_ids.reshape(-1))
    owner = rows // ROWS
    count = owner.shape[0]
    order = jnp.arange(count, dtype=jnp.int32)
    before = (owner[None, :] == owner[:, None]) & (order[None, :] < order[:, None])
    rank = jnp.sum(before.astype(jnp.int32), axis=1)
    return owner * CAP + rank, rows % ROWS


def position(row):
    return ((row >> 3) & 15) * 64 + (row >> 7) * 8 + (row & 7)


def dot_nt(a, b):
    return lax.dot_general(a, b, (((1,), (1,)), ((), ())), preferred_element_type=F32)


def dot_tn(a, b):
    return lax.dot_general(a, b, (((0,), (0,)), ((), ())), preferred_element_type=F32)


def heads_kernel(info, packs, w_in, kept, sent, d_z, gated, w, acts, slope, d_value, d_key):
    hd = HEAD_DIM
    scale = hd**-0.5
    u_cols, v_cols, q_cols, k_cols = (slice(m * hd, (m + 1) * hd) for m in range(4))
    for x in range(X):
        for yc in range(YC):
            start = (x * YC + yc) * 32
            w[start : start + 32, :] = w_in[x, :, yc].reshape(32, HIDDEN)
    d_value[...] = jnp.zeros_like(d_value)
    d_key[...] = jnp.zeros_like(d_key)

    def project(step, carry):
        rows = pl.ds(pl.multiple_of(step * STEP, STEP), STEP)
        z_pre = jnp.dot(packs[0, rows, :], w[:, : 4 * hd], preferred_element_type=F32)
        sigma = jax.nn.sigmoid(z_pre)
        silu = z_pre * sigma
        acts[rows, :] = silu.astype(BF16)
        slope[rows, :] = sigma + silu * (1.0 - sigma)
        return carry

    lax.fori_loop(0, LENGTH // STEP, project, 0)

    pos_k = position(lax.broadcasted_iota(jnp.int32, (1, LENGTH), 1))
    ends = [info[n] for n in range(3)]

    def attend(step, carry):
        base = pl.multiple_of(step * STEP, STEP)
        rows = pl.ds(base, STEP)
        pos_q = position(lax.broadcasted_iota(jnp.int32, (STEP, 1), 0) + base)
        start = jnp.zeros_like(pos_q)
        for end in ends:
            start = jnp.where(pos_q >= end, end, start)
        masked = (pos_k <= pos_q) & (pos_k >= start)
        query = acts[rows, q_cols]
        key = acts[:, k_cols]
        value = acts[:, v_cols]
        scores = dot_nt(query, key) * scale
        sigma = jax.nn.sigmoid(scores)
        silu = scores * sigma
        attn = jnp.where(masked, silu, 0.0).astype(BF16)
        factor = jnp.where(masked, (sigma + silu * (1.0 - sigma)) * scale, 0.0)
        mixed = jnp.dot(attn, value, preferred_element_type=F32)
        centred = mixed - jnp.mean(mixed, axis=-1, keepdims=True)
        inv_std = lax.rsqrt(jnp.mean(centred * centred, axis=-1, keepdims=True) + NORM_FLOOR)
        normed = centred * inv_std
        gating = acts[rows, u_cols].astype(F32)
        gated[rows, :] = (normed * gating).astype(BF16)
        d_gated = jnp.dot(packs[1, rows, :], w[:, 4 * hd :], preferred_element_type=F32)
        d_normed = d_gated * gating
        d_mixed = (
            inv_std
            * (
                d_normed
                - jnp.mean(d_normed, axis=-1, keepdims=True)
                - normed * jnp.mean(d_normed * normed, axis=-1, keepdims=True)
            )
        ).astype(BF16)
        d_scores = (dot_nt(d_mixed, value) * factor).astype(BF16)
        d_query = jnp.dot(d_scores, key, preferred_element_type=F32)
        d_value[...] += dot_tn(attn, d_mixed)
        d_key[...] += dot_tn(d_scores, query)
        d_z[rows, u_cols] = (d_gated * normed * slope[rows, u_cols]).astype(BF16)
        d_z[rows, q_cols] = (d_query * slope[rows, q_cols]).astype(BF16)
        return carry

    lax.fori_loop(0, LENGTH // STEP, attend, 0)
    d_z[:, v_cols] = (d_value[...] * slope[:, v_cols]).astype(BF16)
    d_z[:, k_cols] = (d_key[...] * slope[:, k_cols]).astype(BF16)

    core = info[3]
    groups = STEP // LANES

    def parts(step, carry):
        rows = pl.ds(pl.multiple_of(step * STEP, STEP), STEP)
        part = dot_nt(d_z[rows, :], w[:, : 4 * hd]).astype(BF16)
        for g in range(groups):
            for y in range(Y):
                first = g * LANES + y * 32
                low, high = part[first : first + 16], part[first + 16 : first + 32]

                @pl.when(core == 0)
                def _():
                    kept[y, step * groups + g] = low
                    sent[y, step * groups + g] = high

                @pl.when(core != 0)
                def _():
                    kept[y, step * groups + g] = high
                    sent[y, step * groups + g] = low

        return carry

    lax.fori_loop(0, LENGTH // STEP, parts, 0)


def heads_backward(info, packs, weights):
    vmem = pl.BlockSpec(memory_space=pltpu.VMEM)
    half = jax.ShapeDtypeStruct((Y, 8, 16, WIDTH), BF16)
    return pl.pallas_call(
        heads_kernel,
        out_shape=(
            half,
            half,
            jax.ShapeDtypeStruct((LENGTH, 4 * HEAD_DIM), BF16),
            jax.ShapeDtypeStruct((LENGTH, HEAD_DIM), BF16),
        ),
        in_specs=[pl.BlockSpec(memory_space=pltpu.SMEM), vmem, vmem],
        out_specs=(vmem, vmem, vmem, vmem),
        scratch_shapes=[
            pltpu.VMEM((WIDTH, HIDDEN), BF16),
            pltpu.VMEM((LENGTH, 4 * HEAD_DIM), BF16),
            pltpu.VMEM((LENGTH, 4 * HEAD_DIM), F32),
            pltpu.VMEM((LENGTH, HEAD_DIM), F32),
            pltpu.VMEM((LENGTH, HEAD_DIM), F32),
        ],
        compiler_params=pltpu.CompilerParams(vmem_limit_bytes=44 * 2**20),
        cost_estimate=pl.CostEstimate(
            flops=4_600_000_000, bytes_accessed=9_000_000, transcendentals=3_000_000
        ),
        name="heads",
    )(info, packs, weights)


def grads_kernel(packs, d_z, gated, out):
    for x in range(X):
        cols = slice(x * YC * 32, (x + 1) * YC * 32)
        for dest, source, pack in ((slice(0, 512), d_z, 0), (slice(512, 640), gated, 1)):
            block = dot_tn(packs[pack, :, cols], source[...]).astype(BF16)
            for yc in range(YC):
                for r in range(ZR):
                    first = yc * 32 + r * PART_ROWS
                    out[x, r, yc, :, dest] = block[first : first + PART_ROWS]


def weight_grads(packs, d_z, gated):
    vmem = pl.BlockSpec(memory_space=pltpu.VMEM)
    return pl.pallas_call(
        grads_kernel,
        out_shape=jax.ShapeDtypeStruct((X, ZR, YC, PART_ROWS, HIDDEN), BF16),
        in_specs=[vmem, vmem, vmem],
        out_specs=vmem,
        compiler_params=pltpu.CompilerParams(vmem_limit_bytes=32 * 2**20),
        cost_estimate=pl.CostEstimate(
            flops=1_350_000_000, bytes_accessed=6_800_000, transcendentals=0
        ),
        name="weight_grads",
    )(packs, d_z, gated)


def per_device(inputs, cotangent, lengths, item_ids, owner_row, w_project, w_output):
    width = inputs.shape[3]
    blocks = width // LANES
    core = lax.axis_index("c")
    y_here = lax.axis_index("y")
    z_here = lax.axis_index(SEQ)
    lane = jnp.arange(LANES, dtype=jnp.int32)

    slot, local_row = routing(item_ids, owner_row)
    lens = lengths.reshape(-1)
    lens_row = jnp.concatenate([lens // 256, lens % 256])
    lens_row = jnp.pad(lens_row, (0, LANES - lens_row.shape[0]))
    small = jnp.pad(jnp.stack([slot, local_row, lens_row]), ((0, 5), (0, 0))).astype(BF16)
    high = PART_ROWS // 8
    n_w = 3 * high + 1
    wp_tiles = w_project.reshape(ZR, high, 8, 2, LANES).transpose(0, 1, 3, 2, 4)
    wo_t = w_output.T
    wo_tiles = jnp.concatenate([wo_t, wo_t], axis=1).reshape(ZR, high, 8, LANES)
    small = jnp.broadcast_to(small[None, None], (ZR, 1, 8, LANES))
    w_tiles = jnp.concatenate([wp_tiles.reshape(ZR, 2 * high, 8, LANES), wo_tiles, small], axis=1)

    both = jnp.stack([inputs[0], cotangent[0]]).reshape(2, 2, 8, 8, blocks, LANES)
    spread = exchange(both.transpose(2, 1, 0, 4, 3, 5), PAIR)
    spread = spread.reshape(Z, 2 * blocks, 8, LANES)
    w_tiles = jnp.broadcast_to(w_tiles[None], (ZQ, ZR, n_w, 8, LANES)).reshape(Z, n_w, 8, LANES)
    arrived = exchange(jnp.concatenate([spread, w_tiles], axis=1), SEQ)
    mine = arrived[:, : 2 * blocks].reshape(Z, 2, blocks, 8, LANES)
    mine = mine.transpose(1, 0, 3, 2, 4).reshape(2, Z * 8, width)
    packs = lax.all_gather(mine, PAIR, axis=1, tiled=True)

    by_head = exchange(arrived[:, 2 * blocks :].reshape(YC, 2, n_w, 8, LANES), PAIR)
    wp_part = by_head[:, :, : 2 * high].reshape(YC, 2, high, 2, 8, LANES)
    wp_part = wp_part.transpose(0, 2, 4, 1, 3, 5).reshape(YC, PART_ROWS, 4 * HEAD_DIM)
    wo_part = by_head[:, :, 2 * high : 3 * high]
    wo_part = jnp.where(lane < 64, wo_part[:, 0], wo_part[:, 1])
    w_part = jnp.concatenate([wp_part, wo_part.reshape(YC, PART_ROWS, HEAD_DIM)], axis=2)
    w_all = jnp.broadcast_to(w_part[None], (X * ZR,) + w_part.shape)
    weights = exchange(w_all, SHARE).reshape(X, ZR, YC, PART_ROWS, HIDDEN)

    facts = by_head[:, :, n_w - 1].astype(F32)
    slots = facts[:, :, 0].astype(jnp.int32)
    tag_of = facts[:, :, 1]
    lens_all = facts[:, 0, 2, :12].reshape(YC, 2, 2, 3)
    lens_all = (lens_all[:, 0] * 256.0 + lens_all[:, 1]).astype(jnp.int32).reshape(Z, 3)
    pack_lens = lax.dynamic_index_in_dim(lens_all, z_here, 0, keepdims=False)
    ends = jnp.cumsum(pack_lens)

    info = jnp.concatenate([ends, core[None]]).astype(jnp.int32)
    kept, sent, d_z, gated = heads_backward(info, packs, weights)

    got = lax.ppermute(sent, "c", [(0, 1), (1, 0)])
    pair_sum = (kept.astype(F32) + got.astype(F32)).astype(BF16)
    quad = lax.dynamic_index_in_dim(pair_sum, y_here, 0, keepdims=False).astype(F32)
    for step in range(1, Y):
        there = lax.dynamic_index_in_dim(pair_sum, (y_here + step) % Y, 0, keepdims=False)
        came = lax.ppermute(there, "y", [(i, (i + step) % Y) for i in range(Y)])
        quad = quad + came.astype(F32)
    own = y_here * C + core
    dy_own = lax.dynamic_index_in_dim(
        packs[1].reshape(8, YC, 16, width), own, 1, keepdims=False
    )
    token = (dy_own.astype(F32) + quad).astype(BF16)
    token = token.reshape(8, 2, 8, Z, 64).transpose(3, 0, 2, 1, 4).reshape(Z, 8, 8, LANES)

    grads = weight_grads(packs, d_z, gated)
    shared = exchange(grads.reshape(X * ZR, YC, PART_ROWS, HIDDEN), SHARE)
    w_sum = jnp.sum(shared.astype(F32), axis=0).astype(BF16)
    wp_sum = w_sum[:, :, : 4 * HEAD_DIM].reshape(YC, high, 8, 2, 2, LANES)
    wp_sum = wp_sum.transpose(0, 3, 1, 4, 2, 5).reshape(Z, 2 * high, 8, LANES)
    wo_sum = w_sum[:, None, :, 4 * HEAD_DIM :]
    wo_sum = jnp.broadcast_to(wo_sum, (YC, 2, PART_ROWS, LANES)).reshape(Z, high, 8, LANES)

    merged = exchange(jnp.concatenate([token, wp_sum, wo_sum], axis=1), SEQ)
    w_grad = jnp.sum(merged[:, 8:].astype(F32).reshape(ZQ, ZR, 3 * high, 8, LANES), axis=0)
    turn = [
        ((x * YC + a) * Z + b * 2 + s, (x * YC + b) * Z + a * 2 + s)
        for x in range(X)
        for a in range(YC)
        for b in range(YC)
        for s in range(2)
    ]
    w_grad = lax.ppermute(w_grad, ALL, turn)
    grad_proj = w_grad[:, : 2 * high].reshape(ZR, high, 2, 8, LANES)
    grad_proj = grad_proj.transpose(0, 1, 3, 2, 4).reshape(32, 2 * LANES)
    both_out = w_grad[:, 2 * high :].reshape(32, 2, 64)
    grad_out = lax.dynamic_index_in_dim(both_out, z_here % 2, 1, keepdims=False).T

    tokens = merged[:, :8].reshape(YC, LANES, LANES)
    slot_ids = jnp.arange(SLOTS, dtype=jnp.int32)
    placed = slots[:, :, None, :] == slot_ids[None, None, :, None]
    tags = jnp.sum(jnp.where(placed, tag_of[:, :, None, :], 0.0), axis=3)
    moved = jnp.einsum(
        "asut,atl->saul", placed.astype(BF16), tokens, preferred_element_type=F32
    )
    rows_out = jnp.where(lane < 64, moved[0], moved[1]).astype(BF16)
    rows_out = rows_out.reshape(YC, OWNERS, CAP, LANES).transpose(1, 0, 2, 3)
    tags = tags.reshape(YC, 2, OWNERS, CAP).transpose(2, 0, 1, 3).reshape(OWNERS, 1, 1, LANES)
    tags = jnp.pad(tags.astype(BF16), ((0, 0), (0, 0), (0, 7), (0, 0)))
    owned = exchange(jnp.concatenate([rows_out, tags], axis=1), DP)
    got_rows = owned[:, :YC].reshape(OWNERS * YC * CAP, LANES)
    got_tags = owned[:, YC, 0].astype(F32).astype(jnp.int32).reshape(OWNERS, YC, 2, CAP)
    got_tags = got_tags.transpose(2, 0, 1, 3).reshape(2, 1, OWNERS * YC * CAP)
    row_ids = jnp.arange(ROWS, dtype=jnp.int32)
    select = (got_tags == row_ids[None, :, None]).astype(BF16)
    sums = jnp.einsum("srk,kl->srl", select, got_rows, preferred_element_type=F32)
    grad_table = sums[0, :, :64] + sums[1, :, 64:]
    return (grad_proj, grad_out, grad_table)


def solution(mesh):
    fine = Mesh(mesh.devices.reshape(X, Y, C, ZQ, ZR), ALL)
    return jax.shard_map(
        per_device,
        mesh=fine,
        in_specs=(
            P(DP, None, SEQ, None),
            P(DP, None, SEQ, None),
            P(DP, None, None),
            P(DP, None, SEQ),
            P(),
            P(DP, SEQ),
            P(SEQ, DP),
        ),
        out_specs=(P(DP, SEQ), P(SEQ, DP), P(DP, SEQ)),
        check_vma=False,
    )
```

```python
import jax
import jax.numpy as jnp
from jax import lax
from jax.experimental import pallas as pl
from jax.experimental.pallas import tpu as pltpu
from jax.sharding import Mesh, PartitionSpec as P

HEAD_DIM = 128
NORM_FLOOR = 1.0
F32 = jnp.float32
BF16 = jnp.bfloat16

X, Y, C, ZQ, ZR = 4, 4, 2, 8, 2
YC = Y * C
Z = ZQ * ZR
PAIR = ("y", "c")
DP = ("x", "y", "c")
SEQ = ("zq", "zr")
SHARE = ("x", "zr")
SPREAD = ("x", "y", "c", "zr")
ALL = ("x", "y", "c", "zq", "zr")
OWNERS = X * YC
CAP = 8
ROWS = 256
SLOTS = OWNERS * CAP
LANES = 128
LENGTH = 1024
WIDTH = 1024
HIDDEN = 5 * HEAD_DIM
PART_ROWS = 32 // ZR
STEP = 256
REACH = 512


def exchange(value, axes):
    return lax.all_to_all(value, axes, split_axis=0, concat_axis=0, tiled=True)


def routing(item_ids, owner_row):
    rows = jnp.take(owner_row, item_ids.reshape(-1))
    owner = rows // ROWS
    count = owner.shape[0]
    order = jnp.arange(count, dtype=jnp.int32)
    before = (owner[None, :] == owner[:, None]) & (order[None, :] < order[:, None])
    rank = jnp.sum(before.astype(jnp.int32), axis=1)
    return owner * CAP + rank, rows % ROWS


def dot_nt(a, b):
    return lax.dot_general(a, b, (((1,), (1,)), ((), ())), preferred_element_type=F32)


def dot_tn(a, b):
    return lax.dot_general(a, b, (((0,), (0,)), ((), ())), preferred_element_type=F32)


def heads_kernel(
    info, packs, w_in, kept, sent, grads, x_v, dy_v, w, acts, slope, d_value, d_key, d_z, gated, sems
):
    hd = HEAD_DIM
    scale = hd**-0.5
    u_cols, v_cols, q_cols, k_cols = (slice(m * hd, (m + 1) * hd) for m in range(4))
    x_copy = pltpu.make_async_copy(packs.at[:, 0], x_v, sems.at[0])
    dy_copy = pltpu.make_async_copy(packs.at[:, 1], dy_v, sems.at[1])
    x_copy.start()
    dy_copy.start()
    for x in range(X):
        for yc in range(YC):
            start = (x * YC + yc) * 32
            w[start : start + 32, :] = w_in[x, :, yc].reshape(32, HIDDEN)
    d_value[...] = jnp.zeros_like(d_value)
    d_key[...] = jnp.zeros_like(d_key)
    x_copy.wait()

    def project(step, carry):
        rows = pl.ds(pl.multiple_of(step * STEP, STEP), STEP)
        px = jnp.concatenate([x_v[g, rows, :] for g in range(8)], axis=1)
        z_pre = jnp.dot(px, w[:, : 4 * hd], preferred_element_type=F32)
        sigma = jax.nn.sigmoid(z_pre)
        silu = z_pre * sigma
        acts[rows, :] = silu.astype(BF16)
        slope[rows, :] = sigma + silu * (1.0 - sigma)
        return carry

    lax.fori_loop(0, LENGTH // STEP, project, 0)
    dy_copy.wait()

    for step in range(LENGTH // STEP):
        base = step * STEP
        first = max(0, base - REACH)
        rows = slice(base, base + STEP)
        span = slice(first, base + STEP)
        pos_k = lax.broadcasted_iota(jnp.int32, (1, base + STEP - first), 1) + first
        pos_q = lax.broadcasted_iota(jnp.int32, (STEP, 1), 0) + base
        start = jnp.zeros_like(pos_q)
        for n in range(3):
            start = jnp.where(pos_q >= info[n], info[n], start)
        masked = (pos_k <= pos_q) & (pos_k >= start)
        query = acts[rows, q_cols]
        key = acts[span, k_cols]
        value = acts[span, v_cols]
        scores = dot_nt(query, key) * scale
        sigma = jax.nn.sigmoid(scores)
        silu = scores * sigma
        attn = jnp.where(masked, silu, 0.0).astype(BF16)
        factor = jnp.where(masked, (sigma + silu * (1.0 - sigma)) * scale, 0.0)
        mixed = jnp.dot(attn, value, preferred_element_type=F32)
        centred = mixed - jnp.mean(mixed, axis=-1, keepdims=True)
        inv_std = lax.rsqrt(jnp.mean(centred * centred, axis=-1, keepdims=True) + NORM_FLOOR)
        normed = centred * inv_std
        gating = acts[rows, u_cols].astype(F32)
        gated[rows, :] = (normed * gating).astype(BF16)
        pdy = jnp.concatenate([dy_v[g, rows, :] for g in range(8)], axis=1)
        d_gated = jnp.dot(pdy, w[:, 4 * hd :], preferred_element_type=F32)
        d_normed = d_gated * gating
        d_mixed = (
            inv_std
            * (
                d_normed
                - jnp.mean(d_normed, axis=-1, keepdims=True)
                - normed * jnp.mean(d_normed * normed, axis=-1, keepdims=True)
            )
        ).astype(BF16)
        d_scores = (dot_nt(d_mixed, value) * factor).astype(BF16)
        d_query = jnp.dot(d_scores, key, preferred_element_type=F32)
        d_value[span, :] += dot_tn(attn, d_mixed)
        d_key[span, :] += dot_tn(d_scores, query)
        d_z[rows, u_cols] = (d_gated * normed * slope[rows, u_cols]).astype(BF16)
        d_z[rows, q_cols] = (d_query * slope[rows, q_cols]).astype(BF16)

    d_z[:, v_cols] = (d_value[...] * slope[:, v_cols]).astype(BF16)
    d_z[:, k_cols] = (d_key[...] * slope[:, k_cols]).astype(BF16)

    core = info[3]

    def parts(step, carry):
        rows = pl.ds(pl.multiple_of(step * STEP, STEP), STEP)
        part = dot_nt(d_z[rows, :], w[:, : 4 * hd]).astype(BF16)

        @pl.when(core == 0)
        def _():
            kept[step] = part[:LANES]
            sent[step] = part[LANES:]

        @pl.when(core != 0)
        def _():
            kept[step] = part[LANES:]
            sent[step] = part[:LANES]

        return carry

    lax.fori_loop(0, Y, parts, 0)

    for x in range(X):
        for dest, source, pack in ((slice(0, 512), d_z, x_v), (slice(512, 640), gated, dy_v)):
            columns = jnp.concatenate([pack[2 * x], pack[2 * x + 1]], axis=1)
            block = dot_tn(columns, source[...]).astype(BF16)
            for yc in range(YC):
                for r in range(ZR):
                    at = yc * 32 + r * PART_ROWS
                    grads[x, yc, r, :, dest] = block[at : at + PART_ROWS]


def heads_backward(info, packs, weights):
    vmem = pl.BlockSpec(memory_space=pltpu.VMEM)
    half = jax.ShapeDtypeStruct((Y, LANES, WIDTH), BF16)
    return pl.pallas_call(
        heads_kernel,
        out_shape=(
            half,
            half,
            jax.ShapeDtypeStruct((X, YC, ZR, PART_ROWS, HIDDEN), BF16),
        ),
        in_specs=[
            pl.BlockSpec(memory_space=pltpu.SMEM),
            pl.BlockSpec(memory_space=pltpu.HBM),
            vmem,
        ],
        out_specs=(vmem, vmem, vmem),
        scratch_shapes=[
            pltpu.VMEM((8, LENGTH, LANES), BF16),
            pltpu.VMEM((8, LENGTH, LANES), BF16),
            pltpu.VMEM((WIDTH, HIDDEN), BF16),
            pltpu.VMEM((LENGTH, 4 * HEAD_DIM), BF16),
            pltpu.VMEM((LENGTH, 4 * HEAD_DIM), F32),
            pltpu.VMEM((LENGTH, HEAD_DIM), F32),
            pltpu.VMEM((LENGTH, HEAD_DIM), F32),
            pltpu.VMEM((LENGTH, 4 * HEAD_DIM), BF16),
            pltpu.VMEM((LENGTH, HEAD_DIM), BF16),
            pltpu.SemaphoreType.DMA((2,)),
        ],
        compiler_params=pltpu.CompilerParams(vmem_limit_bytes=44 * 2**20),
        cost_estimate=pl.CostEstimate(
            flops=5_000_000_000, bytes_accessed=9_000_000, transcendentals=2_000_000
        ),
        name="heads",
    )(info, packs, weights)


def per_device(inputs, cotangent, lengths, item_ids, owner_row, w_project, w_output):
    core = lax.axis_index("c")
    y_here = lax.axis_index("y")
    z_here = lax.axis_index(SEQ)
    lane = jnp.arange(LANES, dtype=jnp.int32)

    slot, local_row = routing(item_ids, owner_row)
    lens = lengths.reshape(-1)
    lens_row = jnp.concatenate([lens // 256, lens % 256])
    lens_row = jnp.pad(lens_row, (0, LANES - lens_row.shape[0]))
    small = jnp.pad(jnp.stack([slot, local_row, lens_row]), ((0, 5), (0, 0))).astype(BF16)
    high = PART_ROWS // 8
    n_w = 3 * high + 1
    wp_tiles = w_project.reshape(ZR, high, 8, 2, LANES).transpose(0, 1, 3, 2, 4)
    wo_t = w_output.T
    wo_tiles = jnp.concatenate([wo_t, wo_t], axis=1).reshape(ZR, high, 8, LANES)
    small = jnp.broadcast_to(small[None, None], (ZR, 1, 8, LANES))
    w_tiles = jnp.concatenate([wp_tiles.reshape(ZR, 2 * high, 8, LANES), wo_tiles, small], axis=1)

    both = jnp.stack([inputs[0], cotangent[0]]).reshape(2, 2, 64, 8, LANES)
    spread = exchange(both.transpose(3, 1, 0, 2, 4), PAIR)
    spread = spread.reshape(Z, 16, 8, LANES)
    w_tiles = jnp.broadcast_to(w_tiles[None], (ZQ, ZR, n_w, 8, LANES)).reshape(Z, n_w, 8, LANES)
    arrived = exchange(jnp.concatenate([spread, w_tiles], axis=1), SEQ)
    mine = arrived[:, :16].reshape(Z, 2, 64, LANES).transpose(1, 0, 2, 3)
    packs = lax.all_gather(mine.reshape(1, 2, LENGTH, LANES), PAIR, axis=0, tiled=True)

    by_head = exchange(arrived[:, 16:].reshape(YC, 2, n_w, 8, LANES), PAIR)
    wp_part = by_head[:, :, : 2 * high].reshape(YC, 2, high, 2, 8, LANES)
    wp_part = wp_part.transpose(0, 2, 4, 1, 3, 5).reshape(YC, PART_ROWS, 4 * HEAD_DIM)
    wo_part = by_head[:, :, 2 * high : 3 * high]
    wo_part = jnp.where(lane < 64, wo_part[:, 0], wo_part[:, 1])
    w_part = jnp.concatenate([wp_part, wo_part.reshape(YC, PART_ROWS, HEAD_DIM)], axis=2)
    w_all = jnp.broadcast_to(w_part[None], (X * ZR,) + w_part.shape)
    weights = exchange(w_all, SHARE).reshape(X, ZR, YC, PART_ROWS, HIDDEN)

    facts = by_head[:, :, n_w - 1].astype(F32)
    slots = facts[:, :, 0].astype(jnp.int32)
    tag_of = facts[:, :, 1]
    lens_all = facts[:, 0, 2, :12].reshape(YC, 2, 2, 3)
    lens_all = (lens_all[:, 0] * 256.0 + lens_all[:, 1]).astype(jnp.int32).reshape(Z, 3)
    pack_lens = lax.dynamic_index_in_dim(lens_all, z_here, 0, keepdims=False)
    ends = jnp.cumsum(pack_lens)

    info = jnp.concatenate([ends, core[None]]).astype(jnp.int32)
    kept, sent, grads = heads_backward(info, packs, weights)

    shared = exchange(grads.reshape(X * YC * ZR, PART_ROWS, HIDDEN), SPREAD)
    shared = shared.reshape(X, YC, ZR, PART_ROWS, HIDDEN)
    w_sum = jnp.sum(shared.astype(F32), axis=(0, 2)).astype(BF16)
    wp_sum = w_sum[:, :, : 4 * HEAD_DIM].reshape(YC, high, 8, 2, 2, LANES)
    wp_sum = wp_sum.transpose(0, 3, 1, 4, 2, 5).reshape(Z, 2 * high, 8, LANES)
    wo_sum = w_sum[:, None, :, 4 * HEAD_DIM :]
    wo_sum = jnp.broadcast_to(wo_sum, (YC, 2, PART_ROWS, LANES)).reshape(Z, high, 8, LANES)

    got = lax.ppermute(sent, "c", [(0, 1), (1, 0)])
    pair_sum = (kept.astype(F32) + got.astype(F32)).astype(BF16)
    quad = lax.dynamic_index_in_dim(pair_sum, y_here, 0, keepdims=False).astype(F32)
    for step in range(1, Y):
        there = lax.dynamic_index_in_dim(pair_sum, (y_here + step) & (Y - 1), 0, keepdims=False)
        came = lax.ppermute(there, "y", [(i, (i + step) % Y) for i in range(Y)])
        quad = quad + came.astype(F32)
    own = y_here * C + core
    dy_own = lax.dynamic_slice(packs, (0, 1, own * LANES, 0), (YC, 1, LANES, LANES))
    dy_own = dy_own[:, 0].transpose(1, 0, 2).reshape(LANES, WIDTH)
    token = (dy_own.astype(F32) + quad).astype(BF16)
    token = token.reshape(2, 64, Z, 64).transpose(2, 1, 0, 3).reshape(Z, 8, 8, LANES)

    merged = exchange(jnp.concatenate([token, wp_sum, wo_sum], axis=1), SEQ)
    w_grad = jnp.sum(merged[:, 8:].astype(F32).reshape(ZQ, ZR, 3 * high, 8, LANES), axis=0)
    grad_proj = w_grad[:, : 2 * high].reshape(ZR, high, 2, 8, LANES)
    grad_proj = grad_proj.transpose(0, 1, 3, 2, 4).reshape(32, 2 * LANES)
    both_out = w_grad[:, 2 * high :].reshape(32, 2, 64)
    grad_out = lax.dynamic_index_in_dim(both_out, z_here % 2, 1, keepdims=False).T

    tokens = merged[:, :8].reshape(YC, LANES, LANES)
    slot_ids = jnp.arange(SLOTS, dtype=jnp.int32)
    placed = slots[:, :, None, :] == slot_ids[None, None, :, None]
    tags = jnp.sum(jnp.where(placed, tag_of[:, :, None, :], 0.0), axis=3)
    moved = jnp.einsum(
        "asut,atl->saul", placed.astype(BF16), tokens, preferred_element_type=F32
    )
    rows_out = jnp.where(lane < 64, moved[0], moved[1]).astype(BF16)
    rows_out = rows_out.reshape(YC, OWNERS, CAP, LANES).transpose(1, 0, 2, 3)
    tags = tags.reshape(YC, 2, OWNERS, CAP).transpose(2, 0, 1, 3).reshape(OWNERS, 1, 1, LANES)
    tags = jnp.pad(tags.astype(BF16), ((0, 0), (0, 0), (0, 7), (0, 0)))
    owned = exchange(jnp.concatenate([rows_out, tags], axis=1), DP)
    got_rows = owned[:, :YC].reshape(OWNERS * YC * CAP, LANES)
    got_tags = owned[:, YC, 0].astype(F32).astype(jnp.int32).reshape(OWNERS, YC, 2, CAP)
    got_tags = got_tags.transpose(2, 0, 1, 3).reshape(2, 1, OWNERS * YC * CAP)
    row_ids = jnp.arange(ROWS, dtype=jnp.int32)
    select = (got_tags == row_ids[None, :, None]).astype(BF16)
    sums = jnp.einsum("srk,kl->srl", select, got_rows, preferred_element_type=F32)
    grad_table = sums[0, :, :64] + sums[1, :, 64:]
    return (grad_proj, grad_out, grad_table)


def solution(mesh):
    fine = Mesh(mesh.devices.reshape(X, Y, C, ZQ, ZR), ALL)
    return jax.shard_map(
        per_device,
        mesh=fine,
        in_specs=(
            P(DP, None, SEQ, None),
            P(DP, None, SEQ, None),
            P(DP, None, None),
            P(DP, None, SEQ),
            P(),
            P(DP, SEQ),
            P(SEQ, DP),
        ),
        out_specs=(P(DP, SEQ), P(SEQ, DP), P(DP, SEQ)),
        check_vma=False,
    )
```

```python
import jax
import jax.numpy as jnp
from jax import lax
from jax.experimental import pallas as pl
from jax.experimental.pallas import tpu as pltpu
from jax.sharding import Mesh, PartitionSpec as P

HEAD_DIM = 128
NORM_FLOOR = 1.0
F32 = jnp.float32
BF16 = jnp.bfloat16

X, Y, C, ZQ, ZR = 4, 4, 2, 8, 2
YC = Y * C
Z = ZQ * ZR
PAIR = ("y", "c")
DP = ("x", "y", "c")
SEQ = ("zq", "zr")
SHARE = ("x", "zr")
SPREAD = ("x", "y", "c", "zr")
ALL = ("x", "y", "c", "zq", "zr")
OWNERS = X * YC
CAP = 8
ROWS = 256
SLOTS = OWNERS * CAP
LANES = 128
LENGTH = 1024
WIDTH = 1024
HIDDEN = 5 * HEAD_DIM
PART_ROWS = 32 // ZR
STEP = 256
REACH = 512
VMEM_SPEC = pl.BlockSpec(memory_space=pltpu.VMEM)
SMEM_SPEC = pl.BlockSpec(memory_space=pltpu.SMEM)


def exchange(value, axes):
    return lax.all_to_all(value, axes, split_axis=0, concat_axis=0, tiled=True)


def routing(item_ids, owner_row):
    rows = jnp.take(owner_row, item_ids.reshape(-1))
    owner = rows // ROWS
    count = owner.shape[0]
    order = jnp.arange(count, dtype=jnp.int32)
    before = (owner[None, :] == owner[:, None]) & (order[None, :] < order[:, None])
    rank = jnp.sum(before.astype(jnp.int32), axis=1)
    return owner * CAP + rank, rows % ROWS


def dot_nt(a, b):
    return lax.dot_general(a, b, (((1,), (1,)), ((), ())), preferred_element_type=F32)


def dot_tn(a, b):
    return lax.dot_general(a, b, (((0,), (0,)), ((), ())), preferred_element_type=F32)


def heads_kernel(info, packs, w_in, kept, sent, d_z, gated, w, acts, slope, d_value, d_key):
    hd = HEAD_DIM
    scale = hd**-0.5
    u_cols, v_cols, q_cols, k_cols = (slice(m * hd, (m + 1) * hd) for m in range(4))
    for x in range(X):
        for yc in range(YC):
            start = (x * YC + yc) * 32
            w[start : start + 32, :] = w_in[x, :, yc].reshape(32, HIDDEN)
    d_value[...] = jnp.zeros_like(d_value)
    d_key[...] = jnp.zeros_like(d_key)

    def project(step, carry):
        rows = pl.ds(pl.multiple_of(step * STEP, STEP), STEP)
        px = jnp.concatenate([packs[g, 0, rows, :] for g in range(8)], axis=1)
        z_pre = jnp.dot(px, w[:, : 4 * hd], preferred_element_type=F32)
        sigma = jax.nn.sigmoid(z_pre)
        silu = z_pre * sigma
        acts[rows, :] = silu.astype(BF16)
        slope[rows, :] = sigma + silu * (1.0 - sigma)
        return carry

    lax.fori_loop(0, LENGTH // STEP, project, 0)

    for step in range(LENGTH // STEP):
        base = step * STEP
        first = max(0, base - REACH)
        rows = slice(base, base + STEP)
        span = slice(first, base + STEP)
        pos_k = lax.broadcasted_iota(jnp.int32, (1, base + STEP - first), 1) + first
        pos_q = lax.broadcasted_iota(jnp.int32, (STEP, 1), 0) + base
        start = jnp.zeros_like(pos_q)
        for n in range(3):
            start = jnp.where(pos_q >= info[n], info[n], start)
        masked = (pos_k <= pos_q) & (pos_k >= start)
        query = acts[rows, q_cols]
        key = acts[span, k_cols]
        value = acts[span, v_cols]
        scores = dot_nt(query, key) * scale
        sigma = jax.nn.sigmoid(scores)
        silu = scores * sigma
        attn = jnp.where(masked, silu, 0.0).astype(BF16)
        factor = jnp.where(masked, (sigma + silu * (1.0 - sigma)) * scale, 0.0)
        mixed = jnp.dot(attn, value, preferred_element_type=F32)
        centred = mixed - jnp.mean(mixed, axis=-1, keepdims=True)
        inv_std = lax.rsqrt(jnp.mean(centred * centred, axis=-1, keepdims=True) + NORM_FLOOR)
        normed = centred * inv_std
        gating = acts[rows, u_cols].astype(F32)
        gated[rows, :] = (normed * gating).astype(BF16)
        pdy = jnp.concatenate([packs[g, 1, rows, :] for g in range(8)], axis=1)
        d_gated = jnp.dot(pdy, w[:, 4 * hd :], preferred_element_type=F32)
        d_normed = d_gated * gating
        d_mixed = (
            inv_std
            * (
                d_normed
                - jnp.mean(d_normed, axis=-1, keepdims=True)
                - normed * jnp.mean(d_normed * normed, axis=-1, keepdims=True)
            )
        ).astype(BF16)
        d_scores = (dot_nt(d_mixed, value) * factor).astype(BF16)
        d_query = jnp.dot(d_scores, key, preferred_element_type=F32)
        d_value[span, :] += dot_tn(attn, d_mixed)
        d_key[span, :] += dot_tn(d_scores, query)
        d_z[rows, u_cols] = (d_gated * normed * slope[rows, u_cols]).astype(BF16)
        d_z[rows, q_cols] = (d_query * slope[rows, q_cols]).astype(BF16)

    d_z[:, v_cols] = (d_value[...] * slope[:, v_cols]).astype(BF16)
    d_z[:, k_cols] = (d_key[...] * slope[:, k_cols]).astype(BF16)

    core = info[3]

    def parts(step, carry):
        rows = pl.ds(pl.multiple_of(step * STEP, STEP), STEP)
        part = dot_nt(d_z[rows, :], w[:, : 4 * hd]).astype(BF16)

        @pl.when(core == 0)
        def _():
            kept[step] = part[:LANES]
            sent[step] = part[LANES:]

        @pl.when(core != 0)
        def _():
            kept[step] = part[LANES:]
            sent[step] = part[:LANES]

        return carry

    lax.fori_loop(0, Y, parts, 0)


def heads_backward(info, packs, weights):
    half = jax.ShapeDtypeStruct((Y, LANES, WIDTH), BF16)
    return pl.pallas_call(
        heads_kernel,
        out_shape=(
            half,
            half,
            jax.ShapeDtypeStruct((LENGTH, 4 * HEAD_DIM), BF16),
            jax.ShapeDtypeStruct((LENGTH, HEAD_DIM), BF16),
        ),
        in_specs=[SMEM_SPEC, VMEM_SPEC, VMEM_SPEC],
        out_specs=(VMEM_SPEC,) * 4,
        scratch_shapes=[
            pltpu.VMEM((WIDTH, HIDDEN), BF16),
            pltpu.VMEM((LENGTH, 4 * HEAD_DIM), BF16),
            pltpu.VMEM((LENGTH, 4 * HEAD_DIM), F32),
            pltpu.VMEM((LENGTH, HEAD_DIM), F32),
            pltpu.VMEM((LENGTH, HEAD_DIM), F32),
        ],
        compiler_params=pltpu.CompilerParams(vmem_limit_bytes=44 * 2**20),
        cost_estimate=pl.CostEstimate(
            flops=4_000_000_000, bytes_accessed=9_000_000, transcendentals=2_000_000
        ),
        name="heads",
    )(info, packs, weights)


def grads_kernel(packs, d_z, gated, tags, out):
    for x in range(X):
        for dest, source, t in ((slice(0, 512), d_z, 0), (slice(512, 640), gated, 1)):
            columns = jnp.concatenate([packs[2 * x, t], packs[2 * x + 1, t]], axis=1)
            block = dot_tn(columns, source[...]).astype(BF16)
            for yc in range(YC):
                for r in range(ZR):
                    at = yc * 32 + r * PART_ROWS
                    out[x, yc, r, :, dest] = block[at : at + PART_ROWS]
    for x in range(X):
        for yc in range(YC):
            for r in range(ZR):
                out[x, yc, r, :, HIDDEN:] = tags[x * YC + yc]


def weight_grads(packs, d_z, gated, tags):
    return pl.pallas_call(
        grads_kernel,
        out_shape=jax.ShapeDtypeStruct((X, YC, ZR, PART_ROWS, HIDDEN + LANES), BF16),
        in_specs=[VMEM_SPEC] * 4,
        out_specs=VMEM_SPEC,
        compiler_params=pltpu.CompilerParams(vmem_limit_bytes=32 * 2**20),
        cost_estimate=pl.CostEstimate(
            flops=1_350_000_000, bytes_accessed=6_800_000, transcendentals=0
        ),
        name="weight_grads",
    )(packs, d_z, gated, tags)


def pair_kernel(place, kept, got, own, *to_y):
    y = place[0]
    own[...] = kept[y].astype(F32) + got[y].astype(F32)
    for step in range(1, Y):
        other = (y + step) & (Y - 1)
        to_y[step - 1][...] = (kept[other].astype(F32) + got[other].astype(F32)).astype(BF16)


def pair_sums(y, kept, got):
    block = jax.ShapeDtypeStruct((LANES, WIDTH), BF16)
    return pl.pallas_call(
        pair_kernel,
        out_shape=(jax.ShapeDtypeStruct((LANES, WIDTH), F32),) + (block,) * (Y - 1),
        in_specs=[SMEM_SPEC, VMEM_SPEC, VMEM_SPEC],
        out_specs=(VMEM_SPEC,) * Y,
        compiler_params=pltpu.CompilerParams(vmem_limit_bytes=32 * 2**20),
        cost_estimate=pl.CostEstimate(flops=500_000, bytes_accessed=3_000_000, transcendentals=0),
        name="pair_sums",
    )(y, kept, got)


def payload_kernel(own, came_1, came_2, came_3, dy, shared, out):
    lane = lax.broadcasted_iota(jnp.int32, (64, LANES), 1)
    for m in range(8):
        cols = slice(m * LANES, (m + 1) * LANES)
        total = own[:, cols] + dy[m].astype(F32)
        for came in (came_1, came_2, came_3):
            total = total + came[:, cols].astype(F32)
        low, high = total[:64], total[64:]
        even = jnp.where(lane < 64, low, pltpu.roll(high, 64, 1))
        odd = jnp.where(lane < 64, pltpu.roll(low, 64, 1), high)
        out[2 * m, :64, :] = even.astype(BF16)
        out[2 * m + 1, :64, :] = odd.astype(BF16)
    for h in range(YC):
        total = jnp.zeros((PART_ROWS, HIDDEN), F32)
        for x in range(X):
            for r in range(ZR):
                total = total + shared[x, h, r, :, :HIDDEN].astype(F32)
        total = total.astype(BF16)
        for s in range(2):
            for n, col in enumerate((2 * s, 2 * s + 1, 4)):
                first = 64 + n * PART_ROWS
                out[2 * h + s, first : first + PART_ROWS, :] = total[
                    :, col * LANES : (col + 1) * LANES
                ]


def payload(own, came, dy, shared):
    return pl.pallas_call(
        payload_kernel,
        out_shape=jax.ShapeDtypeStruct((Z, 64 + 3 * PART_ROWS, LANES), BF16),
        in_specs=[VMEM_SPEC] * 6,
        out_specs=VMEM_SPEC,
        compiler_params=pltpu.CompilerParams(vmem_limit_bytes=32 * 2**20),
        cost_estimate=pl.CostEstimate(flops=1_500_000, bytes_accessed=4_000_000, transcendentals=0),
        name="payload",
    )(own, *came, dy, shared)


def place_kernel(slots, merged, out):
    slot_ids = lax.broadcasted_iota(jnp.int32, (SLOTS, LANES), 0)
    lane = lax.broadcasted_iota(jnp.int32, (SLOTS, LANES), 1)
    for pair in range(YC // 2):
        both = []
        for yc in (2 * pair, 2 * pair + 1):
            tokens = jnp.concatenate([merged[2 * yc, :64, :], merged[2 * yc + 1, :64, :]], axis=0)
            moved = [
                jnp.dot(
                    (slots[2 * yc + s : 2 * yc + s + 1, :] == slot_ids).astype(BF16),
                    tokens,
                    preferred_element_type=F32,
                )
                for s in range(2)
            ]
            rows = jnp.where(lane < 64, moved[0], moved[1])
            both.append(rows.reshape(OWNERS, CAP, LANES))
        out[:, pair * 16 : (pair + 1) * 16, :] = jnp.concatenate(both, axis=1).astype(BF16)


def place(slots, merged):
    return pl.pallas_call(
        place_kernel,
        out_shape=jax.ShapeDtypeStruct((OWNERS, YC * CAP, LANES), BF16),
        in_specs=[VMEM_SPEC] * 2,
        out_specs=VMEM_SPEC,
        compiler_params=pltpu.CompilerParams(vmem_limit_bytes=32 * 2**20),
        cost_estimate=pl.CostEstimate(
            flops=135_000_000, bytes_accessed=1_000_000, transcendentals=0
        ),
        name="place",
    )(slots, merged)


def table_kernel(tags, rows, out):
    row_ids = lax.broadcasted_iota(jnp.int32, (ROWS, rows.shape[0]), 0)
    sums = [
        jnp.dot(
            (tags[s : s + 1, :] == row_ids).astype(BF16), rows[...], preferred_element_type=F32
        )
        for s in range(2)
    ]
    out[...] = (sums[0] + pltpu.roll(sums[1], 64, 1)).T[:64]


def table_sum(tags, rows):
    return pl.pallas_call(
        table_kernel,
        out_shape=jax.ShapeDtypeStruct((64, ROWS), F32),
        in_specs=[VMEM_SPEC] * 2,
        out_specs=VMEM_SPEC,
        compiler_params=pltpu.CompilerParams(vmem_limit_bytes=32 * 2**20),
        cost_estimate=pl.CostEstimate(
            flops=270_000_000, bytes_accessed=1_000_000, transcendentals=0
        ),
        name="table_sum",
    )(tags, rows)


def per_device(inputs, cotangent, lengths, item_ids, owner_row, w_project, w_output):
    core = lax.axis_index("c")
    y_here = lax.axis_index("y")
    z_here = lax.axis_index(SEQ)
    lane = jnp.arange(LANES, dtype=jnp.int32)

    slot, local_row = routing(item_ids, owner_row)
    lens = lengths.reshape(-1)
    lens_row = jnp.concatenate([lens // 256, lens % 256])
    lens_row = jnp.pad(lens_row, (0, LANES - lens_row.shape[0]))
    small = jnp.pad(jnp.stack([slot, local_row, lens_row]), ((0, 5), (0, 0))).astype(BF16)
    high = PART_ROWS // 8
    n_w = 3 * high + 1
    wp_tiles = w_project.reshape(ZR, high, 8, 2, LANES).transpose(0, 1, 3, 2, 4)
    wo_t = w_output.T
    wo_tiles = jnp.concatenate([wo_t, wo_t], axis=1).reshape(ZR * high, 8, LANES)
    turned = jnp.concatenate([wp_tiles.reshape(2 * ZR * high, 8, LANES), wo_tiles, small[None]])
    turn = [
        ((x * YC + a) * Z + b * 2 + s, (x * YC + b) * Z + a * 2 + s)
        for x in range(X)
        for a in range(YC)
        for b in range(YC)
        for s in range(2)
    ]
    turned = lax.ppermute(turned, ALL, turn)
    wp_tiles = turned[: 2 * ZR * high].reshape(ZR, 2 * high, 8, LANES)
    wo_tiles = turned[2 * ZR * high : 3 * ZR * high].reshape(ZR, high, 8, LANES)
    small = jnp.broadcast_to(turned[None, -1:], (ZR, 1, 8, LANES))
    w_tiles = jnp.concatenate([wp_tiles, wo_tiles, small], axis=1)

    both = jnp.stack([inputs[0], cotangent[0]]).reshape(2, 2, 64, 8, LANES)
    spread = exchange(both.transpose(3, 1, 0, 2, 4), PAIR)
    spread = spread.reshape(Z, 16, 8, LANES)
    w_tiles = jnp.broadcast_to(w_tiles[None], (ZQ, ZR, n_w, 8, LANES)).reshape(Z, n_w, 8, LANES)
    arrived = exchange(jnp.concatenate([spread, w_tiles], axis=1), SEQ)
    mine = arrived[:, :16].reshape(Z, 2, 64, LANES).transpose(1, 0, 2, 3)
    packs = lax.all_gather(mine.reshape(1, 2, LENGTH, LANES), PAIR, axis=0, tiled=True)

    by_head = arrived[:, 16:].reshape(YC, 2, n_w, 8, LANES)
    wp_part = by_head[:, :, : 2 * high].reshape(YC, 2, high, 2, 8, LANES)
    wp_part = wp_part.transpose(0, 2, 4, 1, 3, 5).reshape(YC, PART_ROWS, 4 * HEAD_DIM)
    wo_part = by_head[:, :, 2 * high : 3 * high]
    wo_part = jnp.where(lane < 64, wo_part[:, 0], wo_part[:, 1])
    w_part = jnp.concatenate([wp_part, wo_part.reshape(YC, PART_ROWS, HEAD_DIM)], axis=2)
    w_all = jnp.broadcast_to(w_part[None], (X * ZR,) + w_part.shape)
    weights = exchange(w_all, SHARE).reshape(X, ZR, YC, PART_ROWS, HIDDEN)

    facts = by_head[:, :, n_w - 1].astype(F32)
    slots = facts[:, :, 0].astype(jnp.int32)
    tag_of = facts[:, :, 1]
    lens_all = facts[:, 0, 2, :12].reshape(YC, 2, 2, 3)
    lens_all = (lens_all[:, 0] * 256.0 + lens_all[:, 1]).astype(jnp.int32).reshape(Z, 3)
    pack_lens = lax.dynamic_index_in_dim(lens_all, z_here, 0, keepdims=False)
    ends = jnp.cumsum(pack_lens)

    info = jnp.concatenate([ends, core[None]]).astype(jnp.int32)
    slot_ids = jnp.arange(SLOTS, dtype=jnp.int32)
    placed = slots[:, :, None, :] == slot_ids[None, None, :, None]
    tags = jnp.sum(jnp.where(placed, tag_of[:, :, None, :], 0.0), axis=3)
    tags = tags.reshape(YC, 2, OWNERS, CAP).transpose(2, 1, 0, 3).reshape(OWNERS, 1, LANES)
    tags = jnp.broadcast_to(tags.astype(BF16), (OWNERS, PART_ROWS, LANES))

    kept, sent, d_z, gated = heads_backward(info, packs, weights)
    got = lax.ppermute(sent, "c", [(0, 1), (1, 0)])

    grads = weight_grads(packs, d_z, gated, tags)
    shared = exchange(grads.reshape(X * YC * ZR, PART_ROWS, HIDDEN + LANES), SPREAD)
    shared = shared.reshape(X, YC, ZR, PART_ROWS, HIDDEN + LANES)

    own, *to_y = pair_sums(y_here[None].astype(jnp.int32), kept, got)
    came = [
        lax.ppermute(to_y[step - 1], "y", [(i, (i + step) % Y) for i in range(Y)])
        for step in range(1, Y)
    ]
    block = (y_here * C + core) * LANES
    dy_own = lax.dynamic_slice(packs, (0, 1, block, 0), (YC, 1, LANES, LANES))[:, 0]

    merged = exchange(payload(own, came, dy_own, shared), SEQ)
    w_grad = merged[:, 64:].astype(F32).reshape(ZQ, ZR, 3, PART_ROWS, LANES)
    w_grad = jnp.sum(w_grad, axis=0)
    grad_proj = w_grad[:, :2].transpose(0, 2, 1, 3).reshape(32, 2 * LANES)
    both_out = w_grad[:, 2].reshape(32, 2, 64)
    grad_out = lax.dynamic_index_in_dim(both_out, z_here & 1, 1, keepdims=False).T

    owned = exchange(place(slots.reshape(2 * YC, LANES), merged), DP)
    got_tags = shared[:, :, 0, 0, HIDDEN:]
    got_tags = got_tags.astype(F32).astype(jnp.int32).reshape(OWNERS, 2, YC * CAP)
    got_tags = got_tags.transpose(1, 0, 2).reshape(2, OWNERS * YC * CAP)
    grad_table = table_sum(got_tags, owned.reshape(OWNERS * YC * CAP, LANES)).T
    return (grad_proj, grad_out, grad_table)


def solution(mesh):
    fine = Mesh(mesh.devices.reshape(X, Y, C, ZQ, ZR), ALL)
    return jax.shard_map(
        per_device,
        mesh=fine,
        in_specs=(
            P(DP, None, SEQ, None),
            P(DP, None, SEQ, None),
            P(DP, None, None),
            P(DP, None, SEQ),
            P(),
            P(DP, SEQ),
            P(SEQ, DP),
        ),
        out_specs=(P(DP, SEQ), P(SEQ, DP), P(DP, SEQ)),
        check_vma=False,
    )
```

```python
import jax
import jax.numpy as jnp
from jax import lax
from jax.experimental import pallas as pl
from jax.experimental.pallas import tpu as pltpu
from jax.sharding import Mesh, PartitionSpec as P

HEAD_DIM = 128
NORM_FLOOR = 1.0
F32 = jnp.float32
BF16 = jnp.bfloat16

X, Y, C, ZQ, ZR = 4, 4, 2, 8, 2
YC = Y * C
Z = ZQ * ZR
PAIR = ("y", "c")
DP = ("x", "y", "c")
SEQ = ("zq", "zr")
SHARE = ("x", "zr")
SPREAD = ("x", "y", "c", "zr")
ALL = ("x", "y", "c", "zq", "zr")
OWNERS = X * YC
CAP = 8
ROWS = 256
SLOTS = OWNERS * CAP
LANES = 128
LENGTH = 1024
WIDTH = 1024
HIDDEN = 5 * HEAD_DIM
PART_ROWS = 32 // ZR
STEP = 256
REACH = 512
VMEM_SPEC = pl.BlockSpec(memory_space=pltpu.VMEM)
SMEM_SPEC = pl.BlockSpec(memory_space=pltpu.SMEM)


def exchange(value, axes):
    return lax.all_to_all(value, axes, split_axis=0, concat_axis=0, tiled=True)


def routing(item_ids, owner_row):
    rows = jnp.take(owner_row, item_ids.reshape(-1))
    owner = rows // ROWS
    count = owner.shape[0]
    order = jnp.arange(count, dtype=jnp.int32)
    before = (owner[None, :] == owner[:, None]) & (order[None, :] < order[:, None])
    rank = jnp.sum(before.astype(jnp.int32), axis=1)
    return owner * CAP + rank, rows % ROWS


def dot_nt(a, b):
    return lax.dot_general(a, b, (((1,), (1,)), ((), ())), preferred_element_type=F32)


def dot_tn(a, b):
    return lax.dot_general(a, b, (((0,), (0,)), ((), ())), preferred_element_type=F32)


def heads_kernel(info, packs, w_in, kept, sent, d_z, gated, w, acts, slope, d_value, d_key):
    hd = HEAD_DIM
    scale = hd**-0.5
    u_cols, v_cols, q_cols, k_cols = (slice(m * hd, (m + 1) * hd) for m in range(4))
    for x in range(X):
        for yc in range(YC):
            start = (x * YC + yc) * 32
            w[start : start + 32, :] = w_in[x, :, yc].reshape(32, HIDDEN)
    d_value[...] = jnp.zeros_like(d_value)
    d_key[...] = jnp.zeros_like(d_key)

    def project(step, carry):
        rows = pl.ds(pl.multiple_of(step * STEP, STEP), STEP)
        px = jnp.concatenate([packs[g, 0, rows, :] for g in range(8)], axis=1)
        z_pre = jnp.dot(px, w[:, : 4 * hd], preferred_element_type=F32)
        sigma = jax.nn.sigmoid(z_pre)
        silu = z_pre * sigma
        acts[rows, :] = silu.astype(BF16)
        slope[rows, :] = sigma + silu * (1.0 - sigma)
        return carry

    lax.fori_loop(0, LENGTH // STEP, project, 0)

    for step in range(LENGTH // STEP):
        base = step * STEP
        first = max(0, base - REACH)
        rows = slice(base, base + STEP)
        span = slice(first, base + STEP)
        pos_k = lax.broadcasted_iota(jnp.int32, (1, base + STEP - first), 1) + first
        pos_q = lax.broadcasted_iota(jnp.int32, (STEP, 1), 0) + base
        start = jnp.zeros_like(pos_q)
        for n in range(3):
            start = jnp.where(pos_q >= info[n], info[n], start)
        masked = (pos_k <= pos_q) & (pos_k >= start)
        query = acts[rows, q_cols]
        key = acts[span, k_cols]
        value = acts[span, v_cols]
        scores = dot_nt(query, key) * scale
        sigma = jax.nn.sigmoid(scores)
        silu = scores * sigma
        attn = jnp.where(masked, silu, 0.0).astype(BF16)
        factor = jnp.where(masked, (sigma + silu * (1.0 - sigma)) * scale, 0.0)
        mixed = jnp.dot(attn, value, preferred_element_type=F32)
        centred = mixed - jnp.mean(mixed, axis=-1, keepdims=True)
        inv_std = lax.rsqrt(jnp.mean(centred * centred, axis=-1, keepdims=True) + NORM_FLOOR)
        normed = centred * inv_std
        gating = acts[rows, u_cols].astype(F32)
        gated[rows, :] = (normed * gating).astype(BF16)
        pdy = jnp.concatenate([packs[g, 1, rows, :] for g in range(8)], axis=1)
        d_gated = jnp.dot(pdy, w[:, 4 * hd :], preferred_element_type=F32)
        d_normed = d_gated * gating
        d_mixed = (
            inv_std
            * (
                d_normed
                - jnp.mean(d_normed, axis=-1, keepdims=True)
                - normed * jnp.mean(d_normed * normed, axis=-1, keepdims=True)
            )
        ).astype(BF16)
        d_scores = (dot_nt(d_mixed, value) * factor).astype(BF16)
        d_query = jnp.dot(d_scores, key, preferred_element_type=F32)
        d_value[span, :] += dot_tn(attn, d_mixed)
        d_key[span, :] += dot_tn(d_scores, query)
        d_z[rows, u_cols] = (d_gated * normed * slope[rows, u_cols]).astype(BF16)
        d_z[rows, q_cols] = (d_query * slope[rows, q_cols]).astype(BF16)

    d_z[:, v_cols] = (d_value[...] * slope[:, v_cols]).astype(BF16)
    d_z[:, k_cols] = (d_key[...] * slope[:, k_cols]).astype(BF16)

    core = info[3]

    def parts(step, carry):
        rows = pl.ds(pl.multiple_of(step * STEP, STEP), STEP)
        part = dot_nt(d_z[rows, :], w[:, : 4 * hd]).astype(BF16)

        @pl.when(core == 0)
        def _():
            kept[step] = part[:LANES]
            sent[step] = part[LANES:]

        @pl.when(core != 0)
        def _():
            kept[step] = part[LANES:]
            sent[step] = part[:LANES]

        return carry

    lax.fori_loop(0, Y, parts, 0)


def heads_backward(info, packs, weights):
    half = jax.ShapeDtypeStruct((Y, LANES, WIDTH), BF16)
    return pl.pallas_call(
        heads_kernel,
        out_shape=(
            half,
            half,
            jax.ShapeDtypeStruct((LENGTH, 4 * HEAD_DIM), BF16),
            jax.ShapeDtypeStruct((LENGTH, HEAD_DIM), BF16),
        ),
        in_specs=[SMEM_SPEC, VMEM_SPEC, VMEM_SPEC],
        out_specs=(VMEM_SPEC,) * 4,
        scratch_shapes=[
            pltpu.VMEM((WIDTH, HIDDEN), BF16),
            pltpu.VMEM((LENGTH, 4 * HEAD_DIM), BF16),
            pltpu.VMEM((LENGTH, 4 * HEAD_DIM), F32),
            pltpu.VMEM((LENGTH, HEAD_DIM), F32),
            pltpu.VMEM((LENGTH, HEAD_DIM), F32),
        ],
        compiler_params=pltpu.CompilerParams(vmem_limit_bytes=44 * 2**20),
        cost_estimate=pl.CostEstimate(
            flops=4_000_000_000, bytes_accessed=9_000_000, transcendentals=2_000_000
        ),
        name="heads",
    )(info, packs, weights)


def grads_kernel(packs, d_z, gated, out):
    for x in range(X):
        for dest, source, t in ((slice(0, 512), d_z, 0), (slice(512, 640), gated, 1)):
            columns = jnp.concatenate([packs[2 * x, t], packs[2 * x + 1, t]], axis=1)
            block = dot_tn(columns, source[...]).astype(BF16)
            for yc in range(YC):
                for r in range(ZR):
                    at = yc * 32 + r * PART_ROWS
                    out[x, yc, r, :, dest] = block[at : at + PART_ROWS]


def weight_grads(packs, d_z, gated):
    return pl.pallas_call(
        grads_kernel,
        out_shape=jax.ShapeDtypeStruct((X, YC, ZR, PART_ROWS, HIDDEN), BF16),
        in_specs=[VMEM_SPEC] * 3,
        out_specs=VMEM_SPEC,
        compiler_params=pltpu.CompilerParams(vmem_limit_bytes=32 * 2**20),
        cost_estimate=pl.CostEstimate(
            flops=1_350_000_000, bytes_accessed=6_800_000, transcendentals=0
        ),
        name="weight_grads",
    )(packs, d_z, gated)


def pair_kernel(place, kept, got, own, *to_y):
    y = place[0]
    own[...] = kept[y].astype(F32) + got[y].astype(F32)
    for step in range(1, Y):
        other = (y + step) & (Y - 1)
        to_y[step - 1][...] = (kept[other].astype(F32) + got[other].astype(F32)).astype(BF16)


def pair_sums(y, kept, got):
    block = jax.ShapeDtypeStruct((LANES, WIDTH), BF16)
    return pl.pallas_call(
        pair_kernel,
        out_shape=(jax.ShapeDtypeStruct((LANES, WIDTH), F32),) + (block,) * (Y - 1),
        in_specs=[SMEM_SPEC, VMEM_SPEC, VMEM_SPEC],
        out_specs=(VMEM_SPEC,) * Y,
        compiler_params=pltpu.CompilerParams(vmem_limit_bytes=32 * 2**20),
        cost_estimate=pl.CostEstimate(flops=500_000, bytes_accessed=3_000_000, transcendentals=0),
        name="pair_sums",
    )(y, kept, got)


def payload_kernel(own, came_1, came_2, came_3, dy, shared, out):
    lane = lax.broadcasted_iota(jnp.int32, (64, LANES), 1)
    for m in range(8):
        cols = slice(m * LANES, (m + 1) * LANES)
        total = own[:, cols] + dy[m].astype(F32)
        for came in (came_1, came_2, came_3):
            total = total + came[:, cols].astype(F32)
        low, high = total[:64], total[64:]
        even = jnp.where(lane < 64, low, pltpu.roll(high, 64, 1))
        odd = jnp.where(lane < 64, pltpu.roll(low, 64, 1), high)
        out[2 * m, :64, :] = even.astype(BF16)
        out[2 * m + 1, :64, :] = odd.astype(BF16)
    for h in range(YC):
        total = jnp.zeros((PART_ROWS, HIDDEN), F32)
        for x in range(X):
            for r in range(ZR):
                total = total + shared[x, h, r].astype(F32)
        total = total.astype(BF16)
        for s in range(2):
            for n, col in enumerate((2 * s, 2 * s + 1, 4)):
                first = 64 + n * PART_ROWS
                out[2 * h + s, first : first + PART_ROWS, :] = total[
                    :, col * LANES : (col + 1) * LANES
                ]


def payload(own, came, dy, shared):
    return pl.pallas_call(
        payload_kernel,
        out_shape=jax.ShapeDtypeStruct((Z, 64 + 3 * PART_ROWS, LANES), BF16),
        in_specs=[VMEM_SPEC] * 6,
        out_specs=VMEM_SPEC,
        compiler_params=pltpu.CompilerParams(vmem_limit_bytes=32 * 2**20),
        cost_estimate=pl.CostEstimate(flops=1_500_000, bytes_accessed=4_000_000, transcendentals=0),
        name="payload",
    )(own, *came, dy, shared)


def place_kernel(slots, tags, merged, out):
    slot_ids = lax.broadcasted_iota(jnp.int32, (SLOTS, LANES), 0)
    lane = lax.broadcasted_iota(jnp.int32, (SLOTS, LANES), 1)
    for pair in range(YC // 2):
        both = []
        for yc in (2 * pair, 2 * pair + 1):
            tokens = jnp.concatenate([merged[2 * yc, :64, :], merged[2 * yc + 1, :64, :]], axis=0)
            moved = [
                jnp.dot(
                    (slots[2 * yc + s : 2 * yc + s + 1, :] == slot_ids).astype(BF16),
                    tokens,
                    preferred_element_type=F32,
                )
                for s in range(2)
            ]
            rows = jnp.where(lane < 64, moved[0], moved[1])
            both.append(rows.reshape(OWNERS, CAP, LANES))
        out[:, pair * 16 : (pair + 1) * 16, :] = jnp.concatenate(both, axis=1).astype(BF16)
    out[:, YC * CAP :, :] = tags[...]


def place(slots, tags, merged):
    return pl.pallas_call(
        place_kernel,
        out_shape=jax.ShapeDtypeStruct((OWNERS, YC * CAP + 16, LANES), BF16),
        in_specs=[VMEM_SPEC] * 3,
        out_specs=VMEM_SPEC,
        compiler_params=pltpu.CompilerParams(vmem_limit_bytes=32 * 2**20),
        cost_estimate=pl.CostEstimate(
            flops=135_000_000, bytes_accessed=1_000_000, transcendentals=0
        ),
        name="place",
    )(slots, tags, merged)


def table_kernel(owned, out):
    count = YC * CAP
    row_ids = lax.broadcasted_iota(jnp.int32, (ROWS, LANES), 0).astype(F32)
    left = lax.broadcasted_iota(jnp.int32, (count, LANES), 1) < 64
    total = jnp.zeros((ROWS, LANES), F32)
    for pair in range(OWNERS // 2):
        select, rows = [], []
        for source in (2 * pair, 2 * pair + 1):
            tag = owned[source, count:, :].astype(F32)[:1]
            select.append((tag == row_ids).astype(BF16))
            here = owned[source, :count, :].astype(F32)
            rows.append(jnp.where(left, here, 0.0).astype(BF16))
            rows.append(jnp.where(left, 0.0, here).astype(BF16))
        total = total + jnp.dot(
            jnp.concatenate(select, axis=1),
            jnp.concatenate(rows, axis=0),
            preferred_element_type=F32,
        )
    out[...] = (total + pltpu.roll(total, 64, 1)).T[:64]


def table_sum(owned):
    return pl.pallas_call(
        table_kernel,
        out_shape=jax.ShapeDtypeStruct((64, ROWS), F32),
        in_specs=[VMEM_SPEC],
        out_specs=VMEM_SPEC,
        compiler_params=pltpu.CompilerParams(vmem_limit_bytes=32 * 2**20),
        cost_estimate=pl.CostEstimate(
            flops=270_000_000, bytes_accessed=1_000_000, transcendentals=0
        ),
        name="table_sum",
    )(owned)


def split_kernel(inputs, cotangent, out):
    for g in range(8):
        for p in range(2):
            for t, source in enumerate((inputs, cotangent)):
                out[g, p, t] = source[p, :, g * LANES : (g + 1) * LANES]


def split_columns(inputs, cotangent):
    return pl.pallas_call(
        split_kernel,
        out_shape=jax.ShapeDtypeStruct((8, 2, 2, 64, LANES), BF16),
        in_specs=[VMEM_SPEC] * 2,
        out_specs=VMEM_SPEC,
        compiler_params=pltpu.CompilerParams(vmem_limit_bytes=32 * 2**20),
        cost_estimate=pl.CostEstimate(flops=0, bytes_accessed=1_000_000, transcendentals=0),
        name="split_columns",
    )(inputs, cotangent)


def per_device(inputs, cotangent, lengths, item_ids, owner_row, w_project, w_output):
    core = lax.axis_index("c")
    y_here = lax.axis_index("y")
    z_here = lax.axis_index(SEQ)
    lane = jnp.arange(LANES, dtype=jnp.int32)

    slot, local_row = routing(item_ids, owner_row)
    lens = lengths.reshape(-1)
    lens_row = jnp.concatenate([lens // 256, lens % 256])
    lens_row = jnp.pad(lens_row, (0, LANES - lens_row.shape[0]))
    small = jnp.pad(jnp.stack([slot, local_row, lens_row]), ((0, 5), (0, 0))).astype(BF16)
    high = PART_ROWS // 8
    wp_high = 2 * high
    n_w = wp_high + 2
    wp_tiles = w_project.reshape(ZR, high, 8, 2, LANES).transpose(0, 1, 3, 2, 4)
    wp_tiles = wp_tiles.reshape(ZR, wp_high, 8, LANES)
    wo_tiles = w_output.T.reshape(ZR, high, 8, 64).transpose(0, 2, 1, 3).reshape(ZR, 1, 8, LANES)
    small = jnp.broadcast_to(small[None, None], (ZR, 1, 8, LANES))
    w_tiles = jnp.concatenate([wp_tiles, wo_tiles, small], axis=1)

    spread = exchange(split_columns(inputs[0], cotangent[0]), PAIR)
    spread = spread.reshape(Z, 16, 8, LANES)
    w_tiles = jnp.broadcast_to(w_tiles[None], (ZQ, ZR, n_w, 8, LANES)).reshape(Z, n_w, 8, LANES)
    arrived = exchange(jnp.concatenate([spread, w_tiles], axis=1), SEQ)
    mine = arrived[:, :16].reshape(Z, 2, 64, LANES).transpose(1, 0, 2, 3)
    packs = lax.all_gather(mine.reshape(1, 2, LENGTH, LANES), PAIR, axis=0, tiled=True)

    by_head = exchange(arrived[:, 16:].reshape(YC, 2, n_w, 8, LANES), PAIR)
    wp_part = by_head[:, :, :wp_high].reshape(YC, 2, high, 2, 8, LANES)
    wp_part = wp_part.transpose(0, 2, 4, 1, 3, 5).reshape(YC, PART_ROWS, 4 * HEAD_DIM)
    wo_part = by_head[:, :, wp_high].reshape(YC, 2, 8, high, 64).transpose(0, 3, 2, 1, 4)
    w_part = jnp.concatenate([wp_part, wo_part.reshape(YC, PART_ROWS, HEAD_DIM)], axis=2)
    w_all = jnp.broadcast_to(w_part[None], (X * ZR,) + w_part.shape)
    weights = exchange(w_all, SHARE).reshape(X, ZR, YC, PART_ROWS, HIDDEN)

    facts = by_head[:, :, n_w - 1].astype(F32)
    slots = facts[:, :, 0].astype(jnp.int32)
    tag_of = facts[:, :, 1]
    lens_all = facts[:, 0, 2, :12].reshape(YC, 2, 2, 3)
    lens_all = (lens_all[:, 0] * 256.0 + lens_all[:, 1]).astype(jnp.int32).reshape(Z, 3)
    pack_lens = lax.dynamic_index_in_dim(lens_all, z_here, 0, keepdims=False)
    ends = jnp.cumsum(pack_lens)

    info = jnp.concatenate([ends, core[None]]).astype(jnp.int32)
    slot_ids = jnp.arange(SLOTS, dtype=jnp.int32)
    placed = slots[:, :, None, :] == slot_ids[None, None, :, None]
    tags = jnp.sum(jnp.where(placed, tag_of[:, :, None, :], 0.0), axis=3)
    tags = tags.reshape(YC, 2, OWNERS, CAP).transpose(2, 1, 0, 3).reshape(OWNERS, 1, LANES)
    tags = jnp.broadcast_to(tags.astype(BF16), (OWNERS, 16, LANES))

    kept, sent, d_z, gated = heads_backward(info, packs, weights)
    got = lax.ppermute(sent, "c", [(0, 1), (1, 0)])

    grads = weight_grads(packs, d_z, gated)
    own, *to_y = pair_sums(y_here[None].astype(jnp.int32), kept, got)
    grads, own = lax.optimization_barrier((grads, own))

    shared = exchange(grads.reshape(X * YC * ZR, PART_ROWS, HIDDEN), SPREAD)
    shared = shared.reshape(X, YC, ZR, PART_ROWS, HIDDEN)
    came = [
        lax.ppermute(to_y[step - 1], "y", [(i, (i + step) % Y) for i in range(Y)])
        for step in range(1, Y)
    ]
    block = (y_here * C + core) * LANES
    dy_own = lax.dynamic_slice(packs, (0, 1, block, 0), (YC, 1, LANES, LANES))[:, 0]

    merged = exchange(payload(own, came, dy_own, shared), SEQ)
    w_grad = merged[:, 64:].astype(F32).reshape(ZQ, ZR, 3, PART_ROWS, LANES)
    w_grad = jnp.sum(w_grad, axis=0)
    grad_proj = w_grad[:, :2].transpose(0, 2, 1, 3).reshape(32, 2 * LANES)
    both_out = w_grad[:, 2].reshape(32, 2, 64)
    grad_out = lax.dynamic_index_in_dim(both_out, z_here & 1, 1, keepdims=False).T

    owned = exchange(place(slots.reshape(2 * YC, LANES), tags, merged), DP)
    return (grad_proj, grad_out, table_sum(owned).T)


def solution(mesh):
    fine = Mesh(mesh.devices.reshape(X, Y, C, ZQ, ZR), ALL)
    return jax.shard_map(
        per_device,
        mesh=fine,
        in_specs=(
            P(DP, None, SEQ, None),
            P(DP, None, SEQ, None),
            P(DP, None, None),
            P(DP, None, SEQ),
            P(),
            P(DP, SEQ),
            P(SEQ, DP),
        ),
        out_specs=(P(DP, SEQ), P(SEQ, DP), P(DP, SEQ)),
        check_vma=False,
    )
```

```python
import jax
import jax.numpy as jnp
from jax import lax
from jax.experimental import pallas as pl
from jax.experimental.pallas import tpu as pltpu
from jax.sharding import Mesh, PartitionSpec as P

HEAD_DIM = 128
NORM_FLOOR = 1.0
F32 = jnp.float32
BF16 = jnp.bfloat16

X, Y, C, ZQ, ZR = 4, 4, 2, 8, 2
YC = Y * C
Z = ZQ * ZR
PAIR = ("y", "c")
DP = ("x", "y", "c")
SEQ = ("zq", "zr")
SHARE = ("x", "zr")
SPREAD = ("x", "y", "c", "zr")
ALL = ("x", "y", "c", "zq", "zr")
OWNERS = X * YC
CAP = 8
ROWS = 256
SLOTS = OWNERS * CAP
LANES = 128
LENGTH = 1024
WIDTH = 1024
HIDDEN = 5 * HEAD_DIM
PART_ROWS = 32 // ZR
STEP = 256
REACH = 512
VMEM_SPEC = pl.BlockSpec(memory_space=pltpu.VMEM)
GRANT = 58
HBM_SPEC = pl.BlockSpec(memory_space=pltpu.HBM)
SMEM_SPEC = pl.BlockSpec(memory_space=pltpu.SMEM)


def exchange(value, axes):
    return lax.all_to_all(value, axes, split_axis=0, concat_axis=0, tiled=True)


def routing(item_ids, owner_row):
    rows = jnp.take(owner_row, item_ids.reshape(-1))
    owner = rows // ROWS
    count = owner.shape[0]
    order = jnp.arange(count, dtype=jnp.int32)
    before = (owner[None, :] == owner[:, None]) & (order[None, :] < order[:, None])
    rank = jnp.sum(before.astype(jnp.int32), axis=1)
    return owner * CAP + rank, rows % ROWS


def dot_nt(a, b):
    return lax.dot_general(a, b, (((1,), (1,)), ((), ())), preferred_element_type=F32)


def dot_tn(a, b):
    return lax.dot_general(a, b, (((0,), (0,)), ((), ())), preferred_element_type=F32)


def heads_kernel(
    info,
    packs,
    weights,
    kept,
    sent,
    grads,
    x_v,
    dy_v,
    w_v,
    acts,
    slope,
    d_value,
    d_key,
    d_z,
    gated,
    kept_v,
    sent_v,
    grads_v,
    sems,
    w_sems,
    out_sems,
):
    hd = HEAD_DIM
    scale = hd**-0.5
    u_cols, v_cols, q_cols, k_cols = (slice(m * hd, (m + 1) * hd) for m in range(4))
    steps = LENGTH // STEP
    copies = [
        pltpu.make_async_copy(
            packs.at[:, t, pl.ds(n * STEP, STEP)],
            held.at[:, pl.ds(n * STEP, STEP)],
            sems.at[t * steps + n],
        )
        for t, held in enumerate((x_v, dy_v))
        for n in range(steps)
    ]
    w_copies = [
        pltpu.make_async_copy(weights.at[x, r], w_v.at[x, :, r], w_sems.at[x * ZR + r])
        for x in range(X)
        for r in range(ZR)
    ]
    for copy in copies[:1] + w_copies + copies[1:]:
        copy.start()
    d_value[...] = jnp.zeros_like(d_value)
    d_key[...] = jnp.zeros_like(d_key)

    for copy in w_copies:
        copy.wait()
    wp = w_v[..., : 4 * hd].reshape(WIDTH, 4 * hd)
    wo = w_v[..., 4 * hd :].reshape(WIDTH, hd)

    for step in range(steps):
        copies[step].wait()
        rows = slice(step * STEP, (step + 1) * STEP)
        px = jnp.concatenate([x_v[g, rows, :] for g in range(8)], axis=1)
        z_pre = jnp.dot(px, wp, preferred_element_type=F32)
        sigma = jax.nn.sigmoid(z_pre)
        silu = z_pre * sigma
        acts[rows, :] = silu.astype(BF16)
        slope[rows, :] = sigma + silu * (1.0 - sigma)

    for step in range(steps):
        copies[steps + step].wait()
        base = step * STEP
        first = max(0, base - REACH)
        rows = slice(base, base + STEP)
        span = slice(first, base + STEP)
        pos_k = lax.broadcasted_iota(jnp.int32, (1, base + STEP - first), 1) + first
        pos_q = lax.broadcasted_iota(jnp.int32, (STEP, 1), 0) + base
        start = jnp.zeros_like(pos_q)
        for n in range(3):
            start = jnp.where(pos_q >= info[n], info[n], start)
        masked = (pos_k <= pos_q) & (pos_k >= start)
        query = acts[rows, q_cols]
        key = acts[span, k_cols]
        value = acts[span, v_cols]
        scores = dot_nt(query, key) * scale
        sigma = jax.nn.sigmoid(scores)
        silu = scores * sigma
        attn = jnp.where(masked, silu, 0.0).astype(BF16)
        factor = jnp.where(masked, (sigma + silu * (1.0 - sigma)) * scale, 0.0)
        mixed = jnp.dot(attn, value, preferred_element_type=F32)
        centred = mixed - jnp.mean(mixed, axis=-1, keepdims=True)
        inv_std = lax.rsqrt(jnp.mean(centred * centred, axis=-1, keepdims=True) + NORM_FLOOR)
        normed = centred * inv_std
        gating = acts[rows, u_cols].astype(F32)
        gated[rows, :] = (normed * gating).astype(BF16)
        pdy = jnp.concatenate([dy_v[g, rows, :] for g in range(8)], axis=1)
        d_gated = jnp.dot(pdy, wo, preferred_element_type=F32)
        d_normed = d_gated * gating
        d_mixed = (
            inv_std
            * (
                d_normed
                - jnp.mean(d_normed, axis=-1, keepdims=True)
                - normed * jnp.mean(d_normed * normed, axis=-1, keepdims=True)
            )
        ).astype(BF16)
        d_scores = (dot_nt(d_mixed, value) * factor).astype(BF16)
        d_query = jnp.dot(d_scores, key, preferred_element_type=F32)
        d_value[span, :] += dot_tn(attn, d_mixed)
        d_key[span, :] += dot_tn(d_scores, query)
        d_z[rows, u_cols] = (d_gated * normed * slope[rows, u_cols]).astype(BF16)
        d_z[rows, q_cols] = (d_query * slope[rows, q_cols]).astype(BF16)

    d_z[:, v_cols] = (d_value[...] * slope[:, v_cols]).astype(BF16)
    d_z[:, k_cols] = (d_key[...] * slope[:, k_cols]).astype(BF16)

    core = info[3]
    outs = []
    for y in range(Y):
        part = dot_nt(d_z[y * STEP : (y + 1) * STEP, :], wp).astype(BF16)

        @pl.when(core == 0)
        def _():
            kept_v[y] = part[:LANES]
            sent_v[y] = part[LANES:]

        @pl.when(core != 0)
        def _():
            kept_v[y] = part[LANES:]
            sent_v[y] = part[:LANES]

        for held, out in ((sent_v, sent), (kept_v, kept)):
            outs.append(pltpu.make_async_copy(held.at[y], out.at[y], out_sems.at[len(outs)]))
            outs[-1].start()

    for x in range(X):
        for dest, source, pack in ((slice(0, 512), d_z, x_v), (slice(512, 640), gated, dy_v)):
            columns = jnp.concatenate([pack[2 * x], pack[2 * x + 1]], axis=1)
            block = dot_tn(columns, source[...]).astype(BF16)
            grads_v[x, :, :, :, dest] = block.reshape(YC, ZR, PART_ROWS, block.shape[1])
        outs.append(pltpu.make_async_copy(grads_v.at[x], grads.at[x], out_sems.at[len(outs)]))
        outs[-1].start()
    for copy in outs:
        copy.wait()


def heads_backward(info, packs, weights):
    half = jax.ShapeDtypeStruct((Y, LANES, WIDTH), BF16)
    return pl.pallas_call(
        heads_kernel,
        out_shape=(
            half,
            half,
            jax.ShapeDtypeStruct((X, YC, ZR, PART_ROWS, HIDDEN), BF16),
        ),
        in_specs=[SMEM_SPEC, HBM_SPEC, HBM_SPEC],
        out_specs=(HBM_SPEC,) * 3,
        scratch_shapes=[
            pltpu.VMEM((8, LENGTH, LANES), BF16),
            pltpu.VMEM((8, LENGTH, LANES), BF16),
            pltpu.VMEM((X, YC, ZR, PART_ROWS, HIDDEN), BF16),
            pltpu.VMEM((LENGTH, 4 * HEAD_DIM), BF16),
            pltpu.VMEM((LENGTH, 4 * HEAD_DIM), F32),
            pltpu.VMEM((LENGTH, HEAD_DIM), F32),
            pltpu.VMEM((LENGTH, HEAD_DIM), F32),
            pltpu.VMEM((LENGTH, 4 * HEAD_DIM), BF16),
            pltpu.VMEM((LENGTH, HEAD_DIM), BF16),
            pltpu.VMEM((Y, LANES, WIDTH), BF16),
            pltpu.VMEM((Y, LANES, WIDTH), BF16),
            pltpu.VMEM((X, YC, ZR, PART_ROWS, HIDDEN), BF16),
            pltpu.SemaphoreType.DMA((2 * LENGTH // STEP,)),
            pltpu.SemaphoreType.DMA((X * ZR,)),
            pltpu.SemaphoreType.DMA((2 * Y + X,)),
        ],
        compiler_params=pltpu.CompilerParams(vmem_limit_bytes=GRANT * 2**20),
        cost_estimate=pl.CostEstimate(
            flops=5_000_000_000, bytes_accessed=9_000_000, transcendentals=2_000_000
        ),
        name="heads",
    )(info, packs, weights)


def pair_kernel(place, kept, got, own, *to_y):
    y = place[0]
    own[...] = kept[y].astype(F32) + got[y].astype(F32)
    for step in range(1, Y):
        other = (y + step) & (Y - 1)
        to_y[step - 1][...] = (kept[other].astype(F32) + got[other].astype(F32)).astype(BF16)


def pair_sums(y, kept, got):
    block = jax.ShapeDtypeStruct((LANES, WIDTH), BF16)
    return pl.pallas_call(
        pair_kernel,
        out_shape=(jax.ShapeDtypeStruct((LANES, WIDTH), F32),) + (block,) * (Y - 1),
        in_specs=[SMEM_SPEC, VMEM_SPEC, VMEM_SPEC],
        out_specs=(VMEM_SPEC,) * Y,
        compiler_params=pltpu.CompilerParams(vmem_limit_bytes=32 * 2**20),
        cost_estimate=pl.CostEstimate(flops=500_000, bytes_accessed=3_000_000, transcendentals=0),
        name="pair_sums",
    )(y, kept, got)


def payload_kernel(own, came_1, came_2, came_3, dy, shared, out):
    lane = lax.broadcasted_iota(jnp.int32, (64, LANES), 1)
    for m in range(8):
        cols = slice(m * LANES, (m + 1) * LANES)
        total = own[:, cols] + dy[m].astype(F32)
        for came in (came_1, came_2, came_3):
            total = total + came[:, cols].astype(F32)
        low, high = total[:64], total[64:]
        even = jnp.where(lane < 64, low, pltpu.roll(high, 64, 1))
        odd = jnp.where(lane < 64, pltpu.roll(low, 64, 1), high)
        out[2 * m, :64, :] = even.astype(BF16)
        out[2 * m + 1, :64, :] = odd.astype(BF16)
    for h in range(YC):
        total = jnp.zeros((PART_ROWS, HIDDEN), F32)
        for x in range(X):
            for r in range(ZR):
                total = total + shared[x, h, r].astype(F32)
        total = total.astype(BF16)
        for s in range(2):
            for n, col in enumerate((2 * s, 2 * s + 1, 4)):
                first = 64 + n * PART_ROWS
                out[2 * h + s, first : first + PART_ROWS, :] = total[
                    :, col * LANES : (col + 1) * LANES
                ]


def payload(own, came, dy, shared):
    return pl.pallas_call(
        payload_kernel,
        out_shape=jax.ShapeDtypeStruct((Z, 64 + 3 * PART_ROWS, LANES), BF16),
        in_specs=[VMEM_SPEC] * 6,
        out_specs=VMEM_SPEC,
        compiler_params=pltpu.CompilerParams(vmem_limit_bytes=32 * 2**20),
        cost_estimate=pl.CostEstimate(flops=1_500_000, bytes_accessed=4_000_000, transcendentals=0),
        name="payload",
    )(own, *came, dy, shared)


def place_kernel(slots, tags, merged, out):
    slot_ids = lax.broadcasted_iota(jnp.int32, (SLOTS, LANES), 0)
    lane = lax.broadcasted_iota(jnp.int32, (SLOTS, LANES), 1)
    for pair in range(YC // 2):
        both = []
        for yc in (2 * pair, 2 * pair + 1):
            tokens = jnp.concatenate([merged[2 * yc, :64, :], merged[2 * yc + 1, :64, :]], axis=0)
            moved = [
                jnp.dot(
                    (slots[2 * yc + s : 2 * yc + s + 1, :] == slot_ids).astype(BF16),
                    tokens,
                    preferred_element_type=F32,
                )
                for s in range(2)
            ]
            rows = jnp.where(lane < 64, moved[0], moved[1])
            both.append(rows.reshape(OWNERS, CAP, LANES))
        out[:, pair * 16 : (pair + 1) * 16, :] = jnp.concatenate(both, axis=1).astype(BF16)
    out[:, YC * CAP :, :] = tags[...]


def place(slots, tags, merged):
    return pl.pallas_call(
        place_kernel,
        out_shape=jax.ShapeDtypeStruct((OWNERS, YC * CAP + 16, LANES), BF16),
        in_specs=[VMEM_SPEC] * 3,
        out_specs=VMEM_SPEC,
        compiler_params=pltpu.CompilerParams(vmem_limit_bytes=32 * 2**20),
        cost_estimate=pl.CostEstimate(
            flops=135_000_000, bytes_accessed=1_000_000, transcendentals=0
        ),
        name="place",
    )(slots, tags, merged)


def table_kernel(owned, out):
    count = YC * CAP
    row_ids = lax.broadcasted_iota(jnp.int32, (ROWS, LANES), 0).astype(F32)
    left = lax.broadcasted_iota(jnp.int32, (count, LANES), 1) < 64
    total = jnp.zeros((ROWS, LANES), F32)
    for pair in range(OWNERS // 2):
        select, rows = [], []
        for source in (2 * pair, 2 * pair + 1):
            tag = owned[source, count:, :].astype(F32)[:1]
            select.append((tag == row_ids).astype(BF16))
            here = owned[source, :count, :].astype(F32)
            rows.append(jnp.where(left, here, 0.0).astype(BF16))
            rows.append(jnp.where(left, 0.0, here).astype(BF16))
        total = total + jnp.dot(
            jnp.concatenate(select, axis=1),
            jnp.concatenate(rows, axis=0),
            preferred_element_type=F32,
        )
    out[...] = (total + pltpu.roll(total, 64, 1)).T[:64]


def table_sum(owned):
    return pl.pallas_call(
        table_kernel,
        out_shape=jax.ShapeDtypeStruct((64, ROWS), F32),
        in_specs=[VMEM_SPEC],
        out_specs=VMEM_SPEC,
        compiler_params=pltpu.CompilerParams(vmem_limit_bytes=32 * 2**20),
        cost_estimate=pl.CostEstimate(
            flops=270_000_000, bytes_accessed=1_000_000, transcendentals=0
        ),
        name="table_sum",
    )(owned)


def split_kernel(inputs, cotangent, out, sems):
    copies = [
        pltpu.make_async_copy(
            source.at[:, :, pl.ds(g * LANES, LANES)], out.at[g, :, t], sems.at[2 * g + t]
        )
        for g in range(8)
        for t, source in enumerate((inputs, cotangent))
    ]
    for copy in copies:
        copy.start()
    for copy in copies:
        copy.wait()


def split_columns(inputs, cotangent):
    return pl.pallas_call(
        split_kernel,
        out_shape=jax.ShapeDtypeStruct((8, 2, 2, 64, LANES), BF16),
        in_specs=[HBM_SPEC] * 2,
        out_specs=HBM_SPEC,
        scratch_shapes=[pltpu.SemaphoreType.DMA((16,))],
        compiler_params=pltpu.CompilerParams(vmem_limit_bytes=32 * 2**20),
        cost_estimate=pl.CostEstimate(flops=0, bytes_accessed=1_000_000, transcendentals=0),
        name="split_columns",
    )(inputs, cotangent)


def per_device(inputs, cotangent, lengths, item_ids, owner_row, w_project, w_output):
    core = lax.axis_index("c")
    y_here = lax.axis_index("y")
    z_here = lax.axis_index(SEQ)
    lane = jnp.arange(LANES, dtype=jnp.int32)

    slot, local_row = routing(item_ids, owner_row)
    lens = lengths.reshape(-1)
    lens_row = jnp.concatenate([lens // 256, lens % 256])
    lens_row = jnp.pad(lens_row, (0, LANES - lens_row.shape[0]))
    small = jnp.pad(jnp.stack([slot, local_row, lens_row]), ((0, 5), (0, 0))).astype(BF16)
    high = PART_ROWS // 8
    wp_high = 2 * high
    n_w = wp_high + 2
    wp_tiles = w_project.reshape(ZR, high, 8, 2, LANES).transpose(0, 1, 3, 2, 4)
    wp_tiles = wp_tiles.reshape(ZR, wp_high, 8, LANES)
    wo_tiles = w_output.T.reshape(ZR, high, 8, 64).transpose(0, 2, 1, 3).reshape(ZR, 1, 8, LANES)
    small = jnp.broadcast_to(small[None, None], (ZR, 1, 8, LANES))
    w_tiles = jnp.concatenate([wp_tiles, wo_tiles, small], axis=1)

    spread = exchange(split_columns(inputs[0], cotangent[0]), PAIR)
    spread = spread.reshape(Z, 16, 8, LANES)
    w_tiles = jnp.broadcast_to(w_tiles[None], (ZQ, ZR, n_w, 8, LANES)).reshape(Z, n_w, 8, LANES)
    arrived = exchange(jnp.concatenate([spread, w_tiles], axis=1), SEQ)
    mine = arrived[:, :16].reshape(Z, 2, 64, LANES).transpose(1, 0, 2, 3)
    packs = lax.all_gather(mine.reshape(1, 2, LENGTH, LANES), PAIR, axis=0, tiled=True)

    by_head = exchange(arrived[:, 16:].reshape(YC, 2, n_w, 8, LANES), PAIR)
    wp_part = by_head[:, :, :wp_high].reshape(YC, 2, high, 2, 8, LANES)
    wp_part = wp_part.transpose(0, 2, 4, 1, 3, 5).reshape(YC, PART_ROWS, 4 * HEAD_DIM)
    wo_part = by_head[:, :, wp_high].reshape(YC, 2, 8, high, 64).transpose(0, 3, 2, 1, 4)
    w_part = jnp.concatenate([wp_part, wo_part.reshape(YC, PART_ROWS, HEAD_DIM)], axis=2)
    w_all = jnp.broadcast_to(w_part[None], (X * ZR,) + w_part.shape)
    weights = exchange(w_all, SHARE).reshape(X, ZR, YC, PART_ROWS, HIDDEN)

    facts = by_head[:, :, n_w - 1].astype(F32)
    slots = facts[:, :, 0].astype(jnp.int32)
    tag_of = facts[:, :, 1]
    lens_all = facts[:, 0, 2, :12].reshape(YC, 2, 2, 3)
    lens_all = (lens_all[:, 0] * 256.0 + lens_all[:, 1]).astype(jnp.int32).reshape(Z, 3)
    pack_lens = lax.dynamic_index_in_dim(lens_all, z_here, 0, keepdims=False)
    ends = jnp.cumsum(pack_lens)

    info = jnp.concatenate([ends, core[None]]).astype(jnp.int32)
    slot_ids = jnp.arange(SLOTS, dtype=jnp.int32)
    placed = slots[:, :, None, :] == slot_ids[None, None, :, None]
    tags = jnp.sum(jnp.where(placed, tag_of[:, :, None, :], 0.0), axis=3)
    tags = tags.reshape(YC, 2, OWNERS, CAP).transpose(2, 1, 0, 3).reshape(OWNERS, 1, LANES)
    tags = jnp.broadcast_to(tags.astype(BF16), (OWNERS, 16, LANES))

    kept, sent, grads = heads_backward(info, packs, weights)

    shared = exchange(grads.reshape(X * YC * ZR, PART_ROWS, HIDDEN), SPREAD)
    shared = shared.reshape(X, YC, ZR, PART_ROWS, HIDDEN)

    got = lax.ppermute(sent, "c", [(0, 1), (1, 0)])
    own, *to_y = pair_sums(y_here[None].astype(jnp.int32), kept, got)
    came = [
        lax.ppermute(to_y[step - 1], "y", [(i, (i + step) % Y) for i in range(Y)])
        for step in range(1, Y)
    ]
    block = (y_here * C + core) * LANES
    dy_own = lax.dynamic_slice(packs, (0, 1, block, 0), (YC, 1, LANES, LANES))[:, 0]

    merged = exchange(payload(own, came, dy_own, shared), SEQ)
    w_grad = merged[:, 64:].astype(F32).reshape(ZQ, ZR, 3, PART_ROWS, LANES)
    w_grad = jnp.sum(w_grad, axis=0)
    grad_proj = w_grad[:, :2].transpose(0, 2, 1, 3).reshape(32, 2 * LANES)
    both_out = w_grad[:, 2].reshape(32, 2, 64)
    grad_out = lax.dynamic_index_in_dim(both_out, z_here & 1, 1, keepdims=False).T

    owned = exchange(place(slots.reshape(2 * YC, LANES), tags, merged), DP)
    return (grad_proj, grad_out, table_sum(owned).T)


def solution(mesh):
    fine = Mesh(mesh.devices.reshape(X, Y, C, ZQ, ZR), ALL)
    return jax.shard_map(
        per_device,
        mesh=fine,
        in_specs=(
            P(DP, None, SEQ, None),
            P(DP, None, SEQ, None),
            P(DP, None, None),
            P(DP, None, SEQ),
            P(),
            P(DP, SEQ),
            P(SEQ, DP),
        ),
        out_specs=(P(DP, SEQ), P(SEQ, DP), P(DP, SEQ)),
        check_vma=False,
    )
```

```python
import jax
import jax.numpy as jnp
from jax import lax
from jax.experimental import pallas as pl
from jax.experimental.pallas import tpu as pltpu
from jax.sharding import Mesh, PartitionSpec as P

HEAD_DIM = 128
NORM_FLOOR = 1.0
F32 = jnp.float32
BF16 = jnp.bfloat16

X, Y, C, ZQ, ZR = 4, 4, 2, 8, 2
YC = Y * C
Z = ZQ * ZR
PAIR = ("y", "c")
DP = ("x", "y", "c")
SEQ = ("zq", "zr")
SHARE = ("x", "zr")
SPREAD = ("x", "y", "c", "zr")
ALL = ("x", "y", "c", "zq", "zr")
OWNERS = X * YC
CAP = 8
ROWS = 256
SLOTS = OWNERS * CAP
LANES = 128
LENGTH = 1024
WIDTH = 1024
HIDDEN = 5 * HEAD_DIM
PART_ROWS = 32 // ZR
STEP = 256
REACH = 512
VMEM_SPEC = pl.BlockSpec(memory_space=pltpu.VMEM)
GRANT = 58
HBM_SPEC = pl.BlockSpec(memory_space=pltpu.HBM)
SMEM_SPEC = pl.BlockSpec(memory_space=pltpu.SMEM)


def exchange(value, axes):
    return lax.all_to_all(value, axes, split_axis=0, concat_axis=0, tiled=True)


def routing(item_ids, owner_row):
    rows = jnp.take(owner_row, item_ids.reshape(-1))
    owner = rows // ROWS
    count = owner.shape[0]
    order = jnp.arange(count, dtype=jnp.int32)
    before = (owner[None, :] == owner[:, None]) & (order[None, :] < order[:, None])
    rank = jnp.sum(before.astype(jnp.int32), axis=1)
    return owner * CAP + rank, rows % ROWS


def dot_nt(a, b):
    return lax.dot_general(a, b, (((1,), (1,)), ((), ())), preferred_element_type=F32)


def dot_tn(a, b):
    return lax.dot_general(a, b, (((0,), (0,)), ((), ())), preferred_element_type=F32)


def heads_kernel(
    info,
    packs,
    weights,
    kept,
    sent,
    grads,
    x_v,
    dy_v,
    w_v,
    acts,
    slope,
    d_value,
    d_key,
    d_z,
    gated,
    kept_v,
    sent_v,
    grads_v,
    sems,
    w_sems,
    out_sems,
):
    hd = HEAD_DIM
    scale = hd**-0.5
    u_cols, v_cols, q_cols, k_cols = (slice(m * hd, (m + 1) * hd) for m in range(4))
    steps = LENGTH // STEP
    copies = [
        pltpu.make_async_copy(
            packs.at[:, t, pl.ds(n * STEP, STEP)],
            held.at[:, pl.ds(n * STEP, STEP)],
            sems.at[t * steps + n],
        )
        for t, held in enumerate((x_v, dy_v))
        for n in range(steps)
    ]
    w_copies = [
        pltpu.make_async_copy(weights.at[x, r], w_v.at[x, :, r], w_sems.at[x * ZR + r])
        for x in range(X)
        for r in range(ZR)
    ]
    for copy in copies[:1] + w_copies + copies[1:]:
        copy.start()
    d_value[...] = jnp.zeros_like(d_value)
    d_key[...] = jnp.zeros_like(d_key)

    for copy in w_copies:
        copy.wait()
    wp = w_v[..., : 4 * hd].reshape(WIDTH, 4 * hd)
    wo = w_v[..., 4 * hd :].reshape(WIDTH, hd)

    for step in range(0, steps, 2):
        copies[step].wait()
        copies[step + 1].wait()
        rows = slice(step * STEP, (step + 2) * STEP)
        px = jnp.concatenate([x_v[g, rows, :] for g in range(8)], axis=1)
        z_pre = jnp.dot(px, wp, preferred_element_type=F32)
        sigma = jax.nn.sigmoid(z_pre)
        silu = z_pre * sigma
        acts[rows, :] = silu.astype(BF16)
        slope[rows, :] = sigma + silu * (1.0 - sigma)

    for step in range(steps):
        copies[steps + step].wait()
    for step in range(steps):
        base = step * STEP
        first = max(0, base - REACH)
        rows = slice(base, base + STEP)
        span = slice(first, base + STEP)
        pos_k = lax.broadcasted_iota(jnp.int32, (1, base + STEP - first), 1) + first
        pos_q = lax.broadcasted_iota(jnp.int32, (STEP, 1), 0) + base
        start = jnp.zeros_like(pos_q)
        for n in range(3):
            start = jnp.where(pos_q >= info[n], info[n], start)
        masked = (pos_k <= pos_q) & (pos_k >= start)
        query = acts[rows, q_cols]
        key = acts[span, k_cols]
        value = acts[span, v_cols]
        scores = dot_nt(query, key) * scale
        sigma = jnp.where(masked, jax.nn.sigmoid(scores), 0.0)
        silu = scores * sigma
        attn = silu.astype(BF16)
        factor = sigma + silu * (1.0 - sigma)
        mixed = jnp.dot(attn, value, preferred_element_type=F32)
        centred = mixed - jnp.mean(mixed, axis=-1, keepdims=True)
        inv_std = lax.rsqrt(jnp.mean(centred * centred, axis=-1, keepdims=True) + NORM_FLOOR)
        normed = centred * inv_std
        gating = acts[rows, u_cols].astype(F32)
        gated[rows, :] = (normed * gating).astype(BF16)
        pdy = jnp.concatenate([dy_v[g, rows, :] for g in range(8)], axis=1)
        d_gated = jnp.dot(pdy, wo, preferred_element_type=F32)
        d_normed = d_gated * gating
        d_mixed = (
            inv_std
            * (
                d_normed
                - jnp.mean(d_normed, axis=-1, keepdims=True)
                - normed * jnp.mean(d_normed * normed, axis=-1, keepdims=True)
            )
        ).astype(BF16)
        d_scores = (dot_nt(d_mixed, value) * factor).astype(BF16)
        d_query = jnp.dot(d_scores, key, preferred_element_type=F32)
        d_value[:, span] += jnp.dot(d_mixed.T, attn, preferred_element_type=F32)
        d_key[:, span] += jnp.dot(query.T, d_scores, preferred_element_type=F32)
        d_z[rows, u_cols] = (d_gated * normed * slope[rows, u_cols]).astype(BF16)
        d_z[rows, q_cols] = (d_query * (slope[rows, q_cols] * scale)).astype(BF16)

    d_z[:, v_cols] = (d_value[...].T * slope[:, v_cols]).astype(BF16)
    d_z[:, k_cols] = (d_key[...].T * (slope[:, k_cols] * scale)).astype(BF16)

    core = info[3]
    outs = []
    whole = dot_nt(d_z[...], wp).astype(BF16)
    for y in range(Y):
        part = whole[y * STEP : (y + 1) * STEP]

        @pl.when(core == 0)
        def _():
            kept_v[y] = part[:LANES]
            sent_v[y] = part[LANES:]

        @pl.when(core != 0)
        def _():
            kept_v[y] = part[LANES:]
            sent_v[y] = part[:LANES]

        for held, out in ((sent_v, sent), (kept_v, kept)):
            outs.append(pltpu.make_async_copy(held.at[y], out.at[y], out_sems.at[len(outs)]))
            outs[-1].start()

    for x in range(X):
        for dest, source, pack in ((slice(0, 512), d_z, x_v), (slice(512, 640), gated, dy_v)):
            columns = jnp.concatenate([pack[2 * x], pack[2 * x + 1]], axis=1)
            block = dot_tn(columns, source[...]).astype(BF16)
            grads_v[x, :, :, :, dest] = block.reshape(YC, ZR, PART_ROWS, block.shape[1])
        outs.append(pltpu.make_async_copy(grads_v.at[x], grads.at[x], out_sems.at[len(outs)]))
        outs[-1].start()
    for copy in outs:
        copy.wait()


def heads_backward(info, packs, weights):
    half = jax.ShapeDtypeStruct((Y, LANES, WIDTH), BF16)
    return pl.pallas_call(
        heads_kernel,
        out_shape=(
            half,
            half,
            jax.ShapeDtypeStruct((X, YC, ZR, PART_ROWS, HIDDEN), BF16),
        ),
        in_specs=[SMEM_SPEC, HBM_SPEC, pl.BlockSpec(memory_space=pl.ANY)],
        out_specs=(HBM_SPEC,) * 3,
        scratch_shapes=[
            pltpu.VMEM((8, LENGTH, LANES), BF16),
            pltpu.VMEM((8, LENGTH, LANES), BF16),
            pltpu.VMEM((X, YC, ZR, PART_ROWS, HIDDEN), BF16),
            pltpu.VMEM((LENGTH, 4 * HEAD_DIM), BF16),
            pltpu.VMEM((LENGTH, 4 * HEAD_DIM), F32),
            pltpu.VMEM((HEAD_DIM, LENGTH), F32),
            pltpu.VMEM((HEAD_DIM, LENGTH), F32),
            pltpu.VMEM((LENGTH, 4 * HEAD_DIM), BF16),
            pltpu.VMEM((LENGTH, HEAD_DIM), BF16),
            pltpu.VMEM((Y, LANES, WIDTH), BF16),
            pltpu.VMEM((Y, LANES, WIDTH), BF16),
            pltpu.VMEM((X, YC, ZR, PART_ROWS, HIDDEN), BF16),
            pltpu.SemaphoreType.DMA((2 * LENGTH // STEP,)),
            pltpu.SemaphoreType.DMA((X * ZR,)),
            pltpu.SemaphoreType.DMA((2 * Y + X,)),
        ],
        compiler_params=pltpu.CompilerParams(vmem_limit_bytes=GRANT * 2**20),
        cost_estimate=pl.CostEstimate(
            flops=5_000_000_000, bytes_accessed=9_000_000, transcendentals=2_000_000
        ),
        name="heads",
    )(info, packs, weights)


def pair_kernel(place, kept, got, own, to_1, to_2, to_3, own_v, sem):
    y = place[0]
    own_v[...] = kept[y].astype(F32) + got[y].astype(F32)
    copy = pltpu.make_async_copy(own_v, own, sem)
    copy.start()
    for step, block in ((1, to_1), (2, to_2), (3, to_3)):
        other = (y + step) & (Y - 1)
        block[...] = (kept[other].astype(F32) + got[other].astype(F32)).astype(BF16)
    copy.wait()


def pair_sums(y, kept, got):
    block = jax.ShapeDtypeStruct((LANES, WIDTH), BF16)
    return pl.pallas_call(
        pair_kernel,
        out_shape=(jax.ShapeDtypeStruct((LANES, WIDTH), F32),) + (block,) * (Y - 1),
        in_specs=[SMEM_SPEC, VMEM_SPEC, VMEM_SPEC],
        out_specs=(HBM_SPEC,) + (VMEM_SPEC,) * (Y - 1),
        scratch_shapes=[pltpu.VMEM((LANES, WIDTH), F32), pltpu.SemaphoreType.DMA],
        compiler_params=pltpu.CompilerParams(vmem_limit_bytes=32 * 2**20),
        cost_estimate=pl.CostEstimate(flops=500_000, bytes_accessed=3_000_000, transcendentals=0),
        name="pair_sums",
    )(y, kept, got)


def payload_kernel(own, came_1, came_2, came_3, dy, shared, out, own_v, sem):
    copy = pltpu.make_async_copy(own, own_v, sem)
    copy.start()
    for h in range(YC):
        total = jnp.zeros((PART_ROWS, HIDDEN), F32)
        for x in range(X):
            for r in range(ZR):
                total = total + shared[x, h, r].astype(F32)
        total = total.astype(BF16)
        for s in range(2):
            for n, col in enumerate((2 * s, 2 * s + 1, 4)):
                first = 64 + n * PART_ROWS
                out[2 * h + s, first : first + PART_ROWS, :] = total[
                    :, col * LANES : (col + 1) * LANES
                ]
    copy.wait()
    lane = lax.broadcasted_iota(jnp.int32, (64, LANES), 1)
    for m in range(8):
        cols = slice(m * LANES, (m + 1) * LANES)
        total = own_v[:, cols] + dy[m].astype(F32)
        for came in (came_1, came_2, came_3):
            total = total + came[:, cols].astype(F32)
        low, high = total[:64], total[64:]
        even = jnp.where(lane < 64, low, pltpu.roll(high, 64, 1))
        odd = jnp.where(lane < 64, pltpu.roll(low, 64, 1), high)
        out[2 * m, :64, :] = even.astype(BF16)
        out[2 * m + 1, :64, :] = odd.astype(BF16)


def payload(own, came, dy, shared):
    return pl.pallas_call(
        payload_kernel,
        out_shape=jax.ShapeDtypeStruct((Z, 64 + 3 * PART_ROWS, LANES), BF16),
        in_specs=[HBM_SPEC] + [VMEM_SPEC] * 5,
        out_specs=VMEM_SPEC,
        scratch_shapes=[pltpu.VMEM((LANES, WIDTH), F32), pltpu.SemaphoreType.DMA],
        compiler_params=pltpu.CompilerParams(vmem_limit_bytes=32 * 2**20),
        cost_estimate=pl.CostEstimate(flops=1_500_000, bytes_accessed=4_000_000, transcendentals=0),
        name="payload",
    )(own, *came, dy, shared)


def place_kernel(slots, tags, merged, out):
    slot_ids = lax.broadcasted_iota(jnp.int32, (SLOTS, LANES), 0)
    lane = lax.broadcasted_iota(jnp.int32, (SLOTS, LANES), 1)
    for pair in range(YC // 2):
        both = []
        for yc in (2 * pair, 2 * pair + 1):
            tokens = jnp.concatenate([merged[2 * yc, :64, :], merged[2 * yc + 1, :64, :]], axis=0)
            moved = [
                jnp.dot(
                    (slots[2 * yc + s : 2 * yc + s + 1, :] == slot_ids).astype(BF16),
                    tokens,
                    preferred_element_type=F32,
                )
                for s in range(2)
            ]
            rows = jnp.where(lane < 64, moved[0], moved[1])
            both.append(rows.reshape(OWNERS, CAP, LANES))
        out[:, pair * 16 : (pair + 1) * 16, :] = jnp.concatenate(both, axis=1).astype(BF16)
    out[:, YC * CAP :, :] = tags[...]


def place(slots, tags, merged):
    return pl.pallas_call(
        place_kernel,
        out_shape=jax.ShapeDtypeStruct((OWNERS, YC * CAP + 16, LANES), BF16),
        in_specs=[VMEM_SPEC] * 3,
        out_specs=VMEM_SPEC,
        compiler_params=pltpu.CompilerParams(vmem_limit_bytes=32 * 2**20),
        cost_estimate=pl.CostEstimate(
            flops=135_000_000, bytes_accessed=1_000_000, transcendentals=0
        ),
        name="place",
    )(slots, tags, merged)


def table_kernel(owned, out):
    count = YC * CAP
    row_ids = lax.broadcasted_iota(jnp.int32, (ROWS, LANES), 0).astype(F32)
    left = lax.broadcasted_iota(jnp.int32, (count, LANES), 1) < 64
    total = jnp.zeros((ROWS, LANES), F32)
    for pair in range(OWNERS // 2):
        select, rows = [], []
        for source in (2 * pair, 2 * pair + 1):
            tag = owned[source, count:, :].astype(F32)[:1]
            select.append((tag == row_ids).astype(BF16))
            here = owned[source, :count, :].astype(F32)
            rows.append(jnp.where(left, here, 0.0).astype(BF16))
            rows.append(jnp.where(left, 0.0, here).astype(BF16))
        total = total + jnp.dot(
            jnp.concatenate(select, axis=1),
            jnp.concatenate(rows, axis=0),
            preferred_element_type=F32,
        )
    out[...] = (total + pltpu.roll(total, 64, 1)).T[:64]


def table_sum(owned):
    return pl.pallas_call(
        table_kernel,
        out_shape=jax.ShapeDtypeStruct((64, ROWS), F32),
        in_specs=[VMEM_SPEC],
        out_specs=VMEM_SPEC,
        compiler_params=pltpu.CompilerParams(vmem_limit_bytes=32 * 2**20),
        cost_estimate=pl.CostEstimate(
            flops=270_000_000, bytes_accessed=1_000_000, transcendentals=0
        ),
        name="table_sum",
    )(owned)


def split_kernel(inputs, cotangent, out, sems):
    copies = [
        pltpu.make_async_copy(
            source.at[:, :, pl.ds(g * LANES, LANES)], out.at[g, :, t], sems.at[2 * g + t]
        )
        for g in range(8)
        for t, source in enumerate((inputs, cotangent))
    ]
    for copy in copies:
        copy.start()
    for copy in copies:
        copy.wait()


def split_columns(inputs, cotangent):
    return pl.pallas_call(
        split_kernel,
        out_shape=jax.ShapeDtypeStruct((8, 2, 2, 64, LANES), BF16),
        in_specs=[HBM_SPEC] * 2,
        out_specs=HBM_SPEC,
        scratch_shapes=[pltpu.SemaphoreType.DMA((16,))],
        compiler_params=pltpu.CompilerParams(vmem_limit_bytes=GRANT * 2**20),
        cost_estimate=pl.CostEstimate(flops=0, bytes_accessed=1_000_000, transcendentals=0),
        name="split_columns",
    )(inputs, cotangent)


def per_device(inputs, cotangent, lengths, item_ids, owner_row, w_project, w_output):
    core = lax.axis_index("c")
    y_here = lax.axis_index("y")
    z_here = lax.axis_index(SEQ)
    lane = jnp.arange(LANES, dtype=jnp.int32)

    slot, local_row = routing(item_ids, owner_row)
    lens = lengths.reshape(-1)
    lens_row = jnp.concatenate([lens // 256, lens % 256])
    lens_row = jnp.pad(lens_row, (0, LANES - lens_row.shape[0]))
    small = jnp.pad(jnp.stack([slot, local_row, lens_row]), ((0, 5), (0, 0))).astype(BF16)
    high = PART_ROWS // 8
    wp_high = 2 * high
    n_w = wp_high + 2
    wp_tiles = w_project.reshape(ZR, high, 8, 2, LANES).transpose(0, 1, 3, 2, 4)
    wp_tiles = wp_tiles.reshape(ZR, wp_high, 8, LANES)
    wo_tiles = w_output.T.reshape(ZR, high, 8, 64).transpose(0, 2, 1, 3).reshape(ZR, 1, 8, LANES)
    small = jnp.broadcast_to(small[None, None], (ZR, 1, 8, LANES))
    w_tiles = jnp.concatenate([wp_tiles, wo_tiles, small], axis=1)

    spread = exchange(split_columns(inputs[0], cotangent[0]), PAIR)
    spread = spread.reshape(Z, 16, 8, LANES)
    w_tiles = jnp.broadcast_to(w_tiles[None], (ZQ, ZR, n_w, 8, LANES)).reshape(Z, n_w, 8, LANES)
    arrived = exchange(jnp.concatenate([spread, w_tiles], axis=1), SEQ)
    mine = arrived[:, :16].reshape(Z, 2, 64, LANES).transpose(1, 0, 2, 3)
    packs = lax.all_gather(mine.reshape(1, 2, LENGTH, LANES), PAIR, axis=0, tiled=True)

    by_head = exchange(arrived[:, 16:].reshape(YC, 2, n_w, 8, LANES), PAIR)
    wp_part = by_head[:, :, :wp_high].reshape(YC, 2, high, 2, 8, LANES)
    wp_part = wp_part.transpose(0, 2, 4, 1, 3, 5).reshape(YC, PART_ROWS, 4 * HEAD_DIM)
    wo_part = by_head[:, :, wp_high].reshape(YC, 2, 8, high, 64).transpose(0, 3, 2, 1, 4)
    w_part = jnp.concatenate([wp_part, wo_part.reshape(YC, PART_ROWS, HEAD_DIM)], axis=2)
    w_all = jnp.broadcast_to(w_part[None], (X * ZR,) + w_part.shape)
    weights = exchange(w_all, SHARE).reshape(X, ZR, YC, PART_ROWS, HIDDEN)

    facts = by_head[:, :, n_w - 1].astype(F32)
    slots = facts[:, :, 0].astype(jnp.int32)
    tag_of = facts[:, :, 1]
    lens_all = facts[:, 0, 2, :12].reshape(YC, 2, 2, 3)
    lens_all = (lens_all[:, 0] * 256.0 + lens_all[:, 1]).astype(jnp.int32).reshape(Z, 3)
    pack_lens = lax.dynamic_index_in_dim(lens_all, z_here, 0, keepdims=False)
    ends = jnp.cumsum(pack_lens)

    info = jnp.concatenate([ends, core[None]]).astype(jnp.int32)
    slot_ids = jnp.arange(SLOTS, dtype=jnp.int32)
    placed = slots[:, :, None, :] == slot_ids[None, None, :, None]
    tags = jnp.sum(jnp.where(placed, tag_of[:, :, None, :], 0.0), axis=3)
    tags = tags.reshape(YC, 2, OWNERS, CAP).transpose(2, 1, 0, 3).reshape(OWNERS, 1, LANES)
    tags = jnp.broadcast_to(tags.astype(BF16), (OWNERS, 16, LANES))

    kept, sent, grads = heads_backward(info, packs, weights)

    shared = exchange(grads.reshape(X * YC * ZR, PART_ROWS, HIDDEN), SPREAD)
    shared = shared.reshape(X, YC, ZR, PART_ROWS, HIDDEN)

    got = lax.ppermute(sent, "c", [(0, 1), (1, 0)])
    own, *to_y = pair_sums(y_here[None].astype(jnp.int32), kept, got)
    came = [
        lax.ppermute(to_y[step - 1], "y", [(i, (i + step) % Y) for i in range(Y)])
        for step in range(1, Y)
    ]
    block = (y_here * C + core) * LANES
    dy_own = lax.dynamic_slice(packs, (0, 1, block, 0), (YC, 1, LANES, LANES))[:, 0]

    merged = exchange(payload(own, came, dy_own, shared), SEQ)
    w_grad = merged[:, 64:].astype(F32).reshape(ZQ, ZR, 3, PART_ROWS, LANES)
    w_grad = jnp.sum(w_grad, axis=0)
    grad_proj = w_grad[:, :2].transpose(0, 2, 1, 3).reshape(32, 2 * LANES)
    both_out = w_grad[:, 2].reshape(32, 2, 64)
    grad_out = lax.dynamic_index_in_dim(both_out, z_here & 1, 1, keepdims=False).T

    owned = exchange(place(slots.reshape(2 * YC, LANES), tags, merged), DP)
    return (grad_proj, grad_out, table_sum(owned).T)


def solution(mesh):
    fine = Mesh(mesh.devices.reshape(X, Y, C, ZQ, ZR), ALL)
    return jax.shard_map(
        per_device,
        mesh=fine,
        in_specs=(
            P(DP, None, SEQ, None),
            P(DP, None, SEQ, None),
            P(DP, None, None),
            P(DP, None, SEQ),
            P(),
            P(DP, SEQ),
            P(SEQ, DP),
        ),
        out_specs=(P(DP, SEQ), P(SEQ, DP), P(DP, SEQ)),
        check_vma=False,
    )
```

```python
import jax
import jax.numpy as jnp
from jax import lax
from jax.experimental import pallas as pl
from jax.experimental.pallas import tpu as pltpu
from jax.sharding import Mesh, PartitionSpec as P

HEAD_DIM = 128
NORM_FLOOR = 1.0
F32 = jnp.float32
BF16 = jnp.bfloat16

X, Y, C, ZQ, ZR = 4, 4, 2, 8, 2
YC = Y * C
Z = ZQ * ZR
PAIR = ("y", "c")
DP = ("x", "y", "c")
SEQ = ("zq", "zr")
SHARE = ("x", "zr")
SPREAD = ("x", "y", "c", "zr")
ALL = ("x", "y", "c", "zq", "zr")
OWNERS = X * YC
CAP = 8
ROWS = 256
SLOTS = OWNERS * CAP
LANES = 128
LENGTH = 1024
WIDTH = 1024
HIDDEN = 5 * HEAD_DIM
PART_ROWS = 32 // ZR
STEP = 256
REACH = 512
VMEM_SPEC = pl.BlockSpec(memory_space=pltpu.VMEM)
GRANT = 58
HBM_SPEC = pl.BlockSpec(memory_space=pltpu.HBM)
SMEM_SPEC = pl.BlockSpec(memory_space=pltpu.SMEM)


def exchange(value, axes):
    return lax.all_to_all(value, axes, split_axis=0, concat_axis=0, tiled=True)


def routing(item_ids, owner_row):
    rows = jnp.take(owner_row, item_ids.reshape(-1))
    owner = rows // ROWS
    count = owner.shape[0]
    order = jnp.arange(count, dtype=jnp.int32)
    before = (owner[None, :] == owner[:, None]) & (order[None, :] < order[:, None])
    rank = jnp.sum(before.astype(jnp.int32), axis=1)
    return owner * CAP + rank, rows % ROWS


def dot_nt(a, b):
    return lax.dot_general(a, b, (((1,), (1,)), ((), ())), preferred_element_type=F32)


def dot_tn(a, b):
    return lax.dot_general(a, b, (((0,), (0,)), ((), ())), preferred_element_type=F32)


def heads_kernel(
    info,
    packs,
    weights,
    kept,
    sent,
    grads,
    x_v,
    dy_v,
    w_v,
    acts,
    slope,
    d_value,
    d_key,
    d_z,
    gated,
    kept_v,
    sent_v,
    grads_v,
    sems,
    w_sems,
    out_sems,
):
    hd = HEAD_DIM
    scale = hd**-0.5
    u_cols, v_cols, q_cols, k_cols = (slice(m * hd, (m + 1) * hd) for m in range(4))
    steps = LENGTH // STEP
    copies = [
        pltpu.make_async_copy(
            packs.at[:, t, pl.ds(n * STEP, STEP)],
            held.at[:, pl.ds(n * STEP, STEP)],
            sems.at[t * steps + n],
        )
        for t, held in enumerate((x_v, dy_v))
        for n in range(steps)
    ]
    w_copies = [
        pltpu.make_async_copy(weights.at[x, r], w_v.at[x, :, r], w_sems.at[x * ZR + r])
        for x in range(X)
        for r in range(ZR)
    ]
    for copy in copies[:1] + w_copies + copies[1:]:
        copy.start()
    d_value[...] = jnp.zeros_like(d_value)
    d_key[...] = jnp.zeros_like(d_key)

    for copy in w_copies:
        copy.wait()
    wp = w_v[..., : 4 * hd].reshape(WIDTH, 4 * hd)
    wo = w_v[..., 4 * hd :].reshape(WIDTH, hd)

    for step in range(0, steps, 2):
        copies[step].wait()
        copies[step + 1].wait()
        rows = slice(step * STEP, (step + 2) * STEP)
        px = jnp.concatenate([x_v[g, rows, :] for g in range(8)], axis=1)
        z_pre = jnp.dot(px, wp, preferred_element_type=F32)
        sigma = jax.nn.sigmoid(z_pre)
        silu = z_pre * sigma
        acts[rows, :] = silu.astype(BF16)
        slope[rows, :] = sigma + silu * (1.0 - sigma)

    for step in range(steps):
        copies[steps + step].wait()
    for step in range(steps):
        base = step * STEP
        first = max(0, base - REACH)
        rows = slice(base, base + STEP)
        span = slice(first, base + STEP)
        pos_k = lax.broadcasted_iota(jnp.int32, (1, base + STEP - first), 1) + first
        pos_q = lax.broadcasted_iota(jnp.int32, (STEP, 1), 0) + base
        start = jnp.zeros_like(pos_q)
        for n in range(3):
            start = jnp.where(pos_q >= info[n], info[n], start)
        masked = (pos_k <= pos_q) & (pos_k >= start)
        query = acts[rows, q_cols]
        key = acts[span, k_cols]
        value = acts[span, v_cols]
        scores = dot_nt(query, key) * scale
        sigma = jnp.where(masked, jax.nn.sigmoid(scores), 0.0)
        silu = scores * sigma
        attn = silu.astype(BF16)
        factor = sigma + silu * (1.0 - sigma)
        mixed = jnp.dot(attn, value, preferred_element_type=F32)
        centred = mixed - jnp.mean(mixed, axis=-1, keepdims=True)
        inv_std = lax.rsqrt(jnp.mean(centred * centred, axis=-1, keepdims=True) + NORM_FLOOR)
        normed = centred * inv_std
        gating = acts[rows, u_cols].astype(F32)
        gated[rows, :] = (normed * gating).astype(BF16)
        pdy = jnp.concatenate([dy_v[g, rows, :] for g in range(8)], axis=1)
        d_gated = jnp.dot(pdy, wo, preferred_element_type=F32)
        d_normed = d_gated * gating
        d_mixed = (
            inv_std
            * (
                d_normed
                - jnp.mean(d_normed, axis=-1, keepdims=True)
                - normed * jnp.mean(d_normed * normed, axis=-1, keepdims=True)
            )
        ).astype(BF16)
        d_scores = (dot_nt(d_mixed, value) * factor).astype(BF16)
        d_query = jnp.dot(d_scores, key, preferred_element_type=F32)
        d_value[:, span] += jnp.dot(d_mixed.T, attn, preferred_element_type=F32)
        d_key[:, span] += jnp.dot(query.T, d_scores, preferred_element_type=F32)
        d_z[rows, u_cols] = (d_gated * normed * slope[rows, u_cols]).astype(BF16)
        d_z[rows, q_cols] = (d_query * (slope[rows, q_cols] * scale)).astype(BF16)

    d_z[:, v_cols] = (d_value[...].T * slope[:, v_cols]).astype(BF16)
    d_z[:, k_cols] = (d_key[...].T * (slope[:, k_cols] * scale)).astype(BF16)

    core = info[3]
    outs = []
    whole = dot_nt(d_z[...], wp).astype(BF16)
    for y in range(Y):
        part = whole[y * STEP : (y + 1) * STEP]

        @pl.when(core == 0)
        def _():
            kept_v[y] = part[:LANES]
            sent_v[y] = part[LANES:]

        @pl.when(core != 0)
        def _():
            kept_v[y] = part[LANES:]
            sent_v[y] = part[:LANES]

        for held, out in ((sent_v, sent), (kept_v, kept)):
            outs.append(pltpu.make_async_copy(held.at[y], out.at[y], out_sems.at[len(outs)]))
            outs[-1].start()

    for x in range(X):
        for dest, source, pack in ((slice(0, 512), d_z, x_v), (slice(512, 640), gated, dy_v)):
            columns = jnp.concatenate([pack[2 * x], pack[2 * x + 1]], axis=1)
            block = dot_tn(columns, source[...]).astype(BF16)
            grads_v[x, :, :, :, dest] = block.reshape(YC, ZR, PART_ROWS, block.shape[1])
        outs.append(pltpu.make_async_copy(grads_v.at[x], grads.at[x], out_sems.at[len(outs)]))
        outs[-1].start()
    for copy in outs:
        copy.wait()


def heads_backward(info, packs, weights):
    half = jax.ShapeDtypeStruct((Y, LANES, WIDTH), BF16)
    return pl.pallas_call(
        heads_kernel,
        out_shape=(
            half,
            half,
            jax.ShapeDtypeStruct((X, YC, ZR, PART_ROWS, HIDDEN), BF16),
        ),
        in_specs=[SMEM_SPEC, HBM_SPEC, pl.BlockSpec(memory_space=pl.ANY)],
        out_specs=(HBM_SPEC,) * 3,
        scratch_shapes=[
            pltpu.VMEM((8, LENGTH, LANES), BF16),
            pltpu.VMEM((8, LENGTH, LANES), BF16),
            pltpu.VMEM((X, YC, ZR, PART_ROWS, HIDDEN), BF16),
            pltpu.VMEM((LENGTH, 4 * HEAD_DIM), BF16),
            pltpu.VMEM((LENGTH, 4 * HEAD_DIM), F32),
            pltpu.VMEM((HEAD_DIM, LENGTH), F32),
            pltpu.VMEM((HEAD_DIM, LENGTH), F32),
            pltpu.VMEM((LENGTH, 4 * HEAD_DIM), BF16),
            pltpu.VMEM((LENGTH, HEAD_DIM), BF16),
            pltpu.VMEM((Y, LANES, WIDTH), BF16),
            pltpu.VMEM((Y, LANES, WIDTH), BF16),
            pltpu.VMEM((X, YC, ZR, PART_ROWS, HIDDEN), BF16),
            pltpu.SemaphoreType.DMA((2 * LENGTH // STEP,)),
            pltpu.SemaphoreType.DMA((X * ZR,)),
            pltpu.SemaphoreType.DMA((2 * Y + X,)),
        ],
        compiler_params=pltpu.CompilerParams(vmem_limit_bytes=GRANT * 2**20),
        cost_estimate=pl.CostEstimate(
            flops=5_000_000_000, bytes_accessed=9_000_000, transcendentals=2_000_000
        ),
        name="heads",
    )(info, packs, weights)


def pair_kernel(place, kept, got, own, to_1, to_2, to_3, own_v, sem):
    y = place[0]
    own_v[...] = (kept[y].astype(F32) + got[y].astype(F32)).astype(BF16)
    copy = pltpu.make_async_copy(own_v, own, sem)
    copy.start()
    for step, block in ((1, to_1), (2, to_2), (3, to_3)):
        other = (y + step) & (Y - 1)
        block[...] = (kept[other].astype(F32) + got[other].astype(F32)).astype(BF16)
    copy.wait()


def pair_sums(y, kept, got):
    block = jax.ShapeDtypeStruct((LANES, WIDTH), BF16)
    return pl.pallas_call(
        pair_kernel,
        out_shape=(block,) * Y,
        in_specs=[SMEM_SPEC, VMEM_SPEC, VMEM_SPEC],
        out_specs=(HBM_SPEC,) + (VMEM_SPEC,) * (Y - 1),
        scratch_shapes=[pltpu.VMEM((LANES, WIDTH), BF16), pltpu.SemaphoreType.DMA],
        compiler_params=pltpu.CompilerParams(vmem_limit_bytes=32 * 2**20),
        cost_estimate=pl.CostEstimate(flops=500_000, bytes_accessed=3_000_000, transcendentals=0),
        name="pair_sums",
    )(y, kept, got)


def payload_kernel(own, came_1, came_2, came_3, dy, shared, out, own_v, sem):
    copy = pltpu.make_async_copy(own, own_v, sem)
    copy.start()
    for h in range(YC):
        total = jnp.zeros((PART_ROWS, HIDDEN), F32)
        for x in range(X):
            for r in range(ZR):
                total = total + shared[x, h, r].astype(F32)
        total = total.astype(BF16)
        for s in range(2):
            for n, col in enumerate((2 * s, 2 * s + 1, 4)):
                first = 64 + n * PART_ROWS
                out[2 * h + s, first : first + PART_ROWS, :] = total[
                    :, col * LANES : (col + 1) * LANES
                ]
    copy.wait()
    lane = lax.broadcasted_iota(jnp.int32, (64, LANES), 1)
    for m in range(8):
        cols = slice(m * LANES, (m + 1) * LANES)
        total = own_v[:, cols].astype(F32) + dy[m].astype(F32)
        for came in (came_1, came_2, came_3):
            total = total + came[:, cols].astype(F32)
        low, high = total[:64], total[64:]
        even = jnp.where(lane < 64, low, pltpu.roll(high, 64, 1))
        odd = jnp.where(lane < 64, pltpu.roll(low, 64, 1), high)
        out[2 * m, :64, :] = even.astype(BF16)
        out[2 * m + 1, :64, :] = odd.astype(BF16)


def payload(own, came, dy, shared):
    return pl.pallas_call(
        payload_kernel,
        out_shape=jax.ShapeDtypeStruct((Z, 64 + 3 * PART_ROWS, LANES), BF16),
        in_specs=[HBM_SPEC] + [VMEM_SPEC] * 5,
        out_specs=VMEM_SPEC,
        scratch_shapes=[pltpu.VMEM((LANES, WIDTH), BF16), pltpu.SemaphoreType.DMA],
        compiler_params=pltpu.CompilerParams(vmem_limit_bytes=32 * 2**20),
        cost_estimate=pl.CostEstimate(flops=1_500_000, bytes_accessed=4_000_000, transcendentals=0),
        name="payload",
    )(own, *came, dy, shared)


def place_kernel(slots, tags, merged, out):
    slot_ids = lax.broadcasted_iota(jnp.int32, (SLOTS, LANES), 0)
    lane = lax.broadcasted_iota(jnp.int32, (SLOTS, LANES), 1)
    for pair in range(YC // 2):
        both = []
        for yc in (2 * pair, 2 * pair + 1):
            tokens = jnp.concatenate([merged[2 * yc, :64, :], merged[2 * yc + 1, :64, :]], axis=0)
            moved = [
                jnp.dot(
                    (slots[2 * yc + s : 2 * yc + s + 1, :] == slot_ids).astype(BF16),
                    tokens,
                    preferred_element_type=F32,
                )
                for s in range(2)
            ]
            rows = jnp.where(lane < 64, moved[0], moved[1])
            both.append(rows.reshape(OWNERS, CAP, LANES))
        out[:, pair * 16 : (pair + 1) * 16, :] = jnp.concatenate(both, axis=1).astype(BF16)
    out[:, YC * CAP :, :] = tags[...]


def place(slots, tags, merged):
    return pl.pallas_call(
        place_kernel,
        out_shape=jax.ShapeDtypeStruct((OWNERS, YC * CAP + 16, LANES), BF16),
        in_specs=[VMEM_SPEC] * 3,
        out_specs=VMEM_SPEC,
        compiler_params=pltpu.CompilerParams(vmem_limit_bytes=32 * 2**20),
        cost_estimate=pl.CostEstimate(
            flops=135_000_000, bytes_accessed=1_000_000, transcendentals=0
        ),
        name="place",
    )(slots, tags, merged)


def table_kernel(owned, out):
    count = YC * CAP
    row_ids = lax.broadcasted_iota(jnp.int32, (ROWS, LANES), 0).astype(F32)
    left = lax.broadcasted_iota(jnp.int32, (count, LANES), 1) < 64
    total = jnp.zeros((ROWS, LANES), F32)
    for pair in range(OWNERS // 2):
        select, rows = [], []
        for source in (2 * pair, 2 * pair + 1):
            tag = owned[source, count:, :].astype(F32)[:1]
            select.append((tag == row_ids).astype(BF16))
            here = owned[source, :count, :].astype(F32)
            rows.append(jnp.where(left, here, 0.0).astype(BF16))
            rows.append(jnp.where(left, 0.0, here).astype(BF16))
        total = total + jnp.dot(
            jnp.concatenate(select, axis=1),
            jnp.concatenate(rows, axis=0),
            preferred_element_type=F32,
        )
    out[...] = (total + pltpu.roll(total, 64, 1)).T[:64]


def table_sum(owned):
    return pl.pallas_call(
        table_kernel,
        out_shape=jax.ShapeDtypeStruct((64, ROWS), F32),
        in_specs=[VMEM_SPEC],
        out_specs=VMEM_SPEC,
        compiler_params=pltpu.CompilerParams(vmem_limit_bytes=32 * 2**20),
        cost_estimate=pl.CostEstimate(
            flops=270_000_000, bytes_accessed=1_000_000, transcendentals=0
        ),
        name="table_sum",
    )(owned)


def split_kernel(inputs, cotangent, out, sems):
    copies = [
        pltpu.make_async_copy(
            source.at[:, :, pl.ds(g * LANES, LANES)], out.at[g, :, t], sems.at[2 * g + t]
        )
        for g in range(8)
        for t, source in enumerate((inputs, cotangent))
    ]
    for copy in copies:
        copy.start()
    for copy in copies:
        copy.wait()


def split_columns(inputs, cotangent):
    return pl.pallas_call(
        split_kernel,
        out_shape=jax.ShapeDtypeStruct((8, 2, 2, 64, LANES), BF16),
        in_specs=[HBM_SPEC] * 2,
        out_specs=VMEM_SPEC,
        scratch_shapes=[pltpu.SemaphoreType.DMA((16,))],
        compiler_params=pltpu.CompilerParams(vmem_limit_bytes=60 * 2**20),
        cost_estimate=pl.CostEstimate(flops=0, bytes_accessed=1_000_000, transcendentals=0),
        name="split_columns",
    )(inputs, cotangent)


def per_device(inputs, cotangent, lengths, item_ids, owner_row, w_project, w_output):
    core = lax.axis_index("c")
    y_here = lax.axis_index("y")
    z_here = lax.axis_index(SEQ)
    lane = jnp.arange(LANES, dtype=jnp.int32)

    slot, local_row = routing(item_ids, owner_row)
    lens = lengths.reshape(-1)
    lens_row = jnp.concatenate([lens // 256, lens % 256])
    lens_row = jnp.pad(lens_row, (0, LANES - lens_row.shape[0]))
    small = jnp.pad(jnp.stack([slot, local_row, lens_row]), ((0, 5), (0, 0))).astype(BF16)
    high = PART_ROWS // 8
    wp_high = 2 * high
    n_w = wp_high + 2
    wp_tiles = w_project.reshape(ZR, high, 8, 2, LANES).transpose(0, 1, 3, 2, 4)
    wp_tiles = wp_tiles.reshape(ZR, wp_high, 8, LANES)
    wo_tiles = w_output.T.reshape(ZR, high, 8, 64).transpose(0, 2, 1, 3).reshape(ZR, 1, 8, LANES)
    small = jnp.broadcast_to(small[None, None], (ZR, 1, 8, LANES))
    w_tiles = jnp.concatenate([wp_tiles, wo_tiles, small], axis=1)

    spread = exchange(split_columns(inputs[0], cotangent[0]), PAIR)
    spread = spread.reshape(Z, 16, 8, LANES)
    w_tiles = jnp.broadcast_to(w_tiles[None], (ZQ, ZR, n_w, 8, LANES)).reshape(Z, n_w, 8, LANES)
    arrived = exchange(jnp.concatenate([spread, w_tiles], axis=1), SEQ)
    mine = arrived[:, :16].reshape(Z, 2, 64, LANES).transpose(1, 0, 2, 3)
    packs = lax.all_gather(mine.reshape(1, 2, LENGTH, LANES), PAIR, axis=0, tiled=True)

    by_head = exchange(arrived[:, 16:].reshape(YC, 2, n_w, 8, LANES), PAIR)
    wp_part = by_head[:, :, :wp_high].reshape(YC, 2, high, 2, 8, LANES)
    wp_part = wp_part.transpose(0, 2, 4, 1, 3, 5).reshape(YC, PART_ROWS, 4 * HEAD_DIM)
    wo_part = by_head[:, :, wp_high].reshape(YC, 2, 8, high, 64).transpose(0, 3, 2, 1, 4)
    w_part = jnp.concatenate([wp_part, wo_part.reshape(YC, PART_ROWS, HEAD_DIM)], axis=2)
    w_all = jnp.broadcast_to(w_part[None], (X * ZR,) + w_part.shape)
    weights = exchange(w_all, SHARE).reshape(X, ZR, YC, PART_ROWS, HIDDEN)

    facts = by_head[:, :, n_w - 1].astype(F32)
    slots = facts[:, :, 0].astype(jnp.int32)
    tag_of = facts[:, :, 1]
    lens_all = facts[:, 0, 2, :12].reshape(YC, 2, 2, 3)
    lens_all = (lens_all[:, 0] * 256.0 + lens_all[:, 1]).astype(jnp.int32).reshape(Z, 3)
    pack_lens = lax.dynamic_index_in_dim(lens_all, z_here, 0, keepdims=False)
    ends = jnp.cumsum(pack_lens)

    info = jnp.concatenate([ends, core[None]]).astype(jnp.int32)
    slot_ids = jnp.arange(SLOTS, dtype=jnp.int32)
    placed = slots[:, :, None, :] == slot_ids[None, None, :, None]
    tags = jnp.sum(jnp.where(placed, tag_of[:, :, None, :], 0.0), axis=3)
    tags = tags.reshape(YC, 2, OWNERS, CAP).transpose(2, 1, 0, 3).reshape(OWNERS, 1, LANES)
    tags = jnp.broadcast_to(tags.astype(BF16), (OWNERS, 16, LANES))

    kept, sent, grads = heads_backward(info, packs, weights)

    shared = exchange(grads.reshape(X * YC * ZR, PART_ROWS, HIDDEN), SPREAD)
    shared = shared.reshape(X, YC, ZR, PART_ROWS, HIDDEN)

    got = lax.ppermute(sent, "c", [(0, 1), (1, 0)])
    own, *to_y = pair_sums(y_here[None].astype(jnp.int32), kept, got)
    came = [
        lax.ppermute(to_y[step - 1], "y", [(i, (i + step) % Y) for i in range(Y)])
        for step in range(1, Y)
    ]
    block = (y_here * C + core) * LANES
    dy_own = lax.dynamic_slice(packs, (0, 1, block, 0), (YC, 1, LANES, LANES))[:, 0]

    merged = exchange(payload(own, came, dy_own, shared), SEQ)
    w_grad = merged[:, 64:].astype(F32).reshape(ZQ, ZR, 3, PART_ROWS, LANES)
    w_grad = jnp.sum(w_grad, axis=0)
    grad_proj = w_grad[:, :2].transpose(0, 2, 1, 3).reshape(32, 2 * LANES)
    both_out = w_grad[:, 2].reshape(32, 2, 64)
    grad_out = lax.dynamic_index_in_dim(both_out, z_here & 1, 1, keepdims=False).T

    owned = exchange(place(slots.reshape(2 * YC, LANES), tags, merged), DP)
    return (grad_proj, grad_out, table_sum(owned).T)


def solution(mesh):
    fine = Mesh(mesh.devices.reshape(X, Y, C, ZQ, ZR), ALL)
    return jax.shard_map(
        per_device,
        mesh=fine,
        in_specs=(
            P(DP, None, SEQ, None),
            P(DP, None, SEQ, None),
            P(DP, None, None),
            P(DP, None, SEQ),
            P(),
            P(DP, SEQ),
            P(SEQ, DP),
        ),
        out_specs=(P(DP, SEQ), P(SEQ, DP), P(DP, SEQ)),
        check_vma=False,
    )
```

```python
import jax
import jax.numpy as jnp
from jax import lax
from jax.experimental import pallas as pl
from jax.experimental.pallas import tpu as pltpu
from jax.sharding import Mesh, PartitionSpec as P

HEAD_DIM = 128
NORM_FLOOR = 1.0
F32 = jnp.float32
BF16 = jnp.bfloat16

X, Y, C, ZQ, ZR = 4, 4, 2, 8, 2
YC = Y * C
Z = ZQ * ZR
PAIR = ("y", "c")
DP = ("x", "y", "c")
SEQ = ("zq", "zr")
SHARE = ("x", "zr")
SPREAD = ("x", "y", "c", "zr")
ALL = ("x", "y", "c", "zq", "zr")
OWNERS = X * YC
CAP = 8
ROWS = 256
SLOTS = OWNERS * CAP
LANES = 128
LENGTH = 1024
WIDTH = 1024
HIDDEN = 5 * HEAD_DIM
PART_ROWS = 32 // ZR
STEP = 256
REACH = 512
VMEM_SPEC = pl.BlockSpec(memory_space=pltpu.VMEM)
GRANT = 58
HBM_SPEC = pl.BlockSpec(memory_space=pltpu.HBM)
SMEM_SPEC = pl.BlockSpec(memory_space=pltpu.SMEM)


def exchange(value, axes):
    return lax.all_to_all(value, axes, split_axis=0, concat_axis=0, tiled=True)


def routing(item_ids, owner_row):
    rows = jnp.take(owner_row, item_ids.reshape(-1))
    owner = rows // ROWS
    count = owner.shape[0]
    order = jnp.arange(count, dtype=jnp.int32)
    before = (owner[None, :] == owner[:, None]) & (order[None, :] < order[:, None])
    rank = jnp.sum(before.astype(jnp.int32), axis=1)
    return owner * CAP + rank, rows % ROWS


def dot_nt(a, b):
    return lax.dot_general(a, b, (((1,), (1,)), ((), ())), preferred_element_type=F32)


def dot_tn(a, b):
    return lax.dot_general(a, b, (((0,), (0,)), ((), ())), preferred_element_type=F32)


def heads_kernel(
    info,
    packs,
    weights,
    kept,
    sent,
    grads,
    x_v,
    dy_v,
    w_v,
    acts,
    slope,
    d_value,
    d_key,
    d_z,
    gated,
    kept_v,
    sent_v,
    grads_v,
    sems,
    w_sems,
    out_sems,
):
    hd = HEAD_DIM
    scale = hd**-0.5
    u_cols, v_cols, q_cols, k_cols = (slice(m * hd, (m + 1) * hd) for m in range(4))
    steps = LENGTH // STEP
    copies = [
        pltpu.make_async_copy(
            packs.at[:, t, pl.ds(n * STEP, STEP)],
            held.at[:, pl.ds(n * STEP, STEP)],
            sems.at[t * steps + n],
        )
        for t, held in enumerate((x_v, dy_v))
        for n in range(steps)
    ]
    w_copies = [
        pltpu.make_async_copy(weights.at[x, r], w_v.at[x, :, r], w_sems.at[x * ZR + r])
        for x in range(X)
        for r in range(ZR)
    ]
    for copy in copies[:1] + w_copies + copies[1:]:
        copy.start()
    d_value[...] = jnp.zeros_like(d_value)
    d_key[...] = jnp.zeros_like(d_key)

    for copy in w_copies:
        copy.wait()
    wp = w_v[..., : 4 * hd].reshape(WIDTH, 4 * hd)
    wo = w_v[..., 4 * hd :].reshape(WIDTH, hd)

    for step in range(0, steps, 2):
        copies[step].wait()
        copies[step + 1].wait()
        rows = slice(step * STEP, (step + 2) * STEP)
        px = jnp.concatenate([x_v[g, rows, :] for g in range(8)], axis=1)
        z_pre = jnp.dot(px, wp, preferred_element_type=F32)
        sigma = jax.nn.sigmoid(z_pre)
        silu = z_pre * sigma
        acts[rows, :] = silu.astype(BF16)
        slope[rows, :] = sigma + silu * (1.0 - sigma)

    for step in range(steps):
        copies[steps + step].wait()
    for step in range(steps):
        base = step * STEP
        first = max(0, base - REACH)
        rows = slice(base, base + STEP)
        span = slice(first, base + STEP)
        pos_k = lax.broadcasted_iota(jnp.int32, (1, base + STEP - first), 1) + first
        pos_q = lax.broadcasted_iota(jnp.int32, (STEP, 1), 0) + base
        start = jnp.zeros_like(pos_q)
        for n in range(3):
            start = jnp.where(pos_q >= info[n], info[n], start)
        masked = (pos_k <= pos_q) & (pos_k >= start)
        query = acts[rows, q_cols]
        key = acts[span, k_cols]
        value = acts[span, v_cols]
        scores = dot_nt(query, key) * scale
        sigma = jnp.where(masked, jax.nn.sigmoid(scores), 0.0)
        silu = scores * sigma
        attn = silu.astype(BF16)
        factor = sigma + silu * (1.0 - sigma)
        mixed = jnp.dot(attn, value, preferred_element_type=F32)
        centred = mixed - jnp.mean(mixed, axis=-1, keepdims=True)
        inv_std = lax.rsqrt(jnp.mean(centred * centred, axis=-1, keepdims=True) + NORM_FLOOR)
        normed = centred * inv_std
        gating = acts[rows, u_cols].astype(F32)
        gated[rows, :] = (normed * gating).astype(BF16)
        pdy = jnp.concatenate([dy_v[g, rows, :] for g in range(8)], axis=1)
        d_gated = jnp.dot(pdy, wo, preferred_element_type=F32)
        d_normed = d_gated * gating
        d_mixed = (
            inv_std
            * (
                d_normed
                - jnp.mean(d_normed, axis=-1, keepdims=True)
                - normed * jnp.mean(d_normed * normed, axis=-1, keepdims=True)
            )
        ).astype(BF16)
        d_scores = (dot_nt(d_mixed, value) * factor).astype(BF16)
        d_query = jnp.dot(d_scores, key, preferred_element_type=F32)
        d_value[:, span] += jnp.dot(d_mixed.T, attn, preferred_element_type=F32)
        d_key[:, span] += jnp.dot(query.T, d_scores, preferred_element_type=F32)
        d_z[rows, u_cols] = (d_gated * normed * slope[rows, u_cols]).astype(BF16)
        d_z[rows, q_cols] = (d_query * (slope[rows, q_cols] * scale)).astype(BF16)

    d_z[:, v_cols] = (d_value[...].T * slope[:, v_cols]).astype(BF16)
    d_z[:, k_cols] = (d_key[...].T * (slope[:, k_cols] * scale)).astype(BF16)

    core = info[3]
    outs = []
    whole = dot_nt(d_z[...], wp).astype(BF16)
    for y in range(Y):
        part = whole[y * STEP : (y + 1) * STEP]

        @pl.when(core == 0)
        def _():
            kept_v[y] = part[:LANES]
            sent_v[y] = part[LANES:]

        @pl.when(core != 0)
        def _():
            kept_v[y] = part[LANES:]
            sent_v[y] = part[:LANES]

        for held, out in ((sent_v, sent), (kept_v, kept)):
            outs.append(pltpu.make_async_copy(held.at[y], out.at[y], out_sems.at[len(outs)]))
            outs[-1].start()

    for x in range(X):
        for dest, source, pack in ((slice(0, 512), d_z, x_v), (slice(512, 640), gated, dy_v)):
            columns = jnp.concatenate([pack[2 * x], pack[2 * x + 1]], axis=1)
            block = dot_tn(columns, source[...]).astype(BF16)
            grads_v[x, :, :, :, dest] = block.reshape(YC, ZR, PART_ROWS, block.shape[1])
        outs.append(pltpu.make_async_copy(grads_v.at[x], grads.at[x], out_sems.at[len(outs)]))
        outs[-1].start()
    for copy in outs:
        copy.wait()


def heads_backward(info, packs, weights):
    half = jax.ShapeDtypeStruct((Y, LANES, WIDTH), BF16)
    return pl.pallas_call(
        heads_kernel,
        out_shape=(
            half,
            half,
            jax.ShapeDtypeStruct((X, YC, ZR, PART_ROWS, HIDDEN), BF16),
        ),
        in_specs=[SMEM_SPEC, HBM_SPEC, pl.BlockSpec(memory_space=pl.ANY)],
        out_specs=(HBM_SPEC,) * 3,
        scratch_shapes=[
            pltpu.VMEM((8, LENGTH, LANES), BF16),
            pltpu.VMEM((8, LENGTH, LANES), BF16),
            pltpu.VMEM((X, YC, ZR, PART_ROWS, HIDDEN), BF16),
            pltpu.VMEM((LENGTH, 4 * HEAD_DIM), BF16),
            pltpu.VMEM((LENGTH, 4 * HEAD_DIM), F32),
            pltpu.VMEM((HEAD_DIM, LENGTH), F32),
            pltpu.VMEM((HEAD_DIM, LENGTH), F32),
            pltpu.VMEM((LENGTH, 4 * HEAD_DIM), BF16),
            pltpu.VMEM((LENGTH, HEAD_DIM), BF16),
            pltpu.VMEM((Y, LANES, WIDTH), BF16),
            pltpu.VMEM((Y, LANES, WIDTH), BF16),
            pltpu.VMEM((X, YC, ZR, PART_ROWS, HIDDEN), BF16),
            pltpu.SemaphoreType.DMA((2 * LENGTH // STEP,)),
            pltpu.SemaphoreType.DMA((X * ZR,)),
            pltpu.SemaphoreType.DMA((2 * Y + X,)),
        ],
        compiler_params=pltpu.CompilerParams(vmem_limit_bytes=GRANT * 2**20),
        cost_estimate=pl.CostEstimate(
            flops=5_000_000_000, bytes_accessed=9_000_000, transcendentals=2_000_000
        ),
        name="heads",
    )(info, packs, weights)


def pair_kernel(place, kept, got, own, to_1, to_2, to_3, own_v, sem):
    y = place[0]
    own_v[...] = (kept[y].astype(F32) + got[y].astype(F32)).astype(BF16)
    copy = pltpu.make_async_copy(own_v, own, sem)
    copy.start()
    for step, block in ((1, to_1), (2, to_2), (3, to_3)):
        other = (y + step) & (Y - 1)
        block[...] = (kept[other].astype(F32) + got[other].astype(F32)).astype(BF16)
    copy.wait()


def pair_sums(y, kept, got):
    block = jax.ShapeDtypeStruct((LANES, WIDTH), BF16)
    return pl.pallas_call(
        pair_kernel,
        out_shape=(block,) * Y,
        in_specs=[SMEM_SPEC, VMEM_SPEC, VMEM_SPEC],
        out_specs=(HBM_SPEC,) + (VMEM_SPEC,) * (Y - 1),
        scratch_shapes=[pltpu.VMEM((LANES, WIDTH), BF16), pltpu.SemaphoreType.DMA],
        compiler_params=pltpu.CompilerParams(vmem_limit_bytes=32 * 2**20),
        cost_estimate=pl.CostEstimate(flops=500_000, bytes_accessed=3_000_000, transcendentals=0),
        name="pair_sums",
    )(y, kept, got)


def payload_kernel(own, came_1, came_2, came_3, dy, out, own_v, sem):
    copy = pltpu.make_async_copy(own, own_v, sem)
    copy.start()
    copy.wait()
    lane = lax.broadcasted_iota(jnp.int32, (64, LANES), 1)
    for m in range(8):
        cols = slice(m * LANES, (m + 1) * LANES)
        total = own_v[:, cols].astype(F32) + dy[m].astype(F32)
        for came in (came_1, came_2, came_3):
            total = total + came[:, cols].astype(F32)
        low, high = total[:64], total[64:]
        even = jnp.where(lane < 64, low, pltpu.roll(high, 64, 1))
        odd = jnp.where(lane < 64, pltpu.roll(low, 64, 1), high)
        out[2 * m] = even.astype(BF16)
        out[2 * m + 1] = odd.astype(BF16)


def payload(own, came, dy):
    return pl.pallas_call(
        payload_kernel,
        out_shape=jax.ShapeDtypeStruct((Z, 64, LANES), BF16),
        in_specs=[HBM_SPEC] + [VMEM_SPEC] * 4,
        out_specs=VMEM_SPEC,
        scratch_shapes=[pltpu.VMEM((LANES, WIDTH), BF16), pltpu.SemaphoreType.DMA],
        compiler_params=pltpu.CompilerParams(vmem_limit_bytes=32 * 2**20),
        cost_estimate=pl.CostEstimate(flops=700_000, bytes_accessed=1_500_000, transcendentals=0),
        name="payload",
    )(own, *came, dy)


def weight_sum_kernel(shared, out):
    for h in range(YC):
        total = jnp.zeros((PART_ROWS, HIDDEN), F32)
        for x in range(X):
            for r in range(ZR):
                total = total + shared[x, h, r].astype(F32)
        for s in range(2):
            for n, col in enumerate((2 * s, 2 * s + 1, 4)):
                first = n * PART_ROWS
                out[h, s, first : first + PART_ROWS, :] = total[:, col * LANES : (col + 1) * LANES]


def weight_sum(shared):
    return pl.pallas_call(
        weight_sum_kernel,
        out_shape=jax.ShapeDtypeStruct((YC, 2, 3 * PART_ROWS, LANES), F32),
        in_specs=[VMEM_SPEC],
        out_specs=VMEM_SPEC,
        compiler_params=pltpu.CompilerParams(vmem_limit_bytes=32 * 2**20),
        cost_estimate=pl.CostEstimate(flops=700_000, bytes_accessed=1_700_000, transcendentals=0),
        name="weight_sum",
    )(shared)


def place_kernel(slots, tags, merged, out):
    slot_ids = lax.broadcasted_iota(jnp.int32, (SLOTS, LANES), 0)
    lane = lax.broadcasted_iota(jnp.int32, (SLOTS, LANES), 1)
    for pair in range(YC // 2):
        both = []
        for yc in (2 * pair, 2 * pair + 1):
            tokens = jnp.concatenate([merged[2 * yc], merged[2 * yc + 1]], axis=0)
            moved = [
                jnp.dot(
                    (slots[2 * yc + s : 2 * yc + s + 1, :] == slot_ids).astype(BF16),
                    tokens,
                    preferred_element_type=F32,
                )
                for s in range(2)
            ]
            rows = jnp.where(lane < 64, moved[0], moved[1])
            both.append(rows.reshape(OWNERS, CAP, LANES))
        out[:, pair * 16 : (pair + 1) * 16, :] = jnp.concatenate(both, axis=1).astype(BF16)
    out[:, YC * CAP :, :] = tags[...]


def place(slots, tags, merged):
    return pl.pallas_call(
        place_kernel,
        out_shape=jax.ShapeDtypeStruct((OWNERS, YC * CAP + 16, LANES), BF16),
        in_specs=[VMEM_SPEC] * 3,
        out_specs=VMEM_SPEC,
        compiler_params=pltpu.CompilerParams(vmem_limit_bytes=32 * 2**20),
        cost_estimate=pl.CostEstimate(
            flops=135_000_000, bytes_accessed=1_000_000, transcendentals=0
        ),
        name="place",
    )(slots, tags, merged)


def table_kernel(owned, out):
    count = YC * CAP
    row_ids = lax.broadcasted_iota(jnp.int32, (ROWS, LANES), 0).astype(F32)
    left = lax.broadcasted_iota(jnp.int32, (count, LANES), 1) < 64
    total = jnp.zeros((ROWS, LANES), F32)
    for pair in range(OWNERS // 2):
        select, rows = [], []
        for source in (2 * pair, 2 * pair + 1):
            tag = owned[source, count:, :].astype(F32)[:1]
            select.append((tag == row_ids).astype(BF16))
            here = owned[source, :count, :].astype(F32)
            rows.append(jnp.where(left, here, 0.0).astype(BF16))
            rows.append(jnp.where(left, 0.0, here).astype(BF16))
        total = total + jnp.dot(
            jnp.concatenate(select, axis=1),
            jnp.concatenate(rows, axis=0),
            preferred_element_type=F32,
        )
    out[...] = (total + pltpu.roll(total, 64, 1)).T[:64]


def table_sum(owned):
    return pl.pallas_call(
        table_kernel,
        out_shape=jax.ShapeDtypeStruct((64, ROWS), F32),
        in_specs=[VMEM_SPEC],
        out_specs=VMEM_SPEC,
        compiler_params=pltpu.CompilerParams(vmem_limit_bytes=32 * 2**20),
        cost_estimate=pl.CostEstimate(
            flops=270_000_000, bytes_accessed=1_000_000, transcendentals=0
        ),
        name="table_sum",
    )(owned)


def split_kernel(inputs, cotangent, out, sems):
    copies = [
        pltpu.make_async_copy(
            source.at[:, :, pl.ds(g * LANES, LANES)], out.at[g, :, t], sems.at[2 * g + t]
        )
        for g in range(8)
        for t, source in enumerate((inputs, cotangent))
    ]
    for copy in copies:
        copy.start()
    for copy in copies:
        copy.wait()


def split_columns(inputs, cotangent):
    return pl.pallas_call(
        split_kernel,
        out_shape=jax.ShapeDtypeStruct((8, 2, 2, 64, LANES), BF16),
        in_specs=[HBM_SPEC] * 2,
        out_specs=VMEM_SPEC,
        scratch_shapes=[pltpu.SemaphoreType.DMA((16,))],
        compiler_params=pltpu.CompilerParams(vmem_limit_bytes=60 * 2**20),
        cost_estimate=pl.CostEstimate(flops=0, bytes_accessed=1_000_000, transcendentals=0),
        name="split_columns",
    )(inputs, cotangent)


def per_device(inputs, cotangent, lengths, item_ids, owner_row, w_project, w_output):
    core = lax.axis_index("c")
    y_here = lax.axis_index("y")
    z_here = lax.axis_index(SEQ)
    lane = jnp.arange(LANES, dtype=jnp.int32)

    slot, local_row = routing(item_ids, owner_row)
    lens = lengths.reshape(-1)
    lens_row = jnp.concatenate([lens // 256, lens % 256])
    lens_row = jnp.pad(lens_row, (0, LANES - lens_row.shape[0]))
    small = jnp.pad(jnp.stack([slot, local_row, lens_row]), ((0, 5), (0, 0))).astype(BF16)
    high = PART_ROWS // 8
    wp_high = 2 * high
    n_w = wp_high + 2
    wp_tiles = w_project.reshape(ZR, high, 8, 2, LANES).transpose(0, 1, 3, 2, 4)
    wp_tiles = wp_tiles.reshape(ZR, wp_high, 8, LANES)
    wo_tiles = w_output.T.reshape(ZR, high, 8, 64).transpose(0, 2, 1, 3).reshape(ZR, 1, 8, LANES)
    small = jnp.broadcast_to(small[None, None], (ZR, 1, 8, LANES))
    w_tiles = jnp.concatenate([wp_tiles, wo_tiles, small], axis=1)

    spread = exchange(split_columns(inputs[0], cotangent[0]), PAIR)
    spread = spread.reshape(Z, 16, 8, LANES)
    w_tiles = jnp.broadcast_to(w_tiles[None], (ZQ, ZR, n_w, 8, LANES)).reshape(Z, n_w, 8, LANES)
    arrived = exchange(jnp.concatenate([spread, w_tiles], axis=1), SEQ)
    mine = arrived[:, :16].reshape(Z, 2, 64, LANES).transpose(1, 0, 2, 3)
    packs = lax.all_gather(mine.reshape(1, 2, LENGTH, LANES), PAIR, axis=0, tiled=True)

    by_head = exchange(arrived[:, 16:].reshape(YC, 2, n_w, 8, LANES), PAIR)
    wp_part = by_head[:, :, :wp_high].reshape(YC, 2, high, 2, 8, LANES)
    wp_part = wp_part.transpose(0, 2, 4, 1, 3, 5).reshape(YC, PART_ROWS, 4 * HEAD_DIM)
    wo_part = by_head[:, :, wp_high].reshape(YC, 2, 8, high, 64).transpose(0, 3, 2, 1, 4)
    w_part = jnp.concatenate([wp_part, wo_part.reshape(YC, PART_ROWS, HEAD_DIM)], axis=2)
    w_all = jnp.broadcast_to(w_part[None], (X * ZR,) + w_part.shape)
    weights = exchange(w_all, SHARE).reshape(X, ZR, YC, PART_ROWS, HIDDEN)

    facts = by_head[:, :, n_w - 1].astype(F32)
    slots = facts[:, :, 0].astype(jnp.int32)
    tag_of = facts[:, :, 1]
    lens_all = facts[:, 0, 2, :12].reshape(YC, 2, 2, 3)
    lens_all = (lens_all[:, 0] * 256.0 + lens_all[:, 1]).astype(jnp.int32).reshape(Z, 3)
    pack_lens = lax.dynamic_index_in_dim(lens_all, z_here, 0, keepdims=False)
    ends = jnp.cumsum(pack_lens)

    info = jnp.concatenate([ends, core[None]]).astype(jnp.int32)
    slot_ids = jnp.arange(SLOTS, dtype=jnp.int32)
    placed = slots[:, :, None, :] == slot_ids[None, None, :, None]
    tags = jnp.sum(jnp.where(placed, tag_of[:, :, None, :], 0.0), axis=3)
    tags = tags.reshape(YC, 2, OWNERS, CAP).transpose(2, 1, 0, 3).reshape(OWNERS, 1, LANES)
    tags = jnp.broadcast_to(tags.astype(BF16), (OWNERS, 16, LANES))

    kept, sent, grads = heads_backward(info, packs, weights)

    shared = exchange(grads.reshape(X * YC * ZR, PART_ROWS, HIDDEN), SPREAD)
    shared = shared.reshape(X, YC, ZR, PART_ROWS, HIDDEN)

    got = lax.ppermute(sent, "c", [(0, 1), (1, 0)])
    own, *to_y = pair_sums(y_here[None].astype(jnp.int32), kept, got)
    came = [
        lax.ppermute(to_y[step - 1], "y", [(i, (i + step) % Y) for i in range(Y)])
        for step in range(1, Y)
    ]
    block = (y_here * C + core) * LANES
    dy_own = lax.dynamic_slice(packs, (0, 1, block, 0), (YC, 1, LANES, LANES))[:, 0]

    merged = exchange(payload(own, came, dy_own), SEQ)

    low = lax.axis_index("zr")
    rest = lax.psum_scatter(weight_sum(shared), "zq", scatter_dimension=0, tiled=True)[0]
    mine = lax.dynamic_index_in_dim(rest, low, 0, keepdims=False)
    other = lax.dynamic_index_in_dim(rest, 1 - low, 0, keepdims=False)
    other = lax.ppermute(other, "zr", [(0, 1), (1, 0)])
    w_grad = jnp.where(low == 0, jnp.stack([mine, other]), jnp.stack([other, mine]))
    w_grad = w_grad.reshape(ZR, 3, PART_ROWS, LANES)
    grad_proj = w_grad[:, :2].transpose(0, 2, 1, 3).reshape(32, 2 * LANES)
    both_out = w_grad[:, 2].reshape(32, 2, 64)
    grad_out = lax.dynamic_index_in_dim(both_out, z_here & 1, 1, keepdims=False).T

    owned = exchange(place(slots.reshape(2 * YC, LANES), tags, merged), DP)
    return (grad_proj, grad_out, table_sum(owned).T)


def solution(mesh):
    fine = Mesh(mesh.devices.reshape(X, Y, C, ZQ, ZR), ALL)
    return jax.shard_map(
        per_device,
        mesh=fine,
        in_specs=(
            P(DP, None, SEQ, None),
            P(DP, None, SEQ, None),
            P(DP, None, None),
            P(DP, None, SEQ),
            P(),
            P(DP, SEQ),
            P(SEQ, DP),
        ),
        out_specs=(P(DP, SEQ), P(SEQ, DP), P(DP, SEQ)),
        check_vma=False,
    )
```

```python
import jax
import jax.numpy as jnp
from jax import lax
from jax.experimental import pallas as pl
from jax.experimental.pallas import tpu as pltpu
from jax.sharding import Mesh, PartitionSpec as P

HEAD_DIM = 128
NORM_FLOOR = 1.0
F32 = jnp.float32
BF16 = jnp.bfloat16

X, Y, C, ZQ, ZR = 4, 4, 2, 8, 2
YC = Y * C
Z = ZQ * ZR
PAIR = ("y", "c")
DP = ("x", "y", "c")
SEQ = ("zq", "zr")
SHARE = ("x", "zr")
SPREAD = ("x", "y", "c", "zr")
ALL = ("x", "y", "c", "zq", "zr")
OWNERS = X * YC
CAP = 8
ROWS = 256
SLOTS = OWNERS * CAP
LANES = 128
LENGTH = 1024
WIDTH = 1024
HIDDEN = 5 * HEAD_DIM
PART_ROWS = 32 // ZR
STEP = 256
REACH = 512
VMEM_SPEC = pl.BlockSpec(memory_space=pltpu.VMEM)
GRANT = 58
HBM_SPEC = pl.BlockSpec(memory_space=pltpu.HBM)
SMEM_SPEC = pl.BlockSpec(memory_space=pltpu.SMEM)


def exchange(value, axes):
    return lax.all_to_all(value, axes, split_axis=0, concat_axis=0, tiled=True)


def routing(item_ids, owner_row):
    rows = jnp.take(owner_row, item_ids.reshape(-1))
    owner = rows // ROWS
    count = owner.shape[0]
    order = jnp.arange(count, dtype=jnp.int32)
    before = (owner[None, :] == owner[:, None]) & (order[None, :] < order[:, None])
    rank = jnp.sum(before.astype(jnp.int32), axis=1)
    return owner * CAP + rank, rows % ROWS


def dot_nt(a, b):
    return lax.dot_general(a, b, (((1,), (1,)), ((), ())), preferred_element_type=F32)


def dot_tn(a, b):
    return lax.dot_general(a, b, (((0,), (0,)), ((), ())), preferred_element_type=F32)


def heads_kernel(
    info,
    packs,
    weights,
    kept,
    sent,
    grads,
    x_v,
    dy_v,
    w_v,
    acts,
    slope,
    d_value,
    d_key,
    d_z,
    gated,
    kept_v,
    sent_v,
    grads_v,
    sems,
    w_sems,
    out_sems,
):
    hd = HEAD_DIM
    scale = hd**-0.5
    u_cols, v_cols, q_cols, k_cols = (slice(m * hd, (m + 1) * hd) for m in range(4))
    steps = LENGTH // STEP
    copies = [
        pltpu.make_async_copy(
            packs.at[:, t, pl.ds(n * STEP, STEP)],
            held.at[:, pl.ds(n * STEP, STEP)],
            sems.at[t * steps + n],
        )
        for t, held in enumerate((x_v, dy_v))
        for n in range(steps)
    ]
    w_copies = [
        pltpu.make_async_copy(weights.at[x, r], w_v.at[x, :, r], w_sems.at[x * ZR + r])
        for x in range(X)
        for r in range(ZR)
    ]
    for copy in copies[:1] + w_copies + copies[1:]:
        copy.start()
    d_value[...] = jnp.zeros_like(d_value)
    d_key[...] = jnp.zeros_like(d_key)

    for copy in w_copies:
        copy.wait()
    wp = w_v[..., : 4 * hd].reshape(WIDTH, 4 * hd)
    wo = w_v[..., 4 * hd :].reshape(WIDTH, hd)

    for step in range(0, steps, 2):
        copies[step].wait()
        copies[step + 1].wait()
        rows = slice(step * STEP, (step + 2) * STEP)
        px = jnp.concatenate([x_v[g, rows, :] for g in range(8)], axis=1)
        z_pre = jnp.dot(px, wp, preferred_element_type=F32)
        sigma = jax.nn.sigmoid(z_pre)
        silu = z_pre * sigma
        acts[rows, :] = silu.astype(BF16)
        slope[rows, :] = sigma + silu * (1.0 - sigma)

    for step in range(steps):
        copies[steps + step].wait()
    for step in range(steps):
        base = step * STEP
        first = max(0, base - REACH)
        rows = slice(base, base + STEP)
        span = slice(first, base + STEP)
        pos_k = lax.broadcasted_iota(jnp.int32, (1, base + STEP - first), 1) + first
        pos_q = lax.broadcasted_iota(jnp.int32, (STEP, 1), 0) + base
        start = jnp.zeros_like(pos_q)
        for n in range(3):
            start = jnp.where(pos_q >= info[n], info[n], start)
        masked = (pos_k <= pos_q) & (pos_k >= start)
        query = acts[rows, q_cols]
        key = acts[span, k_cols]
        value = acts[span, v_cols]
        scores = dot_nt(query, key) * scale
        sigma = jnp.where(masked, jax.nn.sigmoid(scores), 0.0)
        silu = scores * sigma
        attn = silu.astype(BF16)
        factor = sigma + silu * (1.0 - sigma)
        mixed = jnp.dot(attn, value, preferred_element_type=F32)
        centred = mixed - jnp.mean(mixed, axis=-1, keepdims=True)
        inv_std = lax.rsqrt(jnp.mean(centred * centred, axis=-1, keepdims=True) + NORM_FLOOR)
        normed = centred * inv_std
        gating = acts[rows, u_cols].astype(F32)
        gated[rows, :] = (normed * gating).astype(BF16)
        pdy = jnp.concatenate([dy_v[g, rows, :] for g in range(8)], axis=1)
        d_gated = jnp.dot(pdy, wo, preferred_element_type=F32)
        d_normed = d_gated * gating
        d_mixed = (
            inv_std
            * (
                d_normed
                - jnp.mean(d_normed, axis=-1, keepdims=True)
                - normed * jnp.mean(d_normed * normed, axis=-1, keepdims=True)
            )
        ).astype(BF16)
        d_scores = (dot_nt(d_mixed, value) * factor).astype(BF16)
        d_query = jnp.dot(d_scores, key, preferred_element_type=F32)
        d_value[:, span] += jnp.dot(d_mixed.T, attn, preferred_element_type=F32)
        d_key[:, span] += jnp.dot(query.T, d_scores, preferred_element_type=F32)
        d_z[rows, u_cols] = (d_gated * normed * slope[rows, u_cols]).astype(BF16)
        d_z[rows, q_cols] = (d_query * (slope[rows, q_cols] * scale)).astype(BF16)

    d_z[:, v_cols] = (d_value[...].T * slope[:, v_cols]).astype(BF16)
    d_z[:, k_cols] = (d_key[...].T * (slope[:, k_cols] * scale)).astype(BF16)

    core = info[3]
    outs = []
    whole = dot_nt(d_z[...], wp).astype(BF16)
    for y in range(Y):
        part = whole[y * STEP : (y + 1) * STEP]

        @pl.when(core == 0)
        def _():
            kept_v[y] = part[:LANES]
            sent_v[y] = part[LANES:]

        @pl.when(core != 0)
        def _():
            kept_v[y] = part[LANES:]
            sent_v[y] = part[:LANES]

        for held, out in ((sent_v, sent), (kept_v, kept)):
            outs.append(pltpu.make_async_copy(held.at[y], out.at[y], out_sems.at[len(outs)]))
            outs[-1].start()

    for x in range(X):
        for dest, source, pack in ((slice(0, 512), d_z, x_v), (slice(512, 640), gated, dy_v)):
            columns = jnp.concatenate([pack[2 * x], pack[2 * x + 1]], axis=1)
            block = dot_tn(columns, source[...]).astype(BF16)
            grads_v[x, :, :, :, dest] = block.reshape(YC, ZR, PART_ROWS, block.shape[1])
        outs.append(pltpu.make_async_copy(grads_v.at[x], grads.at[x], out_sems.at[len(outs)]))
        outs[-1].start()
    for copy in outs:
        copy.wait()


def heads_backward(info, packs, weights):
    half = jax.ShapeDtypeStruct((Y, LANES, WIDTH), BF16)
    return pl.pallas_call(
        heads_kernel,
        out_shape=(
            half,
            half,
            jax.ShapeDtypeStruct((X, YC, ZR, PART_ROWS, HIDDEN), BF16),
        ),
        in_specs=[SMEM_SPEC, HBM_SPEC, pl.BlockSpec(memory_space=pl.ANY)],
        out_specs=(HBM_SPEC,) * 3,
        scratch_shapes=[
            pltpu.VMEM((8, LENGTH, LANES), BF16),
            pltpu.VMEM((8, LENGTH, LANES), BF16),
            pltpu.VMEM((X, YC, ZR, PART_ROWS, HIDDEN), BF16),
            pltpu.VMEM((LENGTH, 4 * HEAD_DIM), BF16),
            pltpu.VMEM((LENGTH, 4 * HEAD_DIM), F32),
            pltpu.VMEM((HEAD_DIM, LENGTH), F32),
            pltpu.VMEM((HEAD_DIM, LENGTH), F32),
            pltpu.VMEM((LENGTH, 4 * HEAD_DIM), BF16),
            pltpu.VMEM((LENGTH, HEAD_DIM), BF16),
            pltpu.VMEM((Y, LANES, WIDTH), BF16),
            pltpu.VMEM((Y, LANES, WIDTH), BF16),
            pltpu.VMEM((X, YC, ZR, PART_ROWS, HIDDEN), BF16),
            pltpu.SemaphoreType.DMA((2 * LENGTH // STEP,)),
            pltpu.SemaphoreType.DMA((X * ZR,)),
            pltpu.SemaphoreType.DMA((2 * Y + X,)),
        ],
        compiler_params=pltpu.CompilerParams(vmem_limit_bytes=GRANT * 2**20),
        cost_estimate=pl.CostEstimate(
            flops=5_000_000_000, bytes_accessed=9_000_000, transcendentals=2_000_000
        ),
        name="heads",
    )(info, packs, weights)


def pair_kernel(place, kept, got, own, to_1, to_2, to_3, own_v, sem):
    y = place[0]
    own_v[...] = (kept[y].astype(F32) + got[y].astype(F32)).astype(BF16)
    copy = pltpu.make_async_copy(own_v, own, sem)
    copy.start()
    for step, block in ((1, to_1), (2, to_2), (3, to_3)):
        other = (y + step) & (Y - 1)
        block[...] = (kept[other].astype(F32) + got[other].astype(F32)).astype(BF16)
    copy.wait()


def pair_sums(y, kept, got):
    block = jax.ShapeDtypeStruct((LANES, WIDTH), BF16)
    return pl.pallas_call(
        pair_kernel,
        out_shape=(block,) * Y,
        in_specs=[SMEM_SPEC, VMEM_SPEC, VMEM_SPEC],
        out_specs=(HBM_SPEC,) + (VMEM_SPEC,) * (Y - 1),
        scratch_shapes=[pltpu.VMEM((LANES, WIDTH), BF16), pltpu.SemaphoreType.DMA],
        compiler_params=pltpu.CompilerParams(vmem_limit_bytes=32 * 2**20),
        cost_estimate=pl.CostEstimate(flops=500_000, bytes_accessed=3_000_000, transcendentals=0),
        name="pair_sums",
    )(y, kept, got)


def payload_kernel(own, came_1, came_2, came_3, dy, out, own_v, sem):
    copy = pltpu.make_async_copy(own, own_v, sem)
    copy.start()
    copy.wait()
    lane = lax.broadcasted_iota(jnp.int32, (64, LANES), 1)
    for m in range(8):
        cols = slice(m * LANES, (m + 1) * LANES)
        total = own_v[:, cols].astype(F32) + dy[m].astype(F32)
        for came in (came_1, came_2, came_3):
            total = total + came[:, cols].astype(F32)
        low, high = total[:64], total[64:]
        even = jnp.where(lane < 64, low, pltpu.roll(high, 64, 1))
        odd = jnp.where(lane < 64, pltpu.roll(low, 64, 1), high)
        out[2 * m] = even.astype(BF16)
        out[2 * m + 1] = odd.astype(BF16)


def payload(own, came, dy):
    return pl.pallas_call(
        payload_kernel,
        out_shape=jax.ShapeDtypeStruct((Z, 64, LANES), BF16),
        in_specs=[HBM_SPEC] + [VMEM_SPEC] * 4,
        out_specs=VMEM_SPEC,
        scratch_shapes=[pltpu.VMEM((LANES, WIDTH), BF16), pltpu.SemaphoreType.DMA],
        compiler_params=pltpu.CompilerParams(vmem_limit_bytes=32 * 2**20),
        cost_estimate=pl.CostEstimate(flops=700_000, bytes_accessed=1_500_000, transcendentals=0),
        name="payload",
    )(own, *came, dy)


def weight_sum_kernel(shared, out):
    out[..., LANES:] = jnp.zeros((YC, 2, 3 * PART_ROWS, LANES), F32)
    for h in range(YC):
        total = jnp.zeros((PART_ROWS, HIDDEN), F32)
        for x in range(X):
            for r in range(ZR):
                total = total + shared[x, h, r].astype(F32)
        for s in range(2):
            for n, col in enumerate((2 * s, 2 * s + 1, 4)):
                first = n * PART_ROWS
                block = total[:, col * LANES : (col + 1) * LANES]
                out[h, s, first : first + PART_ROWS, :LANES] = block


def weight_sum(shared):
    return pl.pallas_call(
        weight_sum_kernel,
        out_shape=jax.ShapeDtypeStruct((YC, 2, 3 * PART_ROWS, 2 * LANES), F32),
        in_specs=[VMEM_SPEC],
        out_specs=VMEM_SPEC,
        compiler_params=pltpu.CompilerParams(vmem_limit_bytes=32 * 2**20),
        cost_estimate=pl.CostEstimate(flops=700_000, bytes_accessed=1_700_000, transcendentals=0),
        name="weight_sum",
    )(shared)


def place_kernel(slots, tags, merged, out):
    slot_ids = lax.broadcasted_iota(jnp.int32, (SLOTS, LANES), 0)
    lane = lax.broadcasted_iota(jnp.int32, (SLOTS, LANES), 1)
    for pair in range(YC // 2):
        both = []
        for yc in (2 * pair, 2 * pair + 1):
            tokens = jnp.concatenate([merged[2 * yc], merged[2 * yc + 1]], axis=0)
            moved = [
                jnp.dot(
                    (slots[2 * yc + s : 2 * yc + s + 1, :] == slot_ids).astype(BF16),
                    tokens,
                    preferred_element_type=F32,
                )
                for s in range(2)
            ]
            rows = jnp.where(lane < 64, moved[0], moved[1])
            both.append(rows.reshape(OWNERS, CAP, LANES))
        out[:, pair * 16 : (pair + 1) * 16, :] = jnp.concatenate(both, axis=1).astype(BF16)
    out[:, YC * CAP :, :] = tags[...]


def place(slots, tags, merged):
    return pl.pallas_call(
        place_kernel,
        out_shape=jax.ShapeDtypeStruct((OWNERS, YC * CAP + 16, LANES), BF16),
        in_specs=[VMEM_SPEC] * 3,
        out_specs=VMEM_SPEC,
        compiler_params=pltpu.CompilerParams(vmem_limit_bytes=32 * 2**20),
        cost_estimate=pl.CostEstimate(
            flops=135_000_000, bytes_accessed=1_000_000, transcendentals=0
        ),
        name="place",
    )(slots, tags, merged)


def table_kernel(owned, out):
    count = YC * CAP
    row_ids = lax.broadcasted_iota(jnp.int32, (ROWS, LANES), 0).astype(F32)
    left = lax.broadcasted_iota(jnp.int32, (count, LANES), 1) < 64
    total = jnp.zeros((ROWS, LANES), F32)
    for pair in range(OWNERS // 2):
        select, rows = [], []
        for source in (2 * pair, 2 * pair + 1):
            tag = owned[source, count:, :].astype(F32)[:1]
            select.append((tag == row_ids).astype(BF16))
            here = owned[source, :count, :].astype(F32)
            rows.append(jnp.where(left, here, 0.0).astype(BF16))
            rows.append(jnp.where(left, 0.0, here).astype(BF16))
        total = total + jnp.dot(
            jnp.concatenate(select, axis=1),
            jnp.concatenate(rows, axis=0),
            preferred_element_type=F32,
        )
    out[...] = (total + pltpu.roll(total, 64, 1)).T[:64]


def table_sum(owned):
    return pl.pallas_call(
        table_kernel,
        out_shape=jax.ShapeDtypeStruct((64, ROWS), F32),
        in_specs=[VMEM_SPEC],
        out_specs=VMEM_SPEC,
        compiler_params=pltpu.CompilerParams(vmem_limit_bytes=32 * 2**20),
        cost_estimate=pl.CostEstimate(
            flops=270_000_000, bytes_accessed=1_000_000, transcendentals=0
        ),
        name="table_sum",
    )(owned)


def split_kernel(inputs, cotangent, out, sems):
    copies = [
        pltpu.make_async_copy(
            source.at[:, :, pl.ds(g * LANES, LANES)], out.at[g, :, t], sems.at[2 * g + t]
        )
        for g in range(8)
        for t, source in enumerate((inputs, cotangent))
    ]
    for copy in copies:
        copy.start()
    for copy in copies:
        copy.wait()


def split_columns(inputs, cotangent):
    return pl.pallas_call(
        split_kernel,
        out_shape=jax.ShapeDtypeStruct((8, 2, 2, 64, LANES), BF16),
        in_specs=[HBM_SPEC] * 2,
        out_specs=VMEM_SPEC,
        scratch_shapes=[pltpu.SemaphoreType.DMA((16,))],
        compiler_params=pltpu.CompilerParams(vmem_limit_bytes=60 * 2**20),
        cost_estimate=pl.CostEstimate(flops=0, bytes_accessed=1_000_000, transcendentals=0),
        name="split_columns",
    )(inputs, cotangent)


def per_device(inputs, cotangent, lengths, item_ids, owner_row, w_project, w_output):
    core = lax.axis_index("c")
    y_here = lax.axis_index("y")
    z_here = lax.axis_index(SEQ)
    lane = jnp.arange(LANES, dtype=jnp.int32)

    slot, local_row = routing(item_ids, owner_row)
    lens = lengths.reshape(-1)
    lens_row = jnp.concatenate([lens // 256, lens % 256])
    lens_row = jnp.pad(lens_row, (0, LANES - lens_row.shape[0]))
    small = jnp.pad(jnp.stack([slot, local_row, lens_row]), ((0, 5), (0, 0))).astype(BF16)
    high = PART_ROWS // 8
    wp_high = 2 * high
    n_w = wp_high + 2
    wp_tiles = w_project.reshape(ZR, high, 8, 2, LANES).transpose(0, 1, 3, 2, 4)
    wp_tiles = wp_tiles.reshape(ZR, wp_high, 8, LANES)
    wo_tiles = w_output.T.reshape(ZR, high, 8, 64).transpose(0, 2, 1, 3).reshape(ZR, 1, 8, LANES)
    small = jnp.broadcast_to(small[None, None], (ZR, 1, 8, LANES))
    w_tiles = jnp.concatenate([wp_tiles, wo_tiles, small], axis=1)

    spread = exchange(split_columns(inputs[0], cotangent[0]), PAIR)
    spread = spread.reshape(Z, 16, 8, LANES)
    w_tiles = jnp.broadcast_to(w_tiles[None], (ZQ, ZR, n_w, 8, LANES)).reshape(Z, n_w, 8, LANES)
    arrived = exchange(jnp.concatenate([spread, w_tiles], axis=1), SEQ)
    mine = arrived[:, :16].reshape(Z, 2, 64, LANES).transpose(1, 0, 2, 3)
    packs = lax.all_gather(mine.reshape(1, 2, LENGTH, LANES), PAIR, axis=0, tiled=True)

    by_head = exchange(arrived[:, 16:].reshape(YC, 2, n_w, 8, LANES), PAIR)
    wp_part = by_head[:, :, :wp_high].reshape(YC, 2, high, 2, 8, LANES)
    wp_part = wp_part.transpose(0, 2, 4, 1, 3, 5).reshape(YC, PART_ROWS, 4 * HEAD_DIM)
    wo_part = by_head[:, :, wp_high].reshape(YC, 2, 8, high, 64).transpose(0, 3, 2, 1, 4)
    w_part = jnp.concatenate([wp_part, wo_part.reshape(YC, PART_ROWS, HEAD_DIM)], axis=2)
    w_all = jnp.broadcast_to(w_part[None], (X * ZR,) + w_part.shape)
    weights = exchange(w_all, SHARE).reshape(X, ZR, YC, PART_ROWS, HIDDEN)

    facts = by_head[:, :, n_w - 1].astype(F32)
    slots = facts[:, :, 0].astype(jnp.int32)
    tag_of = facts[:, :, 1]
    lens_all = facts[:, 0, 2, :12].reshape(YC, 2, 2, 3)
    lens_all = (lens_all[:, 0] * 256.0 + lens_all[:, 1]).astype(jnp.int32).reshape(Z, 3)
    pack_lens = lax.dynamic_index_in_dim(lens_all, z_here, 0, keepdims=False)
    ends = jnp.cumsum(pack_lens)

    info = jnp.concatenate([ends, core[None]]).astype(jnp.int32)
    slot_ids = jnp.arange(SLOTS, dtype=jnp.int32)
    placed = slots[:, :, None, :] == slot_ids[None, None, :, None]
    tags = jnp.sum(jnp.where(placed, tag_of[:, :, None, :], 0.0), axis=3)
    tags = tags.reshape(YC, 2, OWNERS, CAP).transpose(2, 1, 0, 3).reshape(OWNERS, 1, LANES)
    tags = jnp.broadcast_to(tags.astype(BF16), (OWNERS, 16, LANES))

    kept, sent, grads = heads_backward(info, packs, weights)

    shared = exchange(grads.reshape(X * YC * ZR, PART_ROWS, HIDDEN), SPREAD)
    shared = shared.reshape(X, YC, ZR, PART_ROWS, HIDDEN)

    got = lax.ppermute(sent, "c", [(0, 1), (1, 0)])
    own, *to_y = pair_sums(y_here[None].astype(jnp.int32), kept, got)
    came = [
        lax.ppermute(to_y[step - 1], "y", [(i, (i + step) % Y) for i in range(Y)])
        for step in range(1, Y)
    ]
    block = (y_here * C + core) * LANES
    dy_own = lax.dynamic_slice(packs, (0, 1, block, 0), (YC, 1, LANES, LANES))[:, 0]

    w_sum, came[0] = lax.optimization_barrier((weight_sum(shared), came[0]))
    merged = exchange(payload(own, came, dy_own), SEQ)

    low = lax.axis_index("zr")
    rest = lax.psum_scatter(w_sum, "zq", scatter_dimension=0, tiled=True)
    rest = rest[0, :, :, :LANES]
    mine = lax.dynamic_index_in_dim(rest, low, 0, keepdims=False)
    other = lax.dynamic_index_in_dim(rest, 1 - low, 0, keepdims=False)
    other = lax.ppermute(other, "zr", [(0, 1), (1, 0)])
    w_grad = jnp.where(low == 0, jnp.stack([mine, other]), jnp.stack([other, mine]))
    w_grad = w_grad.reshape(ZR, 3, PART_ROWS, LANES)
    grad_proj = w_grad[:, :2].transpose(0, 2, 1, 3).reshape(32, 2 * LANES)
    both_out = w_grad[:, 2].reshape(32, 2, 64)
    grad_out = lax.dynamic_index_in_dim(both_out, z_here & 1, 1, keepdims=False).T

    owned = exchange(place(slots.reshape(2 * YC, LANES), tags, merged), DP)
    return (grad_proj, grad_out, table_sum(owned).T)


def solution(mesh):
    fine = Mesh(mesh.devices.reshape(X, Y, C, ZQ, ZR), ALL)
    return jax.shard_map(
        per_device,
        mesh=fine,
        in_specs=(
            P(DP, None, SEQ, None),
            P(DP, None, SEQ, None),
            P(DP, None, None),
            P(DP, None, SEQ),
            P(),
            P(DP, SEQ),
            P(SEQ, DP),
        ),
        out_specs=(P(DP, SEQ), P(SEQ, DP), P(DP, SEQ)),
        check_vma=False,
    )
```

```python
import jax
import jax.numpy as jnp
from jax import lax
from jax.experimental import pallas as pl
from jax.experimental.pallas import tpu as pltpu
from jax.sharding import Mesh, PartitionSpec as P

HEAD_DIM = 128
NORM_FLOOR = 1.0
F32 = jnp.float32
BF16 = jnp.bfloat16

X, Y, C, ZQ, ZR = 4, 4, 2, 8, 2
YC = Y * C
Z = ZQ * ZR
PAIR = ("y", "c")
DP = ("x", "y", "c")
SEQ = ("zq", "zr")
SHARE = ("x", "zr")
SPREAD = ("x", "y", "c", "zr")
ALL = ("x", "y", "c", "zq", "zr")
OWNERS = X * YC
CAP = 8
ROWS = 256
SLOTS = OWNERS * CAP
LANES = 128
LENGTH = 1024
WIDTH = 1024
HIDDEN = 5 * HEAD_DIM
PART_ROWS = 32 // ZR
STEP = 256
REACH = 512
VMEM_SPEC = pl.BlockSpec(memory_space=pltpu.VMEM)
GRANT = 58
HBM_SPEC = pl.BlockSpec(memory_space=pltpu.HBM)
SMEM_SPEC = pl.BlockSpec(memory_space=pltpu.SMEM)


def exchange(value, axes):
    return lax.all_to_all(value, axes, split_axis=0, concat_axis=0, tiled=True)


def routing(item_ids, owner_row):
    rows = jnp.take(owner_row, item_ids.reshape(-1))
    owner = rows // ROWS
    count = owner.shape[0]
    order = jnp.arange(count, dtype=jnp.int32)
    before = (owner[None, :] == owner[:, None]) & (order[None, :] < order[:, None])
    rank = jnp.sum(before.astype(jnp.int32), axis=1)
    return owner * CAP + rank, rows % ROWS


def dot_nt(a, b):
    return lax.dot_general(a, b, (((1,), (1,)), ((), ())), preferred_element_type=F32)


def dot_tn(a, b):
    return lax.dot_general(a, b, (((0,), (0,)), ((), ())), preferred_element_type=F32)


def heads_kernel(
    info,
    packs,
    weights,
    kept,
    sent,
    grads,
    x_v,
    dy_v,
    w_v,
    acts,
    slope,
    d_value,
    d_key,
    d_z,
    gated,
    kept_v,
    sent_v,
    grads_v,
    sems,
    w_sems,
    out_sems,
):
    hd = HEAD_DIM
    scale = hd**-0.5
    u_cols, v_cols, q_cols, k_cols = (slice(m * hd, (m + 1) * hd) for m in range(4))
    steps = LENGTH // STEP
    copies = [
        pltpu.make_async_copy(
            packs.at[:, t, pl.ds(n * STEP, STEP)],
            held.at[:, pl.ds(n * STEP, STEP)],
            sems.at[t * steps + n],
        )
        for t, held in enumerate((x_v, dy_v))
        for n in range(steps)
    ]
    w_copies = [
        pltpu.make_async_copy(weights.at[x, r], w_v.at[x, :, r], w_sems.at[x * ZR + r])
        for x in range(X)
        for r in range(ZR)
    ]
    for copy in copies[:1] + w_copies + copies[1:]:
        copy.start()
    d_value[...] = jnp.zeros_like(d_value)
    d_key[...] = jnp.zeros_like(d_key)

    for copy in w_copies:
        copy.wait()
    wp = w_v[..., : 4 * hd].reshape(WIDTH, 4 * hd)
    wo = w_v[..., 4 * hd :].reshape(WIDTH, hd)

    for step in range(0, steps, 2):
        copies[step].wait()
        copies[step + 1].wait()
        rows = slice(step * STEP, (step + 2) * STEP)
        px = jnp.concatenate([x_v[g, rows, :] for g in range(8)], axis=1)
        z_pre = jnp.dot(px, wp, preferred_element_type=F32)
        sigma = jax.nn.sigmoid(z_pre)
        silu = z_pre * sigma
        acts[rows, :] = silu.astype(BF16)
        slope[rows, :] = sigma + silu * (1.0 - sigma)

    for step in range(steps):
        copies[steps + step].wait()
    for step in range(steps):
        base = step * STEP
        first = max(0, base - REACH)
        rows = slice(base, base + STEP)
        span = slice(first, base + STEP)
        pos_k = lax.broadcasted_iota(jnp.int32, (1, base + STEP - first), 1) + first
        pos_q = lax.broadcasted_iota(jnp.int32, (STEP, 1), 0) + base
        start = jnp.zeros_like(pos_q)
        for n in range(3):
            start = jnp.where(pos_q >= info[n], info[n], start)
        masked = (pos_k <= pos_q) & (pos_k >= start)
        query = acts[rows, q_cols]
        key = acts[span, k_cols]
        value = acts[span, v_cols]
        scores = dot_nt(query, key) * scale
        sigma = jnp.where(masked, jax.nn.sigmoid(scores), 0.0)
        silu = scores * sigma
        attn = silu.astype(BF16)
        factor = sigma + silu * (1.0 - sigma)
        mixed = jnp.dot(attn, value, preferred_element_type=F32)
        centred = mixed - jnp.mean(mixed, axis=-1, keepdims=True)
        inv_std = lax.rsqrt(jnp.mean(centred * centred, axis=-1, keepdims=True) + NORM_FLOOR)
        normed = centred * inv_std
        gating = acts[rows, u_cols].astype(F32)
        gated[rows, :] = (normed * gating).astype(BF16)
        pdy = jnp.concatenate([dy_v[g, rows, :] for g in range(8)], axis=1)
        d_gated = jnp.dot(pdy, wo, preferred_element_type=F32)
        d_normed = d_gated * gating
        d_mixed = (
            inv_std
            * (
                d_normed
                - jnp.mean(d_normed, axis=-1, keepdims=True)
                - normed * jnp.mean(d_normed * normed, axis=-1, keepdims=True)
            )
        ).astype(BF16)
        d_scores = (dot_nt(d_mixed, value) * factor).astype(BF16)
        d_query = jnp.dot(d_scores, key, preferred_element_type=F32)
        d_value[:, span] += jnp.dot(d_mixed.T, attn, preferred_element_type=F32)
        d_key[:, span] += jnp.dot(query.T, d_scores, preferred_element_type=F32)
        d_z[rows, u_cols] = (d_gated * normed * slope[rows, u_cols]).astype(BF16)
        d_z[rows, q_cols] = (d_query * (slope[rows, q_cols] * scale)).astype(BF16)

    d_z[:, v_cols] = (d_value[...].T * slope[:, v_cols]).astype(BF16)
    d_z[:, k_cols] = (d_key[...].T * (slope[:, k_cols] * scale)).astype(BF16)

    core = info[3]
    outs = []
    whole = dot_nt(d_z[...], wp).astype(BF16)
    for y in range(Y):
        part = whole[y * STEP : (y + 1) * STEP]

        @pl.when(core == 0)
        def _():
            kept_v[y] = part[:LANES]
            sent_v[y] = part[LANES:]

        @pl.when(core != 0)
        def _():
            kept_v[y] = part[LANES:]
            sent_v[y] = part[:LANES]

        for held, out in ((sent_v, sent), (kept_v, kept)):
            outs.append(pltpu.make_async_copy(held.at[y], out.at[y], out_sems.at[len(outs)]))
            outs[-1].start()

    for x in range(X):
        for dest, source, pack in ((slice(0, 512), d_z, x_v), (slice(512, 640), gated, dy_v)):
            columns = jnp.concatenate([pack[2 * x], pack[2 * x + 1]], axis=1)
            block = dot_tn(columns, source[...]).astype(BF16)
            grads_v[x, :, :, :, dest] = block.reshape(YC, ZR, PART_ROWS, block.shape[1])
        outs.append(pltpu.make_async_copy(grads_v.at[x], grads.at[x], out_sems.at[len(outs)]))
        outs[-1].start()
    for copy in outs:
        copy.wait()


def heads_backward(info, packs, weights):
    half = jax.ShapeDtypeStruct((Y, LANES, WIDTH), BF16)
    return pl.pallas_call(
        heads_kernel,
        out_shape=(
            half,
            half,
            jax.ShapeDtypeStruct((X, YC, ZR, PART_ROWS, HIDDEN), BF16),
        ),
        in_specs=[SMEM_SPEC, HBM_SPEC, pl.BlockSpec(memory_space=pl.ANY)],
        out_specs=(HBM_SPEC,) * 3,
        scratch_shapes=[
            pltpu.VMEM((8, LENGTH, LANES), BF16),
            pltpu.VMEM((8, LENGTH, LANES), BF16),
            pltpu.VMEM((X, YC, ZR, PART_ROWS, HIDDEN), BF16),
            pltpu.VMEM((LENGTH, 4 * HEAD_DIM), BF16),
            pltpu.VMEM((LENGTH, 4 * HEAD_DIM), F32),
            pltpu.VMEM((HEAD_DIM, LENGTH), F32),
            pltpu.VMEM((HEAD_DIM, LENGTH), F32),
            pltpu.VMEM((LENGTH, 4 * HEAD_DIM), BF16),
            pltpu.VMEM((LENGTH, HEAD_DIM), BF16),
            pltpu.VMEM((Y, LANES, WIDTH), BF16),
            pltpu.VMEM((Y, LANES, WIDTH), BF16),
            pltpu.VMEM((X, YC, ZR, PART_ROWS, HIDDEN), BF16),
            pltpu.SemaphoreType.DMA((2 * LENGTH // STEP,)),
            pltpu.SemaphoreType.DMA((X * ZR,)),
            pltpu.SemaphoreType.DMA((2 * Y + X,)),
        ],
        compiler_params=pltpu.CompilerParams(vmem_limit_bytes=GRANT * 2**20),
        cost_estimate=pl.CostEstimate(
            flops=5_000_000_000, bytes_accessed=9_000_000, transcendentals=2_000_000
        ),
        name="heads",
    )(info, packs, weights)


def pair_kernel(place, kept, got, own, to_1, to_2, to_3, own_v, sem):
    y = place[0]
    own_v[...] = (kept[y].astype(F32) + got[y].astype(F32)).astype(BF16)
    copy = pltpu.make_async_copy(own_v, own, sem)
    copy.start()
    for step, block in ((1, to_1), (2, to_2), (3, to_3)):
        other = (y + step) & (Y - 1)
        block[...] = (kept[other].astype(F32) + got[other].astype(F32)).astype(BF16)
    copy.wait()


def pair_sums(y, kept, got):
    block = jax.ShapeDtypeStruct((LANES, WIDTH), BF16)
    return pl.pallas_call(
        pair_kernel,
        out_shape=(block,) * Y,
        in_specs=[SMEM_SPEC, VMEM_SPEC, VMEM_SPEC],
        out_specs=(HBM_SPEC,) + (VMEM_SPEC,) * (Y - 1),
        scratch_shapes=[pltpu.VMEM((LANES, WIDTH), BF16), pltpu.SemaphoreType.DMA],
        compiler_params=pltpu.CompilerParams(vmem_limit_bytes=32 * 2**20),
        cost_estimate=pl.CostEstimate(flops=500_000, bytes_accessed=3_000_000, transcendentals=0),
        name="pair_sums",
    )(y, kept, got)


def payload_kernel(own, came_1, came_2, came_3, dy, out, own_v, sem):
    copy = pltpu.make_async_copy(own, own_v, sem)
    copy.start()
    copy.wait()
    lane = lax.broadcasted_iota(jnp.int32, (64, LANES), 1)
    for m in range(8):
        cols = slice(m * LANES, (m + 1) * LANES)
        total = own_v[:, cols].astype(F32) + dy[m].astype(F32)
        for came in (came_1, came_2, came_3):
            total = total + came[:, cols].astype(F32)
        low, high = total[:64], total[64:]
        even = jnp.where(lane < 64, low, pltpu.roll(high, 64, 1))
        odd = jnp.where(lane < 64, pltpu.roll(low, 64, 1), high)
        out[2 * m] = even.astype(BF16)
        out[2 * m + 1] = odd.astype(BF16)


def payload(own, came, dy):
    return pl.pallas_call(
        payload_kernel,
        out_shape=jax.ShapeDtypeStruct((Z, 64, LANES), BF16),
        in_specs=[HBM_SPEC] + [VMEM_SPEC] * 4,
        out_specs=VMEM_SPEC,
        scratch_shapes=[pltpu.VMEM((LANES, WIDTH), BF16), pltpu.SemaphoreType.DMA],
        compiler_params=pltpu.CompilerParams(vmem_limit_bytes=32 * 2**20),
        cost_estimate=pl.CostEstimate(flops=700_000, bytes_accessed=1_500_000, transcendentals=0),
        name="payload",
    )(own, *came, dy)


def weight_sum_kernel(shared, out, done):
    done[...] = jnp.zeros_like(done)
    out[..., LANES:] = jnp.zeros((YC, 2, 3 * PART_ROWS, LANES), F32)
    for h in range(YC):
        total = jnp.zeros((PART_ROWS, HIDDEN), F32)
        for x in range(X):
            for r in range(ZR):
                total = total + shared[x, h, r].astype(F32)
        for s in range(2):
            for n, col in enumerate((2 * s, 2 * s + 1, 4)):
                first = n * PART_ROWS
                block = total[:, col * LANES : (col + 1) * LANES]
                out[h, s, first : first + PART_ROWS, :LANES] = block


def weight_sum(shared):
    return pl.pallas_call(
        weight_sum_kernel,
        out_shape=(
            jax.ShapeDtypeStruct((YC, 2, 3 * PART_ROWS, 2 * LANES), F32),
            jax.ShapeDtypeStruct((8, LANES), F32),
        ),
        in_specs=[VMEM_SPEC],
        out_specs=(VMEM_SPEC, VMEM_SPEC),
        compiler_params=pltpu.CompilerParams(vmem_limit_bytes=32 * 2**20),
        cost_estimate=pl.CostEstimate(flops=700_000, bytes_accessed=1_700_000, transcendentals=0),
        name="weight_sum",
    )(shared)


def place_kernel(slots, tags, merged, out):
    slot_ids = lax.broadcasted_iota(jnp.int32, (SLOTS, LANES), 0)
    lane = lax.broadcasted_iota(jnp.int32, (SLOTS, LANES), 1)
    for pair in range(YC // 2):
        both = []
        for yc in (2 * pair, 2 * pair + 1):
            tokens = jnp.concatenate([merged[2 * yc], merged[2 * yc + 1]], axis=0)
            moved = [
                jnp.dot(
                    (slots[2 * yc + s : 2 * yc + s + 1, :] == slot_ids).astype(BF16),
                    tokens,
                    preferred_element_type=F32,
                )
                for s in range(2)
            ]
            rows = jnp.where(lane < 64, moved[0], moved[1])
            both.append(rows.reshape(OWNERS, CAP, LANES))
        out[:, pair * 16 : (pair + 1) * 16, :] = jnp.concatenate(both, axis=1).astype(BF16)
    out[:, YC * CAP :, :] = tags[...]


def place(slots, tags, merged):
    return pl.pallas_call(
        place_kernel,
        out_shape=jax.ShapeDtypeStruct((OWNERS, YC * CAP + 16, LANES), BF16),
        in_specs=[VMEM_SPEC] * 3,
        out_specs=VMEM_SPEC,
        compiler_params=pltpu.CompilerParams(vmem_limit_bytes=32 * 2**20),
        cost_estimate=pl.CostEstimate(
            flops=135_000_000, bytes_accessed=1_000_000, transcendentals=0
        ),
        name="place",
    )(slots, tags, merged)


def table_kernel(owned, out):
    count = YC * CAP
    row_ids = lax.broadcasted_iota(jnp.int32, (ROWS, LANES), 0).astype(F32)
    left = lax.broadcasted_iota(jnp.int32, (count, LANES), 1) < 64
    total = jnp.zeros((ROWS, LANES), F32)
    for pair in range(OWNERS // 2):
        select, rows = [], []
        for source in (2 * pair, 2 * pair + 1):
            tag = owned[source, count:, :].astype(F32)[:1]
            select.append((tag == row_ids).astype(BF16))
            here = owned[source, :count, :].astype(F32)
            rows.append(jnp.where(left, here, 0.0).astype(BF16))
            rows.append(jnp.where(left, 0.0, here).astype(BF16))
        total = total + jnp.dot(
            jnp.concatenate(select, axis=1),
            jnp.concatenate(rows, axis=0),
            preferred_element_type=F32,
        )
    out[...] = (total + pltpu.roll(total, 64, 1)).T[:64]


def table_sum(owned):
    return pl.pallas_call(
        table_kernel,
        out_shape=jax.ShapeDtypeStruct((64, ROWS), F32),
        in_specs=[VMEM_SPEC],
        out_specs=VMEM_SPEC,
        compiler_params=pltpu.CompilerParams(vmem_limit_bytes=32 * 2**20),
        cost_estimate=pl.CostEstimate(
            flops=270_000_000, bytes_accessed=1_000_000, transcendentals=0
        ),
        name="table_sum",
    )(owned)


def split_kernel(inputs, cotangent, out, sems):
    copies = [
        pltpu.make_async_copy(
            source.at[:, :, pl.ds(g * LANES, LANES)], out.at[g, :, t], sems.at[2 * g + t]
        )
        for g in range(8)
        for t, source in enumerate((inputs, cotangent))
    ]
    for copy in copies:
        copy.start()
    for copy in copies:
        copy.wait()


def split_columns(inputs, cotangent):
    return pl.pallas_call(
        split_kernel,
        out_shape=jax.ShapeDtypeStruct((8, 2, 2, 64, LANES), BF16),
        in_specs=[HBM_SPEC] * 2,
        out_specs=VMEM_SPEC,
        scratch_shapes=[pltpu.SemaphoreType.DMA((16,))],
        compiler_params=pltpu.CompilerParams(vmem_limit_bytes=60 * 2**20),
        cost_estimate=pl.CostEstimate(flops=0, bytes_accessed=1_000_000, transcendentals=0),
        name="split_columns",
    )(inputs, cotangent)


def per_device(inputs, cotangent, lengths, item_ids, owner_row, w_project, w_output):
    core = lax.axis_index("c")
    y_here = lax.axis_index("y")
    z_here = lax.axis_index(SEQ)
    lane = jnp.arange(LANES, dtype=jnp.int32)

    slot, local_row = routing(item_ids, owner_row)
    lens = lengths.reshape(-1)
    lens_row = jnp.concatenate([lens // 256, lens % 256])
    lens_row = jnp.pad(lens_row, (0, LANES - lens_row.shape[0]))
    small = jnp.pad(jnp.stack([slot, local_row, lens_row]), ((0, 5), (0, 0))).astype(BF16)
    high = PART_ROWS // 8
    wp_high = 2 * high
    n_w = wp_high + 2
    wp_tiles = w_project.reshape(ZR, high, 8, 2, LANES).transpose(0, 1, 3, 2, 4)
    wp_tiles = wp_tiles.reshape(ZR, wp_high, 8, LANES)
    wo_tiles = w_output.T.reshape(ZR, high, 8, 64).transpose(0, 2, 1, 3).reshape(ZR, 1, 8, LANES)
    small = jnp.broadcast_to(small[None, None], (ZR, 1, 8, LANES))
    w_tiles = jnp.concatenate([wp_tiles, wo_tiles, small], axis=1)

    spread = exchange(split_columns(inputs[0], cotangent[0]), PAIR)
    spread = spread.reshape(Z, 16, 8, LANES)
    w_tiles = jnp.broadcast_to(w_tiles[None], (ZQ, ZR, n_w, 8, LANES)).reshape(Z, n_w, 8, LANES)
    arrived = exchange(jnp.concatenate([spread, w_tiles], axis=1), SEQ)
    mine = arrived[:, :16].reshape(Z, 2, 64, LANES).transpose(1, 0, 2, 3)
    packs = lax.all_gather(mine.reshape(1, 2, LENGTH, LANES), PAIR, axis=0, tiled=True)

    by_head = exchange(arrived[:, 16:].reshape(YC, 2, n_w, 8, LANES), PAIR)
    wp_part = by_head[:, :, :wp_high].reshape(YC, 2, high, 2, 8, LANES)
    wp_part = wp_part.transpose(0, 2, 4, 1, 3, 5).reshape(YC, PART_ROWS, 4 * HEAD_DIM)
    wo_part = by_head[:, :, wp_high].reshape(YC, 2, 8, high, 64).transpose(0, 3, 2, 1, 4)
    w_part = jnp.concatenate([wp_part, wo_part.reshape(YC, PART_ROWS, HEAD_DIM)], axis=2)
    w_all = jnp.broadcast_to(w_part[None], (X * ZR,) + w_part.shape)
    weights = exchange(w_all, SHARE).reshape(X, ZR, YC, PART_ROWS, HIDDEN)

    facts = by_head[:, :, n_w - 1].astype(F32)
    slots = facts[:, :, 0].astype(jnp.int32)
    tag_of = facts[:, :, 1]
    lens_all = facts[:, 0, 2, :12].reshape(YC, 2, 2, 3)
    lens_all = (lens_all[:, 0] * 256.0 + lens_all[:, 1]).astype(jnp.int32).reshape(Z, 3)
    pack_lens = lax.dynamic_index_in_dim(lens_all, z_here, 0, keepdims=False)
    ends = jnp.cumsum(pack_lens)

    info = jnp.concatenate([ends, core[None]]).astype(jnp.int32)
    slot_ids = jnp.arange(SLOTS, dtype=jnp.int32)
    placed = slots[:, :, None, :] == slot_ids[None, None, :, None]
    tags = jnp.sum(jnp.where(placed, tag_of[:, :, None, :], 0.0), axis=3)
    tags = tags.reshape(YC, 2, OWNERS, CAP).transpose(2, 1, 0, 3).reshape(OWNERS, 1, LANES)
    tags = jnp.broadcast_to(tags.astype(BF16), (OWNERS, 16, LANES))

    kept, sent, grads = heads_backward(info, packs, weights)

    shared = exchange(grads.reshape(X * YC * ZR, PART_ROWS, HIDDEN), SPREAD)
    shared = shared.reshape(X, YC, ZR, PART_ROWS, HIDDEN)

    got = lax.ppermute(sent, "c", [(0, 1), (1, 0)])
    own, *to_y = pair_sums(y_here[None].astype(jnp.int32), kept, got)
    came = [
        lax.ppermute(to_y[step - 1], "y", [(i, (i + step) % Y) for i in range(Y)])
        for step in range(1, Y)
    ]
    block = (y_here * C + core) * LANES
    dy_own = lax.dynamic_slice(packs, (0, 1, block, 0), (YC, 1, LANES, LANES))[:, 0]

    w_sum, done = weight_sum(shared)
    done, *came = lax.optimization_barrier((done, *came))
    merged = exchange(payload(own, came, dy_own), SEQ)

    low = lax.axis_index("zr")
    rest = lax.psum_scatter(w_sum, "zq", scatter_dimension=0, tiled=True)
    rest = rest[0, :, :, :LANES]
    mine = lax.dynamic_index_in_dim(rest, low, 0, keepdims=False)
    other = lax.dynamic_index_in_dim(rest, 1 - low, 0, keepdims=False)
    other = lax.ppermute(other, "zr", [(0, 1), (1, 0)])
    w_grad = jnp.where(low == 0, jnp.stack([mine, other]), jnp.stack([other, mine]))
    w_grad = w_grad.reshape(ZR, 3, PART_ROWS, LANES)
    grad_proj = w_grad[:, :2].transpose(0, 2, 1, 3).reshape(32, 2 * LANES)
    both_out = w_grad[:, 2].reshape(32, 2, 64)
    grad_out = lax.dynamic_index_in_dim(both_out, z_here & 1, 1, keepdims=False).T

    owned = exchange(place(slots.reshape(2 * YC, LANES), tags, merged), DP)
    return (grad_proj, grad_out, table_sum(owned).T)


def solution(mesh):
    fine = Mesh(mesh.devices.reshape(X, Y, C, ZQ, ZR), ALL)
    return jax.shard_map(
        per_device,
        mesh=fine,
        in_specs=(
            P(DP, None, SEQ, None),
            P(DP, None, SEQ, None),
            P(DP, None, None),
            P(DP, None, SEQ),
            P(),
            P(DP, SEQ),
            P(SEQ, DP),
        ),
        out_specs=(P(DP, SEQ), P(SEQ, DP), P(DP, SEQ)),
        check_vma=False,
    )
```

```python
import jax
import jax.numpy as jnp
from jax import lax
from jax.experimental import pallas as pl
from jax.experimental.pallas import tpu as pltpu
from jax.sharding import Mesh, PartitionSpec as P

HEAD_DIM = 128
NORM_FLOOR = 1.0
F32 = jnp.float32
BF16 = jnp.bfloat16

X, Y, C, ZQ, ZR = 4, 4, 2, 8, 2
YC = Y * C
Z = ZQ * ZR
PAIR = ("y", "c")
DP = ("x", "y", "c")
SEQ = ("zq", "zr")
SHARE = ("x", "zr")
SPREAD = ("x", "y", "c", "zr")
ALL = ("x", "y", "c", "zq", "zr")
OWNERS = X * YC
CAP = 8
ROWS = 256
SLOTS = OWNERS * CAP
LANES = 128
LENGTH = 1024
WIDTH = 1024
HIDDEN = 5 * HEAD_DIM
PART_ROWS = 32 // ZR
STEP = 256
SUM_ROWS = 64
REACH = 512
VMEM_SPEC = pl.BlockSpec(memory_space=pltpu.VMEM)
GRANT = 58
HBM_SPEC = pl.BlockSpec(memory_space=pltpu.HBM)
SMEM_SPEC = pl.BlockSpec(memory_space=pltpu.SMEM)


def exchange(value, axes):
    return lax.all_to_all(value, axes, split_axis=0, concat_axis=0, tiled=True)


def routing(item_ids, owner_row):
    rows = jnp.take(owner_row, item_ids.reshape(-1))
    owner = rows // ROWS
    count = owner.shape[0]
    order = jnp.arange(count, dtype=jnp.int32)
    before = (owner[None, :] == owner[:, None]) & (order[None, :] < order[:, None])
    rank = jnp.sum(before.astype(jnp.int32), axis=1)
    return owner * CAP + rank, rows % ROWS


def dot_nt(a, b):
    return lax.dot_general(a, b, (((1,), (1,)), ((), ())), preferred_element_type=F32)


def dot_tn(a, b):
    return lax.dot_general(a, b, (((0,), (0,)), ((), ())), preferred_element_type=F32)


def heads_kernel(
    info,
    packs,
    weights,
    kept,
    sent,
    grads,
    x_v,
    dy_v,
    w_v,
    acts,
    slope,
    d_value,
    d_key,
    d_z,
    gated,
    kept_v,
    sent_v,
    grads_v,
    sems,
    w_sems,
    out_sems,
):
    hd = HEAD_DIM
    scale = hd**-0.5
    u_cols, v_cols, q_cols, k_cols = (slice(m * hd, (m + 1) * hd) for m in range(4))
    steps = LENGTH // STEP
    copies = [
        pltpu.make_async_copy(
            packs.at[:, t, pl.ds(n * STEP, STEP)],
            held.at[:, pl.ds(n * STEP, STEP)],
            sems.at[t * steps + n],
        )
        for t, held in enumerate((x_v, dy_v))
        for n in range(steps)
    ]
    w_copies = [
        pltpu.make_async_copy(weights.at[x, r], w_v.at[x, :, r], w_sems.at[x * ZR + r])
        for x in range(X)
        for r in range(ZR)
    ]
    for copy in copies[:1] + w_copies + copies[1:]:
        copy.start()
    d_value[...] = jnp.zeros_like(d_value)
    d_key[...] = jnp.zeros_like(d_key)

    for copy in w_copies:
        copy.wait()
    wp = w_v[..., : 4 * hd].reshape(WIDTH, 4 * hd)
    wo = w_v[..., 4 * hd :].reshape(WIDTH, hd)

    for step in range(0, steps, 2):
        copies[step].wait()
        copies[step + 1].wait()
        rows = slice(step * STEP, (step + 2) * STEP)
        px = jnp.concatenate([x_v[g, rows, :] for g in range(8)], axis=1)
        z_pre = jnp.dot(px, wp, preferred_element_type=F32)
        sigma = jax.nn.sigmoid(z_pre)
        silu = z_pre * sigma
        acts[rows, :] = silu.astype(BF16)
        slope[rows, :] = sigma + silu * (1.0 - sigma)

    for step in range(steps):
        copies[steps + step].wait()
    for step in range(steps):
        base = step * STEP
        first = max(0, base - REACH)
        rows = slice(base, base + STEP)
        span = slice(first, base + STEP)
        pos_k = lax.broadcasted_iota(jnp.int32, (1, base + STEP - first), 1) + first
        pos_q = lax.broadcasted_iota(jnp.int32, (STEP, 1), 0) + base
        start = jnp.zeros_like(pos_q)
        for n in range(3):
            start = jnp.where(pos_q >= info[n], info[n], start)
        masked = (pos_k <= pos_q) & (pos_k >= start)
        query = acts[rows, q_cols]
        key = acts[span, k_cols]
        value = acts[span, v_cols]
        scores = dot_nt(query, key) * scale
        sigma = jnp.where(masked, jax.nn.sigmoid(scores), 0.0)
        silu = scores * sigma
        attn = silu.astype(BF16)
        factor = sigma + silu * (1.0 - sigma)
        mixed = jnp.dot(attn, value, preferred_element_type=F32)
        centred = mixed - jnp.mean(mixed, axis=-1, keepdims=True)
        inv_std = lax.rsqrt(jnp.mean(centred * centred, axis=-1, keepdims=True) + NORM_FLOOR)
        normed = centred * inv_std
        gating = acts[rows, u_cols].astype(F32)
        gated[rows, :] = (normed * gating).astype(BF16)
        pdy = jnp.concatenate([dy_v[g, rows, :] for g in range(8)], axis=1)
        d_gated = jnp.dot(pdy, wo, preferred_element_type=F32)
        d_normed = d_gated * gating
        d_mixed = (
            inv_std
            * (
                d_normed
                - jnp.mean(d_normed, axis=-1, keepdims=True)
                - normed * jnp.mean(d_normed * normed, axis=-1, keepdims=True)
            )
        ).astype(BF16)
        d_scores = (dot_nt(d_mixed, value) * factor).astype(BF16)
        d_query = jnp.dot(d_scores, key, preferred_element_type=F32)
        d_value[:, span] += jnp.dot(d_mixed.T, attn, preferred_element_type=F32)
        d_key[:, span] += jnp.dot(query.T, d_scores, preferred_element_type=F32)
        d_z[rows, u_cols] = (d_gated * normed * slope[rows, u_cols]).astype(BF16)
        d_z[rows, q_cols] = (d_query * (slope[rows, q_cols] * scale)).astype(BF16)

    d_z[:, v_cols] = (d_value[...].T * slope[:, v_cols]).astype(BF16)
    d_z[:, k_cols] = (d_key[...].T * (slope[:, k_cols] * scale)).astype(BF16)

    core = info[3]
    outs = []
    whole = dot_nt(d_z[...], wp).astype(BF16)
    for y in range(Y):
        part = whole[y * STEP : (y + 1) * STEP]

        @pl.when(core == 0)
        def _():
            kept_v[y] = part[:LANES]
            sent_v[y] = part[LANES:]

        @pl.when(core != 0)
        def _():
            kept_v[y] = part[LANES:]
            sent_v[y] = part[:LANES]

        for held, out in ((sent_v, sent), (kept_v, kept)):
            outs.append(pltpu.make_async_copy(held.at[y], out.at[y], out_sems.at[len(outs)]))
            outs[-1].start()

    for x in range(X):
        for dest, source, pack in ((slice(0, 512), d_z, x_v), (slice(512, 640), gated, dy_v)):
            columns = jnp.concatenate([pack[2 * x], pack[2 * x + 1]], axis=1)
            block = dot_tn(columns, source[...]).astype(BF16)
            grads_v[x, :, :, :, dest] = block.reshape(YC, ZR, PART_ROWS, block.shape[1])
        outs.append(pltpu.make_async_copy(grads_v.at[x], grads.at[x], out_sems.at[len(outs)]))
        outs[-1].start()
    for copy in outs:
        copy.wait()


def heads_backward(info, packs, weights):
    half = jax.ShapeDtypeStruct((Y, LANES, WIDTH), BF16)
    return pl.pallas_call(
        heads_kernel,
        out_shape=(
            half,
            half,
            jax.ShapeDtypeStruct((X, YC, ZR, PART_ROWS, HIDDEN), BF16),
        ),
        in_specs=[SMEM_SPEC, HBM_SPEC, pl.BlockSpec(memory_space=pl.ANY)],
        out_specs=(HBM_SPEC,) * 3,
        scratch_shapes=[
            pltpu.VMEM((8, LENGTH, LANES), BF16),
            pltpu.VMEM((8, LENGTH, LANES), BF16),
            pltpu.VMEM((X, YC, ZR, PART_ROWS, HIDDEN), BF16),
            pltpu.VMEM((LENGTH, 4 * HEAD_DIM), BF16),
            pltpu.VMEM((LENGTH, 4 * HEAD_DIM), F32),
            pltpu.VMEM((HEAD_DIM, LENGTH), F32),
            pltpu.VMEM((HEAD_DIM, LENGTH), F32),
            pltpu.VMEM((LENGTH, 4 * HEAD_DIM), BF16),
            pltpu.VMEM((LENGTH, HEAD_DIM), BF16),
            pltpu.VMEM((Y, LANES, WIDTH), BF16),
            pltpu.VMEM((Y, LANES, WIDTH), BF16),
            pltpu.VMEM((X, YC, ZR, PART_ROWS, HIDDEN), BF16),
            pltpu.SemaphoreType.DMA((2 * LENGTH // STEP,)),
            pltpu.SemaphoreType.DMA((X * ZR,)),
            pltpu.SemaphoreType.DMA((2 * Y + X,)),
        ],
        compiler_params=pltpu.CompilerParams(vmem_limit_bytes=GRANT * 2**20),
        cost_estimate=pl.CostEstimate(
            flops=5_000_000_000, bytes_accessed=9_000_000, transcendentals=2_000_000
        ),
        name="heads",
    )(info, packs, weights)


def pair_kernel(place, kept, got, own, to_1, to_2, to_3, own_v, sem):
    y = place[0]
    own_v[...] = (kept[y].astype(F32) + got[y].astype(F32)).astype(BF16)
    copy = pltpu.make_async_copy(own_v, own, sem)
    copy.start()
    for step, block in ((1, to_1), (2, to_2), (3, to_3)):
        other = (y + step) & (Y - 1)
        block[...] = (kept[other].astype(F32) + got[other].astype(F32)).astype(BF16)
    copy.wait()


def pair_sums(y, kept, got):
    block = jax.ShapeDtypeStruct((LANES, WIDTH), BF16)
    return pl.pallas_call(
        pair_kernel,
        out_shape=(block,) * Y,
        in_specs=[SMEM_SPEC, VMEM_SPEC, VMEM_SPEC],
        out_specs=(HBM_SPEC,) + (VMEM_SPEC,) * (Y - 1),
        scratch_shapes=[pltpu.VMEM((LANES, WIDTH), BF16), pltpu.SemaphoreType.DMA],
        compiler_params=pltpu.CompilerParams(vmem_limit_bytes=32 * 2**20),
        cost_estimate=pl.CostEstimate(flops=500_000, bytes_accessed=3_000_000, transcendentals=0),
        name="pair_sums",
    )(y, kept, got)


def payload_kernel(own, came_1, came_2, came_3, dy, out, own_v, sem):
    copy = pltpu.make_async_copy(own, own_v, sem)
    copy.start()
    copy.wait()
    lane = lax.broadcasted_iota(jnp.int32, (64, LANES), 1)
    for m in range(8):
        cols = slice(m * LANES, (m + 1) * LANES)
        total = own_v[:, cols].astype(F32) + dy[m].astype(F32)
        for came in (came_1, came_2, came_3):
            total = total + came[:, cols].astype(F32)
        low, high = total[:64], total[64:]
        even = jnp.where(lane < 64, low, pltpu.roll(high, 64, 1))
        odd = jnp.where(lane < 64, pltpu.roll(low, 64, 1), high)
        out[2 * m] = even.astype(BF16)
        out[2 * m + 1] = odd.astype(BF16)


def payload(own, came, dy):
    return pl.pallas_call(
        payload_kernel,
        out_shape=jax.ShapeDtypeStruct((Z, 64, LANES), BF16),
        in_specs=[HBM_SPEC] + [VMEM_SPEC] * 4,
        out_specs=VMEM_SPEC,
        scratch_shapes=[pltpu.VMEM((LANES, WIDTH), BF16), pltpu.SemaphoreType.DMA],
        compiler_params=pltpu.CompilerParams(vmem_limit_bytes=32 * 2**20),
        cost_estimate=pl.CostEstimate(flops=700_000, bytes_accessed=1_500_000, transcendentals=0),
        name="payload",
    )(own, *came, dy)


def weight_sum_kernel(shared, out, done):
    done[...] = jnp.zeros_like(done)
    out[:, :, 3 * PART_ROWS :, :] = jnp.zeros((YC, 2, SUM_ROWS - 3 * PART_ROWS, LANES), F32)
    for h in range(YC):
        total = jnp.zeros((PART_ROWS, HIDDEN), F32)
        for x in range(X):
            for r in range(ZR):
                total = total + shared[x, h, r].astype(F32)
        for s in range(2):
            for n, col in enumerate((2 * s, 2 * s + 1, 4)):
                first = n * PART_ROWS
                block = total[:, col * LANES : (col + 1) * LANES]
                out[h, s, first : first + PART_ROWS, :] = block


def weight_sum(shared):
    return pl.pallas_call(
        weight_sum_kernel,
        out_shape=(
            jax.ShapeDtypeStruct((YC, 2, SUM_ROWS, LANES), F32),
            jax.ShapeDtypeStruct((8, LANES), F32),
        ),
        in_specs=[VMEM_SPEC],
        out_specs=(VMEM_SPEC, VMEM_SPEC),
        compiler_params=pltpu.CompilerParams(vmem_limit_bytes=32 * 2**20),
        cost_estimate=pl.CostEstimate(flops=700_000, bytes_accessed=1_700_000, transcendentals=0),
        name="weight_sum",
    )(shared)


def place_kernel(slots, tags, merged, out):
    slot_ids = lax.broadcasted_iota(jnp.int32, (SLOTS, LANES), 0)
    lane = lax.broadcasted_iota(jnp.int32, (SLOTS, LANES), 1)
    for pair in range(YC // 2):
        both = []
        for yc in (2 * pair, 2 * pair + 1):
            tokens = jnp.concatenate([merged[2 * yc], merged[2 * yc + 1]], axis=0)
            moved = [
                jnp.dot(
                    (slots[2 * yc + s : 2 * yc + s + 1, :] == slot_ids).astype(BF16),
                    tokens,
                    preferred_element_type=F32,
                )
                for s in range(2)
            ]
            rows = jnp.where(lane < 64, moved[0], moved[1])
            both.append(rows.reshape(OWNERS, CAP, LANES))
        out[:, pair * 16 : (pair + 1) * 16, :] = jnp.concatenate(both, axis=1).astype(BF16)
    out[:, YC * CAP :, :] = tags[...]


def place(slots, tags, merged):
    return pl.pallas_call(
        place_kernel,
        out_shape=jax.ShapeDtypeStruct((OWNERS, YC * CAP + 16, LANES), BF16),
        in_specs=[VMEM_SPEC] * 3,
        out_specs=VMEM_SPEC,
        compiler_params=pltpu.CompilerParams(vmem_limit_bytes=32 * 2**20),
        cost_estimate=pl.CostEstimate(
            flops=135_000_000, bytes_accessed=1_000_000, transcendentals=0
        ),
        name="place",
    )(slots, tags, merged)


def table_kernel(owned, out):
    count = YC * CAP
    row_ids = lax.broadcasted_iota(jnp.int32, (ROWS, LANES), 0).astype(F32)
    left = lax.broadcasted_iota(jnp.int32, (count, LANES), 1) < 64
    total = jnp.zeros((ROWS, LANES), F32)
    for pair in range(OWNERS // 2):
        select, rows = [], []
        for source in (2 * pair, 2 * pair + 1):
            tag = owned[source, count:, :].astype(F32)[:1]
            select.append((tag == row_ids).astype(BF16))
            here = owned[source, :count, :].astype(F32)
            rows.append(jnp.where(left, here, 0.0).astype(BF16))
            rows.append(jnp.where(left, 0.0, here).astype(BF16))
        total = total + jnp.dot(
            jnp.concatenate(select, axis=1),
            jnp.concatenate(rows, axis=0),
            preferred_element_type=F32,
        )
    out[...] = (total + pltpu.roll(total, 64, 1)).T[:64]


def table_sum(owned):
    return pl.pallas_call(
        table_kernel,
        out_shape=jax.ShapeDtypeStruct((64, ROWS), F32),
        in_specs=[VMEM_SPEC],
        out_specs=VMEM_SPEC,
        compiler_params=pltpu.CompilerParams(vmem_limit_bytes=32 * 2**20),
        cost_estimate=pl.CostEstimate(
            flops=270_000_000, bytes_accessed=1_000_000, transcendentals=0
        ),
        name="table_sum",
    )(owned)


def split_kernel(inputs, cotangent, out, sems):
    copies = [
        pltpu.make_async_copy(
            source.at[:, :, pl.ds(g * LANES, LANES)], out.at[g, :, t], sems.at[2 * g + t]
        )
        for g in range(8)
        for t, source in enumerate((inputs, cotangent))
    ]
    for copy in copies:
        copy.start()
    for copy in copies:
        copy.wait()


def split_columns(inputs, cotangent):
    return pl.pallas_call(
        split_kernel,
        out_shape=jax.ShapeDtypeStruct((8, 2, 2, 64, LANES), BF16),
        in_specs=[HBM_SPEC] * 2,
        out_specs=VMEM_SPEC,
        scratch_shapes=[pltpu.SemaphoreType.DMA((16,))],
        compiler_params=pltpu.CompilerParams(vmem_limit_bytes=60 * 2**20),
        cost_estimate=pl.CostEstimate(flops=0, bytes_accessed=1_000_000, transcendentals=0),
        name="split_columns",
    )(inputs, cotangent)


def per_device(inputs, cotangent, lengths, item_ids, owner_row, w_project, w_output):
    core = lax.axis_index("c")
    y_here = lax.axis_index("y")
    z_here = lax.axis_index(SEQ)
    lane = jnp.arange(LANES, dtype=jnp.int32)

    slot, local_row = routing(item_ids, owner_row)
    lens = lengths.reshape(-1)
    lens_row = jnp.concatenate([lens // 256, lens % 256])
    lens_row = jnp.pad(lens_row, (0, LANES - lens_row.shape[0]))
    small = jnp.pad(jnp.stack([slot, local_row, lens_row]), ((0, 5), (0, 0))).astype(BF16)
    high = PART_ROWS // 8
    wp_high = 2 * high
    n_w = wp_high + 2
    wp_tiles = w_project.reshape(ZR, high, 8, 2, LANES).transpose(0, 1, 3, 2, 4)
    wp_tiles = wp_tiles.reshape(ZR, wp_high, 8, LANES)
    wo_tiles = w_output.T.reshape(ZR, high, 8, 64).transpose(0, 2, 1, 3).reshape(ZR, 1, 8, LANES)
    small = jnp.broadcast_to(small[None, None], (ZR, 1, 8, LANES))
    w_tiles = jnp.concatenate([wp_tiles, wo_tiles, small], axis=1)

    spread = exchange(split_columns(inputs[0], cotangent[0]), PAIR)
    spread = spread.reshape(Z, 16, 8, LANES)
    w_tiles = jnp.broadcast_to(w_tiles[None], (ZQ, ZR, n_w, 8, LANES)).reshape(Z, n_w, 8, LANES)
    arrived = exchange(jnp.concatenate([spread, w_tiles], axis=1), SEQ)
    mine = arrived[:, :16].reshape(Z, 2, 64, LANES).transpose(1, 0, 2, 3)
    packs = lax.all_gather(mine.reshape(1, 2, LENGTH, LANES), PAIR, axis=0, tiled=True)

    by_head = exchange(arrived[:, 16:].reshape(YC, 2, n_w, 8, LANES), PAIR)
    wp_part = by_head[:, :, :wp_high].reshape(YC, 2, high, 2, 8, LANES)
    wp_part = wp_part.transpose(0, 2, 4, 1, 3, 5).reshape(YC, PART_ROWS, 4 * HEAD_DIM)
    wo_part = by_head[:, :, wp_high].reshape(YC, 2, 8, high, 64).transpose(0, 3, 2, 1, 4)
    w_part = jnp.concatenate([wp_part, wo_part.reshape(YC, PART_ROWS, HEAD_DIM)], axis=2)
    w_all = jnp.broadcast_to(w_part[None], (X * ZR,) + w_part.shape)
    weights = exchange(w_all, SHARE).reshape(X, ZR, YC, PART_ROWS, HIDDEN)

    facts = by_head[:, :, n_w - 1].astype(F32)
    slots = facts[:, :, 0].astype(jnp.int32)
    tag_of = facts[:, :, 1]
    lens_all = facts[:, 0, 2, :12].reshape(YC, 2, 2, 3)
    lens_all = (lens_all[:, 0] * 256.0 + lens_all[:, 1]).astype(jnp.int32).reshape(Z, 3)
    pack_lens = lax.dynamic_index_in_dim(lens_all, z_here, 0, keepdims=False)
    ends = jnp.cumsum(pack_lens)

    info = jnp.concatenate([ends, core[None]]).astype(jnp.int32)
    slot_ids = jnp.arange(SLOTS, dtype=jnp.int32)
    placed = slots[:, :, None, :] == slot_ids[None, None, :, None]
    tags = jnp.sum(jnp.where(placed, tag_of[:, :, None, :], 0.0), axis=3)
    tags = tags.reshape(YC, 2, OWNERS, CAP).transpose(2, 1, 0, 3).reshape(OWNERS, 1, LANES)
    tags = jnp.broadcast_to(tags.astype(BF16), (OWNERS, 16, LANES))

    kept, sent, grads = heads_backward(info, packs, weights)

    shared = exchange(grads.reshape(X * YC * ZR, PART_ROWS, HIDDEN), SPREAD)
    shared = shared.reshape(X, YC, ZR, PART_ROWS, HIDDEN)

    got = lax.ppermute(sent, "c", [(0, 1), (1, 0)])
    own, *to_y = pair_sums(y_here[None].astype(jnp.int32), kept, got)
    came = [
        lax.ppermute(to_y[step - 1], "y", [(i, (i + step) % Y) for i in range(Y)])
        for step in range(1, Y)
    ]
    block = (y_here * C + core) * LANES
    dy_own = lax.dynamic_slice(packs, (0, 1, block, 0), (YC, 1, LANES, LANES))[:, 0]

    w_sum, done = weight_sum(shared)
    done, *came = lax.optimization_barrier((done, *came))
    merged = exchange(payload(own, came, dy_own), SEQ)

    low = lax.axis_index("zr")
    rest = lax.psum_scatter(w_sum, "zq", scatter_dimension=0, tiled=True)
    rest = rest[0, :, : 3 * PART_ROWS]
    mine = lax.dynamic_index_in_dim(rest, low, 0, keepdims=False)
    other = lax.dynamic_index_in_dim(rest, 1 - low, 0, keepdims=False)
    other = lax.ppermute(other, "zr", [(0, 1), (1, 0)])
    w_grad = jnp.where(low == 0, jnp.stack([mine, other]), jnp.stack([other, mine]))
    w_grad = w_grad.reshape(ZR, 3, PART_ROWS, LANES)
    grad_proj = w_grad[:, :2].transpose(0, 2, 1, 3).reshape(32, 2 * LANES)
    both_out = w_grad[:, 2].reshape(32, 2, 64)
    grad_out = lax.dynamic_index_in_dim(both_out, z_here & 1, 1, keepdims=False).T

    owned = exchange(place(slots.reshape(2 * YC, LANES), tags, merged), DP)
    owned, grad_proj, grad_out = lax.optimization_barrier((owned, grad_proj, grad_out))
    return (grad_proj, grad_out, table_sum(owned).T)


def solution(mesh):
    fine = Mesh(mesh.devices.reshape(X, Y, C, ZQ, ZR), ALL)
    return jax.shard_map(
        per_device,
        mesh=fine,
        in_specs=(
            P(DP, None, SEQ, None),
            P(DP, None, SEQ, None),
            P(DP, None, None),
            P(DP, None, SEQ),
            P(),
            P(DP, SEQ),
            P(SEQ, DP),
        ),
        out_specs=(P(DP, SEQ), P(SEQ, DP), P(DP, SEQ)),
        check_vma=False,
    )
```

```python
import jax
import jax.numpy as jnp
from jax import lax
from jax.experimental import pallas as pl
from jax.experimental.pallas import tpu as pltpu
from jax.sharding import Mesh, PartitionSpec as P

HEAD_DIM = 128
NORM_FLOOR = 1.0
F32 = jnp.float32
BF16 = jnp.bfloat16

X, Y, C, ZQ, ZR = 4, 4, 2, 8, 2
YC = Y * C
Z = ZQ * ZR
PAIR = ("y", "c")
DP = ("x", "y", "c")
SEQ = ("zq", "zr")
SHARE = ("x", "zr")
SPREAD = ("x", "y", "c", "zr")
ALL = ("x", "y", "c", "zq", "zr")
OWNERS = X * YC
CAP = 8
ROWS = 256
SLOTS = OWNERS * CAP
LANES = 128
LENGTH = 1024
WIDTH = 1024
HIDDEN = 5 * HEAD_DIM
PART_ROWS = 32 // ZR
STEP = 256
SUM_ROWS = 64
REACH = 512
VMEM_SPEC = pl.BlockSpec(memory_space=pltpu.VMEM)
GRANT = 58
HBM_SPEC = pl.BlockSpec(memory_space=pltpu.HBM)
SMEM_SPEC = pl.BlockSpec(memory_space=pltpu.SMEM)


def exchange(value, axes):
    return lax.all_to_all(value, axes, split_axis=0, concat_axis=0, tiled=True)


def routing(item_ids, owner_row):
    rows = jnp.take(owner_row, item_ids.reshape(-1))
    owner = rows // ROWS
    count = owner.shape[0]
    order = jnp.arange(count, dtype=jnp.int32)
    before = (owner[None, :] == owner[:, None]) & (order[None, :] < order[:, None])
    rank = jnp.sum(before.astype(jnp.int32), axis=1)
    return owner * CAP + rank, rows % ROWS


def dot_nt(a, b):
    return lax.dot_general(a, b, (((1,), (1,)), ((), ())), preferred_element_type=F32)


def dot_tn(a, b):
    return lax.dot_general(a, b, (((0,), (0,)), ((), ())), preferred_element_type=F32)


def heads_kernel(
    info,
    packs,
    weights,
    kept,
    sent,
    grads,
    x_v,
    dy_v,
    w_v,
    acts,
    slope,
    d_value,
    d_key,
    d_z,
    gated,
    kept_v,
    sent_v,
    grads_v,
    sems,
    w_sems,
    out_sems,
):
    hd = HEAD_DIM
    scale = hd**-0.5
    u_cols, v_cols, q_cols, k_cols = (slice(m * hd, (m + 1) * hd) for m in range(4))
    steps = LENGTH // STEP
    copies = [
        pltpu.make_async_copy(
            packs.at[:, t, pl.ds(n * STEP, STEP)],
            held.at[:, pl.ds(n * STEP, STEP)],
            sems.at[t * steps + n],
        )
        for t, held in enumerate((x_v, dy_v))
        for n in range(steps)
    ]
    w_copies = [
        pltpu.make_async_copy(weights.at[x, r], w_v.at[x, :, r], w_sems.at[x * ZR + r])
        for x in range(X)
        for r in range(ZR)
    ]
    for copy in copies[:1] + w_copies + copies[1:]:
        copy.start()
    d_value[...] = jnp.zeros_like(d_value)
    d_key[...] = jnp.zeros_like(d_key)

    for copy in w_copies:
        copy.wait()
    wp = w_v[..., : 4 * hd].reshape(WIDTH, 4 * hd)
    wo = w_v[..., 4 * hd :].reshape(WIDTH, hd)

    for step in range(0, steps, 2):
        copies[step].wait()
        copies[step + 1].wait()
        rows = slice(step * STEP, (step + 2) * STEP)
        px = jnp.concatenate([x_v[g, rows, :] for g in range(8)], axis=1)
        z_pre = jnp.dot(px, wp, preferred_element_type=F32)
        sigma = jax.nn.sigmoid(z_pre)
        silu = z_pre * sigma
        acts[rows, :] = silu.astype(BF16)
        slope[rows, :] = sigma + silu * (1.0 - sigma)

    for step in range(steps):
        copies[steps + step].wait()
    for step in range(steps):
        base = step * STEP
        first = max(0, base - REACH)
        rows = slice(base, base + STEP)
        span = slice(first, base + STEP)
        pos_k = lax.broadcasted_iota(jnp.int32, (1, base + STEP - first), 1) + first
        pos_q = lax.broadcasted_iota(jnp.int32, (STEP, 1), 0) + base
        start = jnp.zeros_like(pos_q)
        for n in range(3):
            start = jnp.where(pos_q >= info[n], info[n], start)
        masked = (pos_k <= pos_q) & (pos_k >= start)
        query = acts[rows, q_cols]
        key = acts[span, k_cols]
        value = acts[span, v_cols]
        scores = dot_nt(query, key) * scale
        sigma = jnp.where(masked, jax.nn.sigmoid(scores), 0.0)
        silu = scores * sigma
        attn = silu.astype(BF16)
        factor = sigma + silu * (1.0 - sigma)
        mixed = jnp.dot(attn, value, preferred_element_type=F32)
        centred = mixed - jnp.mean(mixed, axis=-1, keepdims=True)
        inv_std = lax.rsqrt(jnp.mean(centred * centred, axis=-1, keepdims=True) + NORM_FLOOR)
        normed = centred * inv_std
        gating = acts[rows, u_cols].astype(F32)
        gated[rows, :] = (normed * gating).astype(BF16)
        pdy = jnp.concatenate([dy_v[g, rows, :] for g in range(8)], axis=1)
        d_gated = jnp.dot(pdy, wo, preferred_element_type=F32)
        d_normed = d_gated * gating
        d_mixed = (
            inv_std
            * (
                d_normed
                - jnp.mean(d_normed, axis=-1, keepdims=True)
                - normed * jnp.mean(d_normed * normed, axis=-1, keepdims=True)
            )
        ).astype(BF16)
        d_scores = (dot_nt(d_mixed, value) * factor).astype(BF16)
        d_query = jnp.dot(d_scores, key, preferred_element_type=F32)
        d_value[:, span] += jnp.dot(d_mixed.T, attn, preferred_element_type=F32)
        d_key[:, span] += jnp.dot(query.T, d_scores, preferred_element_type=F32)
        d_z[rows, u_cols] = (d_gated * normed * slope[rows, u_cols]).astype(BF16)
        d_z[rows, q_cols] = (d_query * (slope[rows, q_cols] * scale)).astype(BF16)

    d_z[:, v_cols] = (d_value[...].T * slope[:, v_cols]).astype(BF16)
    d_z[:, k_cols] = (d_key[...].T * (slope[:, k_cols] * scale)).astype(BF16)

    core = info[3]
    outs = []
    whole = dot_nt(d_z[...], wp).astype(BF16)
    for y in range(Y):
        part = whole[y * STEP : (y + 1) * STEP]

        @pl.when(core == 0)
        def _():
            kept_v[y] = part[:LANES]
            sent_v[y] = part[LANES:]

        @pl.when(core != 0)
        def _():
            kept_v[y] = part[LANES:]
            sent_v[y] = part[:LANES]

        for held, out in ((sent_v, sent), (kept_v, kept)):
            outs.append(pltpu.make_async_copy(held.at[y], out.at[y], out_sems.at[len(outs)]))
            outs[-1].start()

    for x in range(X):
        for dest, source, pack in ((slice(0, 512), d_z, x_v), (slice(512, 640), gated, dy_v)):
            columns = jnp.concatenate([pack[2 * x], pack[2 * x + 1]], axis=1)
            block = dot_tn(columns, source[...]).astype(BF16)
            grads_v[x, :, :, :, dest] = block.reshape(YC, ZR, PART_ROWS, block.shape[1])
        outs.append(pltpu.make_async_copy(grads_v.at[x], grads.at[x], out_sems.at[len(outs)]))
        outs[-1].start()
    for copy in outs:
        copy.wait()


def heads_backward(info, packs, weights):
    half = jax.ShapeDtypeStruct((Y, LANES, WIDTH), BF16)
    return pl.pallas_call(
        heads_kernel,
        out_shape=(
            half,
            half,
            jax.ShapeDtypeStruct((X, YC, ZR, PART_ROWS, HIDDEN), BF16),
        ),
        in_specs=[SMEM_SPEC, HBM_SPEC, pl.BlockSpec(memory_space=pl.ANY)],
        out_specs=(HBM_SPEC,) * 3,
        scratch_shapes=[
            pltpu.VMEM((8, LENGTH, LANES), BF16),
            pltpu.VMEM((8, LENGTH, LANES), BF16),
            pltpu.VMEM((X, YC, ZR, PART_ROWS, HIDDEN), BF16),
            pltpu.VMEM((LENGTH, 4 * HEAD_DIM), BF16),
            pltpu.VMEM((LENGTH, 4 * HEAD_DIM), F32),
            pltpu.VMEM((HEAD_DIM, LENGTH), F32),
            pltpu.VMEM((HEAD_DIM, LENGTH), F32),
            pltpu.VMEM((LENGTH, 4 * HEAD_DIM), BF16),
            pltpu.VMEM((LENGTH, HEAD_DIM), BF16),
            pltpu.VMEM((Y, LANES, WIDTH), BF16),
            pltpu.VMEM((Y, LANES, WIDTH), BF16),
            pltpu.VMEM((X, YC, ZR, PART_ROWS, HIDDEN), BF16),
            pltpu.SemaphoreType.DMA((2 * LENGTH // STEP,)),
            pltpu.SemaphoreType.DMA((X * ZR,)),
            pltpu.SemaphoreType.DMA((2 * Y + X,)),
        ],
        compiler_params=pltpu.CompilerParams(vmem_limit_bytes=GRANT * 2**20),
        cost_estimate=pl.CostEstimate(
            flops=5_000_000_000, bytes_accessed=9_000_000, transcendentals=2_000_000
        ),
        name="heads",
    )(info, packs, weights)


def pair_kernel(place, kept, got, own, to_1, to_2, to_3, own_v, sem):
    y = place[0]
    own_v[...] = (kept[y].astype(F32) + got[y].astype(F32)).astype(BF16)
    copy = pltpu.make_async_copy(own_v, own, sem)
    copy.start()
    for step, block in ((1, to_1), (2, to_2), (3, to_3)):
        other = (y + step) & (Y - 1)
        block[...] = (kept[other].astype(F32) + got[other].astype(F32)).astype(BF16)
    copy.wait()


def pair_sums(y, kept, got):
    block = jax.ShapeDtypeStruct((LANES, WIDTH), BF16)
    return pl.pallas_call(
        pair_kernel,
        out_shape=(block,) * Y,
        in_specs=[SMEM_SPEC, VMEM_SPEC, VMEM_SPEC],
        out_specs=(HBM_SPEC,) + (VMEM_SPEC,) * (Y - 1),
        scratch_shapes=[pltpu.VMEM((LANES, WIDTH), BF16), pltpu.SemaphoreType.DMA],
        compiler_params=pltpu.CompilerParams(vmem_limit_bytes=32 * 2**20),
        cost_estimate=pl.CostEstimate(flops=500_000, bytes_accessed=3_000_000, transcendentals=0),
        name="pair_sums",
    )(y, kept, got)


def payload_kernel(own, came_1, came_2, came_3, dy, out, own_v, sem):
    copy = pltpu.make_async_copy(own, own_v, sem)
    copy.start()
    copy.wait()
    lane = lax.broadcasted_iota(jnp.int32, (64, LANES), 1)
    for m in range(8):
        cols = slice(m * LANES, (m + 1) * LANES)
        total = own_v[:, cols].astype(F32) + dy[m].astype(F32)
        for came in (came_1, came_2, came_3):
            total = total + came[:, cols].astype(F32)
        low, high = total[:64], total[64:]
        even = jnp.where(lane < 64, low, pltpu.roll(high, 64, 1))
        odd = jnp.where(lane < 64, pltpu.roll(low, 64, 1), high)
        out[2 * m] = even.astype(BF16)
        out[2 * m + 1] = odd.astype(BF16)


def payload(own, came, dy):
    return pl.pallas_call(
        payload_kernel,
        out_shape=jax.ShapeDtypeStruct((Z, 64, LANES), BF16),
        in_specs=[HBM_SPEC] + [VMEM_SPEC] * 4,
        out_specs=VMEM_SPEC,
        scratch_shapes=[pltpu.VMEM((LANES, WIDTH), BF16), pltpu.SemaphoreType.DMA],
        compiler_params=pltpu.CompilerParams(vmem_limit_bytes=32 * 2**20),
        cost_estimate=pl.CostEstimate(flops=700_000, bytes_accessed=1_500_000, transcendentals=0),
        name="payload",
    )(own, *came, dy)


def weight_sum_kernel(shared, out, done):
    done[...] = jnp.zeros_like(done)
    out[:, :, 3 * PART_ROWS :, :] = jnp.zeros((YC, 2, SUM_ROWS - 3 * PART_ROWS, LANES), F32)
    for h in range(YC):
        total = jnp.zeros((PART_ROWS, HIDDEN), F32)
        for x in range(X):
            for r in range(ZR):
                total = total + shared[x, h, r].astype(F32)
        for s in range(2):
            for n, col in enumerate((2 * s, 2 * s + 1, 4)):
                first = n * PART_ROWS
                block = total[:, col * LANES : (col + 1) * LANES]
                out[h, s, first : first + PART_ROWS, :] = block


def weight_sum(shared):
    return pl.pallas_call(
        weight_sum_kernel,
        out_shape=(
            jax.ShapeDtypeStruct((YC, 2, SUM_ROWS, LANES), F32),
            jax.ShapeDtypeStruct((8, LANES), F32),
        ),
        in_specs=[VMEM_SPEC],
        out_specs=(VMEM_SPEC, VMEM_SPEC),
        compiler_params=pltpu.CompilerParams(vmem_limit_bytes=32 * 2**20),
        cost_estimate=pl.CostEstimate(flops=700_000, bytes_accessed=1_700_000, transcendentals=0),
        name="weight_sum",
    )(shared)


def place_kernel(slots, tags, merged, out):
    slot_ids = lax.broadcasted_iota(jnp.int32, (SLOTS, LANES), 0)
    lane = lax.broadcasted_iota(jnp.int32, (SLOTS, LANES), 1)
    for pair in range(YC // 2):
        both = []
        for yc in (2 * pair, 2 * pair + 1):
            tokens = jnp.concatenate([merged[2 * yc], merged[2 * yc + 1]], axis=0)
            moved = [
                jnp.dot(
                    (slots[2 * yc + s : 2 * yc + s + 1, :] == slot_ids).astype(BF16),
                    tokens,
                    preferred_element_type=F32,
                )
                for s in range(2)
            ]
            rows = jnp.where(lane < 64, moved[0], moved[1])
            both.append(rows.reshape(OWNERS, CAP, LANES))
        out[:, pair * 16 : (pair + 1) * 16, :] = jnp.concatenate(both, axis=1).astype(BF16)
    out[:, YC * CAP :, :] = tags[...]


def place(slots, tags, merged):
    return pl.pallas_call(
        place_kernel,
        out_shape=jax.ShapeDtypeStruct((OWNERS, YC * CAP + 16, LANES), BF16),
        in_specs=[VMEM_SPEC] * 3,
        out_specs=VMEM_SPEC,
        compiler_params=pltpu.CompilerParams(vmem_limit_bytes=32 * 2**20),
        cost_estimate=pl.CostEstimate(
            flops=135_000_000, bytes_accessed=1_000_000, transcendentals=0
        ),
        name="place",
    )(slots, tags, merged)


def table_kernel(owned, out):
    count = YC * CAP
    row_ids = lax.broadcasted_iota(jnp.int32, (ROWS, LANES), 0).astype(F32)
    left = lax.broadcasted_iota(jnp.int32, (count, LANES), 1) < 64
    total = jnp.zeros((ROWS, LANES), F32)
    for pair in range(OWNERS // 2):
        select, rows = [], []
        for source in (2 * pair, 2 * pair + 1):
            tag = owned[source, count:, :].astype(F32)[:1]
            select.append((tag == row_ids).astype(BF16))
            here = owned[source, :count, :].astype(F32)
            rows.append(jnp.where(left, here, 0.0).astype(BF16))
            rows.append(jnp.where(left, 0.0, here).astype(BF16))
        total = total + jnp.dot(
            jnp.concatenate(select, axis=1),
            jnp.concatenate(rows, axis=0),
            preferred_element_type=F32,
        )
    out[...] = (total + pltpu.roll(total, 64, 1)).T[:64]


def table_sum(owned):
    return pl.pallas_call(
        table_kernel,
        out_shape=jax.ShapeDtypeStruct((64, ROWS), F32),
        in_specs=[VMEM_SPEC],
        out_specs=VMEM_SPEC,
        compiler_params=pltpu.CompilerParams(vmem_limit_bytes=32 * 2**20),
        cost_estimate=pl.CostEstimate(
            flops=270_000_000, bytes_accessed=1_000_000, transcendentals=0
        ),
        name="table_sum",
    )(owned)


def split_kernel(inputs, cotangent, out, sems):
    copies = [
        pltpu.make_async_copy(
            source.at[:, :, pl.ds(g * LANES, LANES)], out.at[g, :, t], sems.at[2 * g + t]
        )
        for g in range(8)
        for t, source in enumerate((inputs, cotangent))
    ]
    for copy in copies:
        copy.start()
    for copy in copies:
        copy.wait()


def split_columns(inputs, cotangent):
    return pl.pallas_call(
        split_kernel,
        out_shape=jax.ShapeDtypeStruct((8, 2, 2, 64, LANES), BF16),
        in_specs=[HBM_SPEC] * 2,
        out_specs=VMEM_SPEC,
        scratch_shapes=[pltpu.SemaphoreType.DMA((16,))],
        compiler_params=pltpu.CompilerParams(vmem_limit_bytes=60 * 2**20),
        cost_estimate=pl.CostEstimate(flops=0, bytes_accessed=1_000_000, transcendentals=0),
        name="split_columns",
    )(inputs, cotangent)


def per_device(inputs, cotangent, lengths, item_ids, owner_row, w_project, w_output):
    core = lax.axis_index("c")
    y_here = lax.axis_index("y")
    z_here = lax.axis_index(SEQ)
    lane = jnp.arange(LANES, dtype=jnp.int32)

    slot, local_row = routing(item_ids, owner_row)
    lens = lengths.reshape(-1)
    lens_row = jnp.concatenate([lens // 256, lens % 256])
    lens_row = jnp.pad(lens_row, (0, LANES - lens_row.shape[0]))
    small = jnp.pad(jnp.stack([slot, local_row, lens_row]), ((0, 5), (0, 0))).astype(BF16)
    high = PART_ROWS // 8
    wp_high = 2 * high
    n_w = wp_high + 2
    wp_tiles = w_project.reshape(ZR, high, 8, 2, LANES).transpose(0, 1, 3, 2, 4)
    wp_tiles = wp_tiles.reshape(ZR, wp_high, 8, LANES)
    wo_tiles = w_output.T.reshape(ZR, high, 8, 64).transpose(0, 2, 1, 3).reshape(ZR, 1, 8, LANES)
    small = jnp.broadcast_to(small[None, None], (ZR, 1, 8, LANES))
    w_tiles = jnp.concatenate([wp_tiles, wo_tiles, small], axis=1)

    spread = exchange(split_columns(inputs[0], cotangent[0]), PAIR)
    spread = spread.reshape(Z, 16, 8, LANES)
    w_tiles = jnp.broadcast_to(w_tiles[None], (ZQ, ZR, n_w, 8, LANES)).reshape(Z, n_w, 8, LANES)
    arrived = exchange(jnp.concatenate([spread, w_tiles], axis=1), SEQ)
    mine = arrived[:, :16].reshape(Z, 2, 64, LANES).transpose(1, 0, 2, 3)
    packs = lax.all_gather(mine.reshape(1, 2, LENGTH, LANES), PAIR, axis=0, tiled=True)

    by_head = exchange(arrived[:, 16:].reshape(YC, 2, n_w, 8, LANES), PAIR)
    wp_part = by_head[:, :, :wp_high].reshape(YC, 2, high, 2, 8, LANES)
    wp_part = wp_part.transpose(0, 2, 4, 1, 3, 5).reshape(YC, PART_ROWS, 4 * HEAD_DIM)
    wo_part = by_head[:, :, wp_high].reshape(YC, 2, 8, high, 64).transpose(0, 3, 2, 1, 4)
    w_part = jnp.concatenate([wp_part, wo_part.reshape(YC, PART_ROWS, HEAD_DIM)], axis=2)
    w_all = jnp.broadcast_to(w_part[None], (X * ZR,) + w_part.shape)
    weights = exchange(w_all, SHARE).reshape(X, ZR, YC, PART_ROWS, HIDDEN)

    facts = by_head[:, :, n_w - 1].astype(F32)
    slots = facts[:, :, 0].astype(jnp.int32)
    tag_of = facts[:, :, 1]
    lens_all = facts[:, 0, 2, :12].reshape(YC, 2, 2, 3)
    lens_all = (lens_all[:, 0] * 256.0 + lens_all[:, 1]).astype(jnp.int32).reshape(Z, 3)
    pack_lens = lax.dynamic_index_in_dim(lens_all, z_here, 0, keepdims=False)
    ends = jnp.cumsum(pack_lens)

    info = jnp.concatenate([ends, core[None]]).astype(jnp.int32)
    slot_ids = jnp.arange(SLOTS, dtype=jnp.int32)
    placed = slots[:, :, None, :] == slot_ids[None, None, :, None]
    tags = jnp.sum(jnp.where(placed, tag_of[:, :, None, :], 0.0), axis=3)
    tags = tags.reshape(YC, 2, OWNERS, CAP).transpose(2, 1, 0, 3).reshape(OWNERS, 1, LANES)
    tags = jnp.broadcast_to(tags.astype(BF16), (OWNERS, 16, LANES))

    kept, sent, grads = heads_backward(info, packs, weights)

    shared = exchange(grads.reshape(X * YC * ZR, PART_ROWS, HIDDEN), SPREAD)
    shared = shared.reshape(X, YC, ZR, PART_ROWS, HIDDEN)

    got = lax.ppermute(sent, "c", [(0, 1), (1, 0)])
    own, *to_y = pair_sums(y_here[None].astype(jnp.int32), kept, got)
    came = [
        lax.ppermute(to_y[step - 1], "y", [(i, (i + step) % Y) for i in range(Y)])
        for step in range(1, Y)
    ]
    block = (y_here * C + core) * LANES
    dy_own = lax.dynamic_slice(packs, (0, 1, block, 0), (YC, 1, LANES, LANES))[:, 0]

    w_sum, done = weight_sum(shared)
    done, *came = lax.optimization_barrier((done, *came))
    own = lax.dynamic_index_in_dim(kept, y_here, 0, keepdims=False).astype(F32)
    own = own + lax.dynamic_index_in_dim(got, y_here, 0, keepdims=False).astype(F32)
    merged = exchange(payload(own.astype(BF16), came, dy_own), SEQ)

    low = lax.axis_index("zr")
    rest = lax.psum_scatter(w_sum, "zq", scatter_dimension=0, tiled=True)
    rest = rest[0, :, : 3 * PART_ROWS]
    mine = lax.dynamic_index_in_dim(rest, low, 0, keepdims=False)
    other = lax.dynamic_index_in_dim(rest, 1 - low, 0, keepdims=False)
    other = lax.ppermute(other, "zr", [(0, 1), (1, 0)])
    w_grad = jnp.where(low == 0, jnp.stack([mine, other]), jnp.stack([other, mine]))
    w_grad = w_grad.reshape(ZR, 3, PART_ROWS, LANES)
    grad_proj = w_grad[:, :2].transpose(0, 2, 1, 3).reshape(32, 2 * LANES)
    both_out = w_grad[:, 2].reshape(32, 2, 64)
    grad_out = lax.dynamic_index_in_dim(both_out, z_here & 1, 1, keepdims=False).T

    owned = exchange(place(slots.reshape(2 * YC, LANES), tags, merged), DP)
    owned, grad_proj, grad_out = lax.optimization_barrier((owned, grad_proj, grad_out))
    return (grad_proj, grad_out, table_sum(owned).T)


def solution(mesh):
    fine = Mesh(mesh.devices.reshape(X, Y, C, ZQ, ZR), ALL)
    return jax.shard_map(
        per_device,
        mesh=fine,
        in_specs=(
            P(DP, None, SEQ, None),
            P(DP, None, SEQ, None),
            P(DP, None, None),
            P(DP, None, SEQ),
            P(),
            P(DP, SEQ),
            P(SEQ, DP),
        ),
        out_specs=(P(DP, SEQ), P(SEQ, DP), P(DP, SEQ)),
        check_vma=False,
    )
```
